32 devices in a mesh: grp: 2 (over x), row: 8 (over z, y), col: 2 (over core).
Axes of the slice: x: 2, y: 2, z: 4, core: 2. Of those that a mesh axis runs over, the one named last changes fastest.
Arguments:
- pair_act: bfloat16 [352, 176, 128], P(('grp', 'row'), 'col'), parts along dimension 0, may hold values from -6 to 6
- chain_lengths: int32 [16], P('grp'), parts along dimension 0, may hold values from 1 to 44, 176 in all
- resolved: int32 [16], P('grp'), parts along dimension 0, may hold values from 22 to 44
- in_gain: float32 [128], replicated, may hold values from 0.1 to 1.9
- out_gain: float32 [128], replicated, may hold values from 0.1 to 1.9
- w_left: bfloat16 [128, 256], replicated, may hold values from -0.5 to 0.5
- w_right: bfloat16 [128, 256], replicated, may hold values from -0.5 to 0.5
- w_gate: bfloat16 [128, 128], replicated, may hold values from -0.5 to 0.5
- w_out: bfloat16 [128, 128], replicated, may hold values from -0.5 to 0.5
Outputs:
- update: bfloat16 [352, 176, 128], P(('grp', 'row'), 'col'), parts along dimension 0
The draws below stay inside these ranges and needn't reach their ends.
There are 2 independent parts, one for each index of `grp`. The reference program is written for one: setup_inputs(seed, part) draws one part's arguments, and reference() takes and returns one part's arrays. A program takes and returns all parts, laid end to end along the dimension named above; an argument that names none is the same for every part. Nothing has to cross between parts.
Inputs may be any that keep to these rules, and one draw needn't show every extreme that they name: chain_lengths sum to 176; the longest chain has exactly 44 residues.
All inputs are finite; a program needn't handle non-finite values.
Results may differ from the reference program's by a relative error of at most 0.0079.
Values may be sent and summed in bfloat16 or wider, within the bound.
No kernel may reach another device: no remote copies, remote signals or barrier semaphores. Data moves between devices by JAX's collectives and lax.ppermute only.
A program may use at most 64 MiB of HBM per device.

```python
import math
import jax
import jax.numpy as jnp
import numpy as np
from jax import lax

C = 128
CH = 128
CHAINS = 8
RESIDUES = 176


def with_ends(drawn, stream_key, low, high):
    dims = drawn.shape
    index_at = [jax.random.randint(jax.random.fold_in(stream_key, axis), (), 0, dims[axis]) for axis in range(len(dims))]
    drawn = drawn.at[tuple(index_at)].set(low)
    longest = dims.index(max(dims))
    index_at[longest] = (index_at[longest] + 1) % dims[longest]
    return drawn.at[tuple(index_at)].set(high)


def level_of(rng, dims, split, low, top_value):
    loudness = 1.0
    for dim, blocks in split:
        steps = jax.random.uniform(jax.random.fold_in(jax.random.fold_in(rng, 6), dim), (blocks,), jnp.float32, low / len(split), top_value / len(split))
        loudness = loudness * jnp.repeat(jnp.exp(steps), dims[dim] // blocks).reshape((-1,) + (1,) * (len(dims) - 1 - dim))
    return loudness


def split_up(count, total, reach, skew):
    loads = [(1 << 20) // math.isqrt(standing ** skew) + 1 for standing in range(2, count + 1)]
    spare, given = total - reach - (count - 1), [1] * (count - 1)
    while spare > 0:
        free = [i for i in range(count - 1) if given[i] < reach]
        pool, budget = sum([loads[i] for i in free]), spare
        for i in free:
            more = min(reach - given[i], max(1, budget * loads[i] // pool), spare)
            given[i] = given[i] + more
            spare = spare - more
    return np.array([reach] + given)


def ragged(own_key, amount, total, limit, skew):
    if amount == 2:
        one = jax.random.randint(own_key, (), max(1, total - limit), min(limit, total - 1) + 1)
        return jnp.stack([one, total - one])
    tallies = jnp.asarray(split_up(amount, total, limit, skew), jnp.int32)
    couples = (amount - 1) // 2
    source_of, sink = tallies[1:1 + 2 * couples:2], tallies[2:2 + 2 * couples:2]
    margin = jnp.minimum(source_of - 1, limit - sink)
    moved = jax.random.randint(jax.random.fold_in(own_key, 1), (couples,), 0, 1 << 20) % (margin + 1)
    tallies = tallies.at[1:1 + 2 * couples:2].set(source_of - moved).at[2:2 + 2 * couples:2].set(sink + moved)
    return tallies[jax.random.permutation(jax.random.fold_in(own_key, 2), amount)]


def scatter_about(key, extent, spread, bound, shards=(), held_as=jnp.bfloat16):
    entries = jax.random.normal(key, extent, jnp.float32) * spread
    if len(shards) > 0:
        entries = level_of(key, extent, shards, -0.22, 0.18) * entries
    return jnp.clip(entries, min=-bound, max=bound).astype(held_as)


def setup_inputs(seed: int = 0, part: int = 0) -> dict:
    key_of = jax.random.split(jax.random.key(seed), 10)
    part_keys = jax.random.split(jax.random.fold_in(key_of[9], part), 10)
    return {
        "pair_act": scatter_about(part_keys[0], (RESIDUES, RESIDUES, C), 1.0, 6.0, ((0, 8), (1, 2))),
        "chain_lengths": ragged(part_keys[1], CHAINS, RESIDUES, RESIDUES // 4, 1).astype(jnp.int32),
        "resolved": with_ends(jax.random.randint(part_keys[2], (CHAINS,), RESIDUES // 8, RESIDUES // 4 + 1), jax.random.fold_in(part_keys[2], 1), RESIDUES // 8, (RESIDUES // 4 + 1) - 1).astype(jnp.int32),
        "in_gain": jnp.clip(1.0 + 0.18 * jax.random.normal(key_of[3], (C,), jnp.float32), 0.1, 1.9),
        "out_gain": jnp.clip(1.0 + 0.18 * jax.random.normal(key_of[4], (CH,), jnp.float32), 0.1, 1.9),
        "w_left": scatter_about(key_of[5], (C, 2 * CH), C ** -0.5, 0.5),
        "w_right": scatter_about(key_of[6], (C, 2 * CH), C ** -0.5, 0.5),
        "w_gate": scatter_about(key_of[7], (C, C), C ** -0.5, 0.5),
        "w_out": scatter_about(key_of[8], (CH, C), CH ** -0.5, 0.5),
    }


def layer_norm(values, gain):
    mean = lax.optimization_barrier(jnp.mean(values, axis=-1, keepdims=True))
    centred = values - mean
    variance = lax.optimization_barrier(jnp.mean(centred * centred, axis=-1, keepdims=True))
    return centred * jax.lax.rsqrt(variance + 1e-05) * gain

def valid_residues(chain_lengths, resolved, total):
    ends = jnp.cumsum(chain_lengths).astype(jnp.int32)
    starts = ends - chain_lengths
    position = jnp.arange(total, dtype=jnp.int32)
    inside = (position[:, None] >= starts[None, :]) & (position[:, None] < ends[None, :])
    kept = inside & (position[:, None] - starts[None, :] < resolved[None, :])
    return jnp.any(kept, axis=1).astype(jnp.float32)

def edges(normed, weight, mask, hidden):
    projected = jnp.einsum('ijc,cd->ijd', normed.astype(jnp.float32), weight.astype(jnp.float32))
    return (mask[..., None] * jax.nn.sigmoid(projected[..., :hidden]) * projected[..., hidden:]).astype(jnp.bfloat16)

def reference(pair_act, chain_lengths, resolved, in_gain, out_gain, w_left, w_right, w_gate, w_out):
    valid = valid_residues(chain_lengths, resolved, RESIDUES)
    mask = valid[:, None] * valid[None, :]
    normed = layer_norm(pair_act.astype(jnp.float32), in_gain).astype(jnp.bfloat16)
    left_edge = edges(normed, w_left, mask, CH)
    right_edge = edges(normed, w_right, mask, CH)
    gate_values = jax.nn.sigmoid(jnp.einsum('ijc,cd->ijd', normed.astype(jnp.float32), w_gate.astype(jnp.float32)))
    product = jnp.einsum('ikc,jkc->ijc', left_edge.astype(jnp.float32), right_edge.astype(jnp.float32))
    normed_out = layer_norm(product, out_gain).astype(jnp.bfloat16)
    projected = jnp.einsum('ijc,cd->ijd', normed_out.astype(jnp.float32), w_out.astype(jnp.float32))
    return (gate_values * projected).astype(jnp.bfloat16)
```

```python
import functools

import jax
import jax.numpy as jnp
from jax import lax
from jax.experimental import pallas as pl
from jax.experimental.pallas import tpu as pltpu
from jax.sharding import PartitionSpec as P

EPS = 1e-05
LANES = 128
VMEM_LIMIT = 48 * 1024 * 1024


def ceil_to(n, m):
    return -(-n // m) * m


def edges_kernel(rows, cols, n_dev, chains, lens_ref, res_ref, first_ref, x_ref, gain_ref, wl_ref, wr_ref,
                 edge_ref, normed_ref):
    block = x_ref.shape[0]
    hidden = wl_ref.shape[1] // 2
    x = x_ref[...].astype(jnp.float32)
    mean = jnp.mean(x, axis=-1, keepdims=True)
    centred = x - mean
    variance = jnp.mean(centred * centred, axis=-1, keepdims=True)
    normed = (centred * lax.rsqrt(variance + EPS) * gain_ref[...]).astype(jnp.bfloat16)
    normed_ref[...] = normed
    position = pl.program_id(0) * block + lax.broadcasted_iota(jnp.int32, (8, block), 1)
    i_here = jnp.floor((position.astype(jnp.float32) + 0.5) * (1.0 / cols)).astype(jnp.int32)
    k_here = position - i_here * cols
    i_at = first_ref[0] + i_here
    k_at = first_ref[1] + k_here
    i_ok = jnp.zeros((8, block), jnp.float32)
    k_ok = jnp.zeros((8, block), jnp.float32)
    start = 0
    for q in range(chains):
        length = lens_ref[q]
        stop = start + jnp.minimum(length, res_ref[q])
        i_ok = jnp.where((i_at >= start) & (i_at < stop), 1.0, i_ok)
        k_ok = jnp.where((k_at >= start) & (k_at < stop), 1.0, k_ok)
        start = start + length
    mask = i_ok * k_ok
    parts = []
    for w_ref in (wl_ref, wr_ref):
        projected = lax.dot_general(
            w_ref[...], normed, (((0,), (1,)), ((), ())), preferred_element_type=jnp.float32
        )
        edge = jax.nn.sigmoid(projected[:hidden]) * projected[hidden:]
        parts.append(edge.reshape(n_dev, hidden // n_dev, block))
    both = jnp.concatenate(parts, axis=1)
    if both.shape[1] % 8 == 0:
        both = (both.reshape(-1, 8, block) * mask[None]).reshape(both.shape)
    else:
        both = both * mask[None, : 1]
    edge_ref[...] = both.astype(jnp.bfloat16)


def make_edges(pair, lens, resolved, first, gain, w_left, w_right, n_dev, rows, cols):
    count, channels = pair.shape
    hidden = w_left.shape[1] // 2
    per_dev = hidden // n_dev
    block = 512
    smem = pl.BlockSpec(memory_space=pltpu.SMEM)
    return pl.pallas_call(
        functools.partial(edges_kernel, rows, cols, n_dev, lens.shape[0]),
        grid=(pl.cdiv(count, block),),
        in_specs=[
            smem, smem, smem,
            pl.BlockSpec((block, channels), lambda b: (b, 0)),
            pl.BlockSpec((1, channels), lambda b: (0, 0)),
            pl.BlockSpec(w_left.shape, lambda b: (0, 0)),
            pl.BlockSpec(w_right.shape, lambda b: (0, 0)),
        ],
        out_specs=[
            pl.BlockSpec((n_dev, 2 * per_dev, block), lambda b: (0, 0, b)),
            pl.BlockSpec((block, channels), lambda b: (b, 0)),
        ],
        out_shape=[
            jax.ShapeDtypeStruct((n_dev, 2 * per_dev, count), jnp.bfloat16),
            jax.ShapeDtypeStruct((count, channels), jnp.bfloat16),
        ],
        compiler_params=pltpu.CompilerParams(vmem_limit_bytes=VMEM_LIMIT),
    )(lens, resolved, first, pair, gain, w_left, w_right)


def product_kernel(n_rows, n_cols, rows, cols, got_ref, out_ref, left_s, right_s, prod_s):
    ch = out_ref.shape[1]
    step = left_s.shape[1] // (n_rows * rows)
    total = n_rows * rows
    tiles = pl.cdiv(cols, LANES)
    flat = rows * cols
    lane = lax.broadcasted_iota(jnp.int32, (2 * ch, LANES), 1)
    lane_out = lax.broadcasted_iota(jnp.int32, (ch, LANES), 1)

    def unpack(r, carry):
        for c in range(n_cols):
            src = r * n_cols + c
            held = {}

            def tile_of(t):
                if t not in held:
                    width = min(LANES, flat - t * LANES)
                    got = got_ref[src, :, pl.ds(t * LANES, width)].astype(jnp.float32)
                    if width < LANES:
                        got = jnp.concatenate([got, jnp.zeros((2 * ch, LANES - width), jnp.float32)], axis=1)
                    held[t] = got
                return held[t]

            for i in range(rows):
                for tt in range(tiles):
                    at = cols * i + LANES * tt
                    length = min(LANES, cols - LANES * tt)
                    t0, off = divmod(at, LANES)
                    piece = tile_of(t0)
                    if off:
                        piece = pltpu.roll(piece, LANES - off, 1)
                    if off + length > LANES:
                        piece = jnp.where(lane < LANES - off, piece, pltpu.roll(tile_of(t0 + 1), LANES - off, 1))
                    if length < LANES:
                        piece = jnp.where(lane < length, piece, 0.0)
                    base = pl.multiple_of((r * rows + i) * step, 8)
                    left_s[c * tiles + tt, pl.ds(base, ch), :] = piece[:ch]
                    right_s[c * tiles + tt, pl.ds(base, ch), :] = piece[ch:]
        return carry

    lax.fori_loop(0, n_rows, unpack, 0)

    pad = tiles * LANES - cols
    for d in range(ch):
        left = jnp.concatenate(
            [left_s[t, pl.ds(d, total, stride=step), :] for t in range(n_cols * tiles)], axis=1
        ).astype(jnp.bfloat16)
        right = jnp.concatenate(
            [right_s[t, pl.ds(d, total, stride=step), :] for t in range(n_cols * tiles)], axis=1
        )
        pieces = []
        for c in range(n_cols):
            pieces.append(right[c * cols:(c + 1) * cols])
            if pad:
                pieces.append(jnp.zeros((pad, right.shape[1]), jnp.float32))
        right = jnp.concatenate(pieces, axis=0).astype(jnp.bfloat16)
        prod = lax.dot_general(left, right, (((1,), (1,)), ((), ())), preferred_element_type=jnp.float32)
        for t in range(n_cols * tiles):
            prod_s[t, pl.ds(d, total, stride=step), :] = prod[:, t * LANES:(t + 1) * LANES]

    def pack(r, carry):
        for c in range(n_cols):
            for t in range(pl.cdiv(flat, LANES)):
                tile = None
                for i in range(rows):
                    for tt in range(tiles):
                        shift = cols * i + LANES * tt - LANES * t
                        length = min(LANES, cols - LANES * tt)
                        if shift >= LANES or shift + length <= 0:
                            continue
                        base = pl.multiple_of((r * rows + i) * step, 8)
                        piece = prod_s[c * tiles + tt, pl.ds(base, ch), :]
                        if shift % LANES:
                            piece = pltpu.roll(piece, shift % LANES, 1)
                        tile = piece if tile is None else jnp.where(lane_out < shift, tile, piece)
                width = min(LANES, flat - t * LANES)
                out_ref[r * n_cols + c, :, pl.ds(t * LANES, width)] = tile[:, :width].astype(out_ref.dtype)
        return carry

    lax.fori_loop(0, n_rows, pack, 0)


def make_product(got, n_rows, n_cols, rows, cols):
    n_dev, both, flat = got.shape
    ch = both // 2
    step = ceil_to(ch, 8)
    tiles = n_cols * pl.cdiv(cols, LANES)
    held = pltpu.VMEM((tiles, n_rows * rows * step, LANES), jnp.float32)
    whole = pl.BlockSpec(memory_space=pltpu.VMEM)
    return pl.pallas_call(
        functools.partial(product_kernel, n_rows, n_cols, rows, cols),
        in_specs=[whole],
        out_specs=whole,
        out_shape=jax.ShapeDtypeStruct((n_dev, ch, flat), jnp.bfloat16),
        scratch_shapes=[held, held, held],
        compiler_params=pltpu.CompilerParams(vmem_limit_bytes=VMEM_LIMIT),
    )(got)


def update_kernel(prod_ref, gain_ref, w_ref, gate_ref, out_ref):
    prod = prod_ref[...].astype(jnp.float32).reshape(-1, prod_ref.shape[2])
    mean = jnp.mean(prod, axis=0, keepdims=True)
    centred = prod - mean
    variance = jnp.mean(centred * centred, axis=0, keepdims=True)
    normed = (centred * lax.rsqrt(variance + EPS) * gain_ref[...]).astype(jnp.bfloat16)
    projected = lax.dot_general(normed, w_ref[...], (((0,), (0,)), ((), ())), preferred_element_type=jnp.float32)
    out_ref[...] = (gate_ref[...] * projected).astype(out_ref.dtype)


def make_update(prod, gain, w_out, gate):
    n_dev, ch, count = prod.shape
    channels = w_out.shape[1]
    block = 512
    return pl.pallas_call(
        update_kernel,
        grid=(pl.cdiv(count, block),),
        in_specs=[
            pl.BlockSpec((n_dev, ch, block), lambda b: (0, 0, b)),
            pl.BlockSpec((n_dev * ch, 1), lambda b: (0, 0)),
            pl.BlockSpec(w_out.shape, lambda b: (0, 0)),
            pl.BlockSpec((block, channels), lambda b: (b, 0)),
        ],
        out_specs=pl.BlockSpec((block, channels), lambda b: (b, 0)),
        out_shape=jax.ShapeDtypeStruct((count, channels), jnp.bfloat16),
        compiler_params=pltpu.CompilerParams(vmem_limit_bytes=VMEM_LIMIT),
    )(prod, gain, w_out, gate)


def shards(pair_act, chain_lengths, resolved, in_gain, out_gain, w_left, w_right, w_gate, w_out):
    rows, cols, channels = pair_act.shape
    hidden = w_out.shape[0]
    n_rows = lax.axis_size("row")
    n_cols = lax.axis_size("col")
    n_dev = n_rows * n_cols
    first = jnp.stack([lax.axis_index("row") * rows, lax.axis_index("col") * cols]).astype(jnp.int32)
    edges, normed = make_edges(
        pair_act.reshape(rows * cols, channels), chain_lengths, resolved, first,
        in_gain.reshape(1, channels), w_left, w_right, n_dev, rows, cols,
    )
    got = lax.all_to_all(edges, ("row", "col"), split_axis=0, concat_axis=0, tiled=True)
    gate = jax.nn.sigmoid(jnp.dot(normed, w_gate, preferred_element_type=jnp.float32))
    outgoing = make_product(got, n_rows, n_cols, rows, cols)
    returned = lax.all_to_all(outgoing, ("row", "col"), split_axis=0, concat_axis=0, tiled=True)
    update = make_update(returned, out_gain.reshape(hidden, 1), w_out, gate)
    return update.reshape(rows, cols, channels)


def solution(mesh):
    return jax.shard_map(
        shards,
        mesh=mesh,
        in_specs=(P(("grp", "row"), "col", None), P("grp"), P("grp"), P(), P(), P(), P(), P(), P()),
        out_specs=P(("grp", "row"), "col", None),
        check_vma=False,
    )
```

```python
import functools

import jax
import jax.numpy as jnp
from jax import lax
from jax.experimental import pallas as pl
from jax.experimental.pallas import tpu as pltpu
from jax.sharding import PartitionSpec as P

EPS = 1e-05
LANES = 128
VMEM_LIMIT = 32 * 1024 * 1024
VMEM_FIRST = 60 * 1024 * 1024


def ceil_to(n, m):
    return -(-n // m) * m


def edges_kernel(rows, cols, n_dev, chains, lens_ref, res_ref, first_ref, x_ref, gain_ref, wl_ref, wr_ref,
                 normed_ref, *refs):
    edge_refs, held = refs[:n_dev], refs[n_dev]
    block = x_ref.shape[0]
    hidden = wl_ref.shape[1] // 2
    x = x_ref[...].astype(jnp.float32)
    mean = jnp.mean(x, axis=-1, keepdims=True)
    centred = x - mean
    variance = jnp.mean(centred * centred, axis=-1, keepdims=True)
    normed = (centred * lax.rsqrt(variance + EPS) * gain_ref[...]).astype(jnp.bfloat16)
    normed_ref[...] = normed
    position = pl.program_id(0) * block + lax.broadcasted_iota(jnp.int32, (8, block), 1)
    i_here = jnp.floor((position.astype(jnp.float32) + 0.5) * (1.0 / cols)).astype(jnp.int32)
    k_here = position - i_here * cols
    i_at = first_ref[0] + i_here
    k_at = first_ref[1] + k_here
    i_ok = jnp.zeros((8, block), jnp.float32)
    k_ok = jnp.zeros((8, block), jnp.float32)
    start = 0
    for q in range(chains):
        length = lens_ref[q]
        stop = start + jnp.minimum(length, res_ref[q])
        i_ok = jnp.where((i_at >= start) & (i_at < stop), 1.0, i_ok)
        k_ok = jnp.where((k_at >= start) & (k_at < stop), 1.0, k_ok)
        start = start + length
    mask = i_ok * k_ok
    parts = []
    for w_ref in (wl_ref, wr_ref):
        projected = lax.dot_general(
            w_ref[...], normed, (((0,), (1,)), ((), ())), preferred_element_type=jnp.float32
        )
        edge = jax.nn.sigmoid(projected[:hidden]) * projected[hidden:]
        parts.append(edge.reshape(n_dev, hidden // n_dev, block))
    both = jnp.concatenate(parts, axis=1)
    if both.shape[1] % 8 == 0:
        both = (both.reshape(-1, 8, block) * mask[None]).reshape(both.shape)
    else:
        both = both * mask[None, : 1]
    held[...] = both.astype(jnp.bfloat16)
    for s in range(n_dev):
        edge_refs[s][...] = held[jnp.bitwise_xor(first_ref[2], s)]


def make_edges(pair, lens, resolved, first, gain, w_left, w_right, n_dev, rows, cols):
    count, channels = pair.shape
    hidden = w_left.shape[1] // 2
    per_dev = hidden // n_dev
    block = 512
    smem = pl.BlockSpec(memory_space=pltpu.SMEM)
    return pl.pallas_call(
        functools.partial(edges_kernel, rows, cols, n_dev, lens.shape[0]),
        grid=(pl.cdiv(count, block),),
        in_specs=[
            smem, smem, smem,
            pl.BlockSpec((block, channels), lambda b: (b, 0)),
            pl.BlockSpec((1, channels), lambda b: (0, 0)),
            pl.BlockSpec(w_left.shape, lambda b: (0, 0)),
            pl.BlockSpec(w_right.shape, lambda b: (0, 0)),
        ],
        out_specs=[pl.BlockSpec((block, channels), lambda b: (b, 0))]
        + [pl.BlockSpec((2 * per_dev, block), lambda b: (0, b))] * n_dev,
        out_shape=[jax.ShapeDtypeStruct((count, channels), jnp.bfloat16)]
        + [jax.ShapeDtypeStruct((2 * per_dev, count), jnp.bfloat16)] * n_dev,
        scratch_shapes=[pltpu.VMEM((n_dev, 2 * per_dev, block), jnp.bfloat16)],
        compiler_params=pltpu.CompilerParams(vmem_limit_bytes=VMEM_FIRST),
    )(lens, resolved, first, pair, gain, w_left, w_right)


def product_kernel(n_rows, n_cols, rows, cols, me_ref, *refs):
    n_dev = n_rows * n_cols
    got_refs, out_refs = refs[:n_dev], refs[n_dev:2 * n_dev]
    left_s, right_s, prod_s = refs[2 * n_dev:]
    ch = out_refs[0].shape[0]
    step = left_s.shape[1] // (n_rows * rows)
    total = n_rows * rows
    tiles = pl.cdiv(cols, LANES)
    flat = rows * cols
    lane = lax.broadcasted_iota(jnp.int32, (2 * ch, LANES), 1)
    lane_out = lax.broadcasted_iota(jnp.int32, (ch, LANES), 1)

    for s in range(n_dev):
        src = jnp.bitwise_xor(me_ref[2], s)
        r, c = src // n_cols, lax.rem(src, n_cols)
        got_ref = got_refs[s]
        if True:
            held = {}

            def tile_of(t):
                if t not in held:
                    width = min(LANES, flat - t * LANES)
                    got = got_ref[:, pl.ds(t * LANES, width)].astype(jnp.float32)
                    if width < LANES:
                        got = jnp.concatenate([got, jnp.zeros((2 * ch, LANES - width), jnp.float32)], axis=1)
                    held[t] = got
                return held[t]

            for i in range(rows):
                for tt in range(tiles):
                    at = cols * i + LANES * tt
                    length = min(LANES, cols - LANES * tt)
                    t0, off = divmod(at, LANES)
                    piece = tile_of(t0)
                    if off:
                        piece = pltpu.roll(piece, LANES - off, 1)
                    if off + length > LANES:
                        piece = jnp.where(lane < LANES - off, piece, pltpu.roll(tile_of(t0 + 1), LANES - off, 1))
                    if length < LANES:
                        piece = jnp.where(lane < length, piece, 0.0)
                    base = pl.multiple_of((r * rows + i) * step, 8)
                    left_s[c * tiles + tt, pl.ds(base, ch), :] = piece[:ch]
                    right_s[c * tiles + tt, pl.ds(base, ch), :] = piece[ch:]

    pad = tiles * LANES - cols
    for d in range(ch):
        left = jnp.concatenate(
            [left_s[t, pl.ds(d, total, stride=step), :] for t in range(n_cols * tiles)], axis=1
        ).astype(jnp.bfloat16)
        right = jnp.concatenate(
            [right_s[t, pl.ds(d, total, stride=step), :] for t in range(n_cols * tiles)], axis=1
        )
        pieces = []
        for c in range(n_cols):
            pieces.append(right[c * cols:(c + 1) * cols])
            if pad:
                pieces.append(jnp.zeros((pad, right.shape[1]), jnp.float32))
        right = jnp.concatenate(pieces, axis=0).astype(jnp.bfloat16)
        prod = lax.dot_general(left, right, (((1,), (1,)), ((), ())), preferred_element_type=jnp.float32)
        for t in range(n_cols * tiles):
            prod_s[t, pl.ds(d, total, stride=step), :] = prod[:, t * LANES:(t + 1) * LANES]

    for s in range(n_dev):
        dst = jnp.bitwise_xor(me_ref[2], s)
        r, c = dst // n_cols, lax.rem(dst, n_cols)
        if True:
            for t in range(pl.cdiv(flat, LANES)):
                tile = None
                for i in range(rows):
                    for tt in range(tiles):
                        shift = cols * i + LANES * tt - LANES * t
                        length = min(LANES, cols - LANES * tt)
                        if shift >= LANES or shift + length <= 0:
                            continue
                        base = pl.multiple_of((r * rows + i) * step, 8)
                        piece = prod_s[c * tiles + tt, pl.ds(base, ch), :]
                        if shift % LANES:
                            piece = pltpu.roll(piece, shift % LANES, 1)
                        tile = piece if tile is None else jnp.where(lane_out < shift, tile, piece)
                width = min(LANES, flat - t * LANES)
                out_refs[s][:, pl.ds(t * LANES, width)] = tile[:, :width].astype(jnp.bfloat16)


def make_product(got, first, n_rows, n_cols, rows, cols):
    n_dev = len(got)
    both, flat = got[0].shape
    ch = both // 2
    step = ceil_to(ch, 8)
    tiles = n_cols * pl.cdiv(cols, LANES)
    held = pltpu.VMEM((tiles, n_rows * rows * step, LANES), jnp.float32)
    whole = pl.BlockSpec(memory_space=pltpu.VMEM)
    return pl.pallas_call(
        functools.partial(product_kernel, n_rows, n_cols, rows, cols),
        in_specs=[pl.BlockSpec(memory_space=pltpu.SMEM)] + [whole] * n_dev,
        out_specs=[whole] * n_dev,
        out_shape=[jax.ShapeDtypeStruct((ch, flat), jnp.bfloat16)] * n_dev,
        scratch_shapes=[held, held, held],
        compiler_params=pltpu.CompilerParams(vmem_limit_bytes=VMEM_LIMIT),
    )(first, *got)


def update_kernel(n_dev, first_ref, gain_ref, w_ref, gate_ref, *refs):
    prod_refs, out_ref, held = refs[:n_dev], refs[n_dev], refs[n_dev + 1]
    for s in range(n_dev):
        held[jnp.bitwise_xor(first_ref[2], s)] = prod_refs[s][...].astype(jnp.float32)
    prod = held[...].reshape(-1, held.shape[2])
    mean = jnp.mean(prod, axis=0, keepdims=True)
    centred = prod - mean
    variance = jnp.mean(centred * centred, axis=0, keepdims=True)
    normed = (centred * lax.rsqrt(variance + EPS) * gain_ref[...]).astype(jnp.bfloat16)
    projected = lax.dot_general(normed, w_ref[...], (((0,), (0,)), ((), ())), preferred_element_type=jnp.float32)
    out_ref[...] = (gate_ref[...] * projected).astype(out_ref.dtype)


def make_update(prods, first, gain, w_out, gate):
    n_dev = len(prods)
    ch, count = prods[0].shape
    channels = w_out.shape[1]
    block = 512
    return pl.pallas_call(
        functools.partial(update_kernel, n_dev),
        grid=(pl.cdiv(count, block),),
        in_specs=[
            pl.BlockSpec(memory_space=pltpu.SMEM),
            pl.BlockSpec((n_dev * ch, 1), lambda b: (0, 0)),
            pl.BlockSpec(w_out.shape, lambda b: (0, 0)),
            pl.BlockSpec((block, channels), lambda b: (b, 0)),
        ]
        + [pl.BlockSpec((ch, block), lambda b: (0, b))] * n_dev,
        out_specs=pl.BlockSpec((block, channels), lambda b: (b, 0)),
        out_shape=jax.ShapeDtypeStruct((count, channels), jnp.bfloat16),
        scratch_shapes=[pltpu.VMEM((n_dev, ch, block), jnp.float32)],
        compiler_params=pltpu.CompilerParams(vmem_limit_bytes=VMEM_LIMIT),
    )(first, gain, w_out, gate, *prods)


def exchange(blocks):
    n_dev = len(blocks)
    return [blocks[0]] + [
        lax.ppermute(blocks[s], ("row", "col"), [(d, d ^ s) for d in range(n_dev)]) for s in range(1, n_dev)
    ]


def shards(pair_act, chain_lengths, resolved, in_gain, out_gain, w_left, w_right, w_gate, w_out):
    rows, cols, channels = pair_act.shape
    hidden = w_out.shape[0]
    n_rows = lax.axis_size("row")
    n_cols = lax.axis_size("col")
    n_dev = n_rows * n_cols
    row, col = lax.axis_index("row"), lax.axis_index("col")
    first = jnp.stack([row * rows, col * cols, row * n_cols + col]).astype(jnp.int32)
    normed, *edges = make_edges(
        pair_act.reshape(rows * cols, channels), chain_lengths, resolved, first,
        in_gain.reshape(1, channels), w_left, w_right, n_dev, rows, cols,
    )
    got = exchange(edges)
    gate = jax.nn.sigmoid(jnp.dot(normed, w_gate, preferred_element_type=jnp.float32))
    outgoing = make_product(got, first, n_rows, n_cols, rows, cols)
    returned = exchange(outgoing)
    update = make_update(returned, first, out_gain.reshape(hidden, 1), w_out, gate)
    return update.reshape(rows, cols, channels)


def solution(mesh):
    return jax.shard_map(
        shards,
        mesh=mesh,
        in_specs=(P(("grp", "row"), "col", None), P("grp"), P("grp"), P(), P(), P(), P(), P(), P()),
        out_specs=P(("grp", "row"), "col", None),
        check_vma=False,
    )
```

```python
import functools

import jax
import jax.numpy as jnp
from jax import lax
from jax.experimental import pallas as pl
from jax.experimental.pallas import tpu as pltpu
from jax.sharding import PartitionSpec as P

EPS = 1e-05
LANES = 128
VMEM_LIMIT = 32 * 1024 * 1024
VMEM_FIRST = 60 * 1024 * 1024


def ceil_to(n, m):
    return -(-n // m) * m


def edges_kernel(cols, groups, chains, lens_ref, res_ref, place_ref, x_ref, gain_ref, wl_ref, wr_ref,
                 normed_ref, *refs):
    both_refs, right_refs, held = refs[:groups], refs[groups:2 * groups], refs[2 * groups]
    block = x_ref.shape[0]
    hidden = wl_ref.shape[1] // 2
    x = x_ref[...].astype(jnp.float32)
    mean = jnp.mean(x, axis=-1, keepdims=True)
    centred = x - mean
    variance = jnp.mean(centred * centred, axis=-1, keepdims=True)
    normed = (centred * lax.rsqrt(variance + EPS) * gain_ref[...]).astype(jnp.bfloat16)
    normed_ref[...] = normed
    position = pl.program_id(0) * block + lax.broadcasted_iota(jnp.int32, (8, block), 1)
    i_here = jnp.floor((position.astype(jnp.float32) + 0.5) * (1.0 / cols)).astype(jnp.int32)
    k_here = position - i_here * cols
    i_at = place_ref[0] + i_here
    k_at = place_ref[1] + k_here
    i_ok = jnp.zeros((8, block), jnp.float32)
    k_ok = jnp.zeros((8, block), jnp.float32)
    start = 0
    for q in range(chains):
        length = lens_ref[q]
        stop = start + jnp.minimum(length, res_ref[q])
        i_ok = jnp.where((i_at >= start) & (i_at < stop), 1.0, i_ok)
        k_ok = jnp.where((k_at >= start) & (k_at < stop), 1.0, k_ok)
        start = start + length
    mask = i_ok * k_ok
    parts = []
    for w_ref in (wl_ref, wr_ref):
        projected = lax.dot_general(
            w_ref[...], normed, (((0,), (1,)), ((), ())), preferred_element_type=jnp.float32
        )
        edge = jax.nn.sigmoid(projected[:hidden]) * projected[hidden:]
        parts.append(edge.reshape(groups, hidden // groups, block))
    both = jnp.concatenate(parts, axis=1)
    held[...] = (both.reshape(-1, 8, block) * mask[None]).reshape(both.shape).astype(jnp.bfloat16)
    own = hidden // groups
    for u in range(groups):
        group = jnp.bitwise_xor(place_ref[2], u)
        both_refs[u][...] = held[group]
        right_refs[u][...] = held[group, own:]


def make_edges(pair, lens, resolved, place, gain, w_left, w_right, groups, cols):
    count, channels = pair.shape
    own = w_left.shape[1] // 2 // groups
    block = 512
    smem = pl.BlockSpec(memory_space=pltpu.SMEM)
    return pl.pallas_call(
        functools.partial(edges_kernel, cols, groups, lens.shape[0]),
        grid=(pl.cdiv(count, block),),
        in_specs=[
            smem, smem, smem,
            pl.BlockSpec((block, channels), lambda b: (b, 0)),
            pl.BlockSpec((1, channels), lambda b: (0, 0)),
            pl.BlockSpec(w_left.shape, lambda b: (0, 0)),
            pl.BlockSpec(w_right.shape, lambda b: (0, 0)),
        ],
        out_specs=[pl.BlockSpec((block, channels), lambda b: (b, 0))]
        + [pl.BlockSpec((2 * own, block), lambda b: (0, b))] * groups
        + [pl.BlockSpec((own, block), lambda b: (0, b))] * groups,
        out_shape=[jax.ShapeDtypeStruct((count, channels), jnp.bfloat16)]
        + [jax.ShapeDtypeStruct((2 * own, count), jnp.bfloat16)] * groups
        + [jax.ShapeDtypeStruct((own, count), jnp.bfloat16)] * groups,
        scratch_shapes=[pltpu.VMEM((groups, 2 * own, block), jnp.bfloat16)],
        compiler_params=pltpu.CompilerParams(vmem_limit_bytes=VMEM_FIRST),
    )(lens, resolved, place, pair, gain, w_left, w_right)


def unpack(got_ref, held_refs, block, rows, cols, step):
    tiles = pl.cdiv(cols, LANES)
    flat = rows * cols
    height = got_ref.shape[0]
    ch = height // len(held_refs)
    lane = lax.broadcasted_iota(jnp.int32, (height, LANES), 1)
    seen = {}

    def tile_of(t):
        if t not in seen:
            width = min(LANES, flat - t * LANES)
            got = got_ref[:, pl.ds(t * LANES, width)].astype(jnp.float32)
            if width < LANES:
                got = jnp.concatenate([got, jnp.zeros((height, LANES - width), jnp.float32)], axis=1)
            seen[t] = got
        return seen[t]

    for i in range(rows):
        for tt in range(tiles):
            length = min(LANES, cols - LANES * tt)
            t0, off = divmod(cols * i + LANES * tt, LANES)
            piece = tile_of(t0)
            if off:
                piece = pltpu.roll(piece, LANES - off, 1)
            if off + length > LANES:
                piece = jnp.where(lane < LANES - off, piece, pltpu.roll(tile_of(t0 + 1), LANES - off, 1))
            if length < LANES:
                piece = jnp.where(lane < length, piece, 0.0)
            base = pl.multiple_of((block * rows + i) * step, 8)
            for n, held in enumerate(held_refs):
                held[tt, pl.ds(base, ch), :] = piece[n * ch:(n + 1) * ch]


def pack(held, store, block, rows, cols, step, ch):
    tiles = pl.cdiv(cols, LANES)
    flat = rows * cols
    lane = lax.broadcasted_iota(jnp.int32, (ch, LANES), 1)
    for t in range(pl.cdiv(flat, LANES)):
        tile = None
        for i in range(rows):
            for tt in range(tiles):
                shift = cols * i + LANES * tt - LANES * t
                length = min(LANES, cols - LANES * tt)
                if shift >= LANES or shift + length <= 0:
                    continue
                base = pl.multiple_of((block * rows + i) * step, 8)
                piece = held[tt, pl.ds(base, ch), :]
                if shift % LANES:
                    piece = pltpu.roll(piece, shift % LANES, 1)
                tile = piece if tile is None else jnp.where(lane < shift, tile, piece)
        width = min(LANES, flat - t * LANES)
        store(t, width, tile[:, :width].astype(jnp.bfloat16))


def channel_of(held, d, count, step):
    lines = [held[t, pl.ds(d, count, stride=step), :] for t in range(held.shape[0])]
    return jnp.concatenate(lines, axis=1)


def multiply(left_ref, right_s, prod_s, ch, step):
    count = left_ref.shape[1]
    pad = right_s.shape[0] * LANES - count
    for d in range(ch):
        right = channel_of(right_s, d, count, step)
        if pad:
            right = jnp.concatenate([right, jnp.zeros((pad, right.shape[1]), jnp.float32)], axis=0)
        prod = lax.dot_general(
            left_ref[d], right.astype(jnp.bfloat16), (((1,), (1,)), ((), ())), preferred_element_type=jnp.float32
        )
        for t in range(prod_s.shape[0]):
            prod_s[t, pl.ds(d, count, stride=step), :] = prod[:, t * LANES:(t + 1) * LANES]


def near_kernel(groups, rows, cols, place_ref, *refs):
    got_refs = refs[:groups]
    left_ref, near_ref, left_s, right_s, prod_s = refs[groups:]
    ch = near_ref.shape[1]
    step = left_s.shape[1] // (groups * rows)
    for u in range(groups):
        unpack(got_refs[u], (left_s, right_s), jnp.bitwise_xor(place_ref[2], u), rows, cols, step)
    for d in range(ch):
        left_ref[d] = channel_of(left_s, d, groups * rows, step).astype(jnp.bfloat16)
    multiply(left_ref, right_s, prod_s, ch, step)
    for u in range(groups):
        def store(t, width, tile):
            near_ref[u, :, pl.ds(t * LANES, width)] = tile
        pack(prod_s, store, jnp.bitwise_xor(place_ref[2], u), rows, cols, step, ch)


def far_kernel(groups, rows, cols, place_ref, left_ref, near_ref, *refs):
    got_refs = refs[:groups]
    keep_ref, send_ref, right_s, prod_s, pair_s = refs[groups:]
    ch = near_ref.shape[1]
    step = right_s.shape[1] // (groups * rows)
    far_at = place_ref[3]
    pair_s[1 - far_at] = near_ref[...]
    for u in range(groups):
        unpack(got_refs[u], (right_s,), jnp.bitwise_xor(place_ref[2], u), rows, cols, step)
    multiply(left_ref, right_s, prod_s, ch, step)
    for u in range(groups):
        def store(t, width, tile):
            pair_s[far_at, u, :, pl.ds(t * LANES, width)] = tile
        pack(prod_s, store, jnp.bitwise_xor(place_ref[2], u), rows, cols, step, ch)
    keep_ref[...] = pair_s[0]
    send_ref[...] = pair_s[1]


def make_near(got, place, rows, cols):
    groups = len(got)
    both, flat = got[0].shape
    ch = both // 2
    count = groups * rows
    tiles = pl.cdiv(cols, LANES)
    held = pltpu.VMEM((tiles, count * ceil_to(ch, 8), LANES), jnp.float32)
    whole = pl.BlockSpec(memory_space=pltpu.VMEM)
    return pl.pallas_call(
        functools.partial(near_kernel, groups, rows, cols),
        in_specs=[pl.BlockSpec(memory_space=pltpu.SMEM)] + [whole] * groups,
        out_specs=[whole] * 2,
        out_shape=[
            jax.ShapeDtypeStruct((ch, count, tiles * LANES), jnp.bfloat16),
            jax.ShapeDtypeStruct((groups, ch, flat), jnp.bfloat16),
        ],
        scratch_shapes=[held, held, held],
        compiler_params=pltpu.CompilerParams(vmem_limit_bytes=VMEM_LIMIT),
    )(place, *got)


def make_far(got, place, left, near, rows, cols):
    groups = len(got)
    ch, flat = got[0].shape
    tiles = pl.cdiv(cols, LANES)
    held = pltpu.VMEM((tiles, groups * rows * ceil_to(ch, 8), LANES), jnp.float32)
    whole = pl.BlockSpec(memory_space=pltpu.VMEM)
    return pl.pallas_call(
        functools.partial(far_kernel, groups, rows, cols),
        in_specs=[pl.BlockSpec(memory_space=pltpu.SMEM)] + [whole] * (groups + 2),
        out_specs=[whole] * 2,
        out_shape=[jax.ShapeDtypeStruct((groups, ch, flat), jnp.bfloat16)] * 2,
        scratch_shapes=[held, held, pltpu.VMEM((2, groups, ch, flat), jnp.bfloat16)],
        compiler_params=pltpu.CompilerParams(vmem_limit_bytes=VMEM_LIMIT),
    )(place, left, near, *got)


def add_kernel(a_ref, b_ref, *out_refs):
    for u, out_ref in enumerate(out_refs):
        out_ref[...] = (a_ref[u].astype(jnp.float32) + b_ref[u].astype(jnp.float32)).astype(out_ref.dtype)


def make_sums(a, b):
    groups, ch, flat = a.shape
    whole = pl.BlockSpec(memory_space=pltpu.VMEM)
    return pl.pallas_call(
        add_kernel,
        in_specs=[whole] * 2,
        out_specs=[whole] * groups,
        out_shape=[jax.ShapeDtypeStruct((ch, flat), a.dtype)] * groups,
        compiler_params=pltpu.CompilerParams(vmem_limit_bytes=VMEM_LIMIT),
    )(a, b)


def update_kernel(n_dev, place_ref, gain_ref, w_ref, gate_ref, *refs):
    prod_refs, out_ref, held = refs[:n_dev], refs[n_dev], refs[n_dev + 1]
    for s in range(n_dev):
        held[jnp.bitwise_xor(place_ref[2], s)] = prod_refs[s][...].astype(jnp.float32)
    prod = held[...].reshape(-1, held.shape[2])
    mean = jnp.mean(prod, axis=0, keepdims=True)
    centred = prod - mean
    variance = jnp.mean(centred * centred, axis=0, keepdims=True)
    normed = (centred * lax.rsqrt(variance + EPS) * gain_ref[...]).astype(jnp.bfloat16)
    projected = lax.dot_general(normed, w_ref[...], (((0,), (0,)), ((), ())), preferred_element_type=jnp.float32)
    out_ref[...] = (gate_ref[...] * projected).astype(out_ref.dtype)


def make_update(prods, place, gain, w_out, gate):
    n_dev = len(prods)
    ch, count = prods[0].shape
    channels = w_out.shape[1]
    block = 512
    return pl.pallas_call(
        functools.partial(update_kernel, n_dev),
        grid=(pl.cdiv(count, block),),
        in_specs=[
            pl.BlockSpec(memory_space=pltpu.SMEM),
            pl.BlockSpec((n_dev * ch, 1), lambda b: (0, 0)),
            pl.BlockSpec(w_out.shape, lambda b: (0, 0)),
            pl.BlockSpec((block, channels), lambda b: (b, 0)),
        ]
        + [pl.BlockSpec((ch, block), lambda b: (0, b))] * n_dev,
        out_specs=pl.BlockSpec((block, channels), lambda b: (b, 0)),
        out_shape=jax.ShapeDtypeStruct((count, channels), jnp.bfloat16),
        scratch_shapes=[pltpu.VMEM((n_dev, ch, block), jnp.float32)],
        compiler_params=pltpu.CompilerParams(vmem_limit_bytes=VMEM_LIMIT),
    )(place, gain, w_out, gate, *prods)


def swap(value, shift):
    return lax.ppermute(value, "row", [(r, r ^ shift) for r in range(lax.axis_size("row"))])


def shards(pair_act, chain_lengths, resolved, in_gain, out_gain, w_left, w_right, w_gate, w_out):
    rows, cols, channels = pair_act.shape
    hidden = w_out.shape[0]
    groups = lax.axis_size("row") // 2
    row, col = lax.axis_index("row"), lax.axis_index("col")
    far_at = (col == row // groups).astype(jnp.int32)
    place = jnp.stack([row * rows, col * cols, lax.rem(row, groups), far_at]).astype(jnp.int32)
    normed, *edges = make_edges(
        pair_act.reshape(rows * cols, channels), chain_lengths, resolved, place,
        in_gain.reshape(1, channels), w_left, w_right, groups, cols,
    )
    both, right = edges[:groups], edges[groups:]
    far_got = [swap(right[u], groups + u) for u in range(groups)]
    near_got = [both[0]] + [swap(both[u], u) for u in range(1, groups)]
    gate = jax.nn.sigmoid(jnp.dot(normed, w_gate, preferred_element_type=jnp.float32))
    left, near = make_near(near_got, place, rows, cols)
    keep, send = make_far(far_got, place, left, near, rows, cols)
    sums = make_sums(keep, lax.ppermute(send, "col", [(0, 1), (1, 0)]))
    returned = [sums[0]] + [swap(sums[u], u) for u in range(1, groups)]
    update = make_update(returned, place, out_gain.reshape(hidden, 1), w_out, gate)
    return update.reshape(rows, cols, channels)


def solution(mesh):
    return jax.shard_map(
        shards,
        mesh=mesh,
        in_specs=(P(("grp", "row"), "col", None), P("grp"), P("grp"), P(), P(), P(), P(), P(), P()),
        out_specs=P(("grp", "row"), "col", None),
        check_vma=False,
    )
```

```python
import functools

import jax
import jax.numpy as jnp
from jax import lax
from jax.experimental import pallas as pl
from jax.experimental.pallas import tpu as pltpu
from jax.sharding import PartitionSpec as P

EPS = 1e-05
LANES = 128
VMEM_LIMIT = 32 * 1024 * 1024
VMEM_FIRST = 60 * 1024 * 1024


def ceil_to(n, m):
    return -(-n // m) * m


def place_of(groups, rows, cols):
    row, col = lax.axis_index("row"), lax.axis_index("col")
    return row * rows, col * cols, lax.rem(row, groups), row // groups, col


def mask_of(cols, first_row, first_col, lens_ref, res_ref, block):
    position = pl.program_id(0) * block + lax.broadcasted_iota(jnp.int32, (8, block), 1)
    i_here = jnp.floor((position.astype(jnp.float32) + 0.5) * (1.0 / cols)).astype(jnp.int32)
    i_at = first_row + i_here
    k_at = first_col + position - i_here * cols
    i_ok = jnp.zeros((8, block), jnp.float32)
    k_ok = jnp.zeros((8, block), jnp.float32)
    start = 0
    for q in range(lens_ref.shape[0]):
        length = lens_ref[q]
        stop = start + jnp.minimum(length, res_ref[q])
        i_ok = jnp.where((i_at >= start) & (i_at < stop), 1.0, i_ok)
        k_ok = jnp.where((k_at >= start) & (k_at < stop), 1.0, k_ok)
        start = start + length
    return i_ok * k_ok


def edge_of(normed, w_ref, mask, groups):
    hidden = w_ref.shape[1] // 2
    block = normed.shape[0]
    projected = lax.dot_general(w_ref[...], normed, (((0,), (1,)), ((), ())), preferred_element_type=jnp.float32)
    edge = jax.nn.sigmoid(projected[:hidden]) * projected[hidden:]
    edge = edge.reshape(hidden // 8, 8, block) * mask[None]
    return edge.reshape(groups, hidden // groups, block).astype(jnp.bfloat16)


def right_kernel(groups, rows, cols, lens_ref, res_ref, x_ref, gain_ref, w_ref, normed_ref, *refs):
    right_refs, held = refs[:groups], refs[groups]
    first_row, first_col, mine, _, _ = place_of(groups, rows, cols)
    x = x_ref[...].astype(jnp.float32)
    mean = jnp.mean(x, axis=-1, keepdims=True)
    centred = x - mean
    variance = jnp.mean(centred * centred, axis=-1, keepdims=True)
    normed = (centred * lax.rsqrt(variance + EPS) * gain_ref[...]).astype(jnp.bfloat16)
    normed_ref[...] = normed
    mask = mask_of(cols, first_row, first_col, lens_ref, res_ref, x.shape[0])
    held[...] = edge_of(normed, w_ref, mask, groups)
    for u in range(groups):
        right_refs[u][...] = held[jnp.bitwise_xor(mine, u)]


def left_kernel(groups, rows, cols, lens_ref, res_ref, normed_ref, w_ref, *refs):
    right_refs, both_ref = refs[:groups], refs[groups]
    first_row, first_col, mine, _, _ = place_of(groups, rows, cols)
    own = both_ref.shape[1] // 2
    mask = mask_of(cols, first_row, first_col, lens_ref, res_ref, normed_ref.shape[0])
    both_ref[:, :own] = edge_of(normed_ref[...], w_ref, mask, groups)
    for u in range(groups):
        both_ref[jnp.bitwise_xor(mine, u), own:] = right_refs[u][...]


def make_right(pair, lens, resolved, gain, w_right, groups, rows, cols):
    count, channels = pair.shape
    own = w_right.shape[1] // 2 // groups
    block = 512
    smem = pl.BlockSpec(memory_space=pltpu.SMEM)
    return pl.pallas_call(
        functools.partial(right_kernel, groups, rows, cols),
        grid=(pl.cdiv(count, block),),
        in_specs=[
            smem, smem,
            pl.BlockSpec((block, channels), lambda b: (b, 0)),
            pl.BlockSpec((1, channels), lambda b: (0, 0)),
            pl.BlockSpec(w_right.shape, lambda b: (0, 0)),
        ],
        out_specs=[pl.BlockSpec((block, channels), lambda b: (b, 0))]
        + [pl.BlockSpec((own, block), lambda b: (0, b))] * groups,
        out_shape=[jax.ShapeDtypeStruct((count, channels), jnp.bfloat16)]
        + [jax.ShapeDtypeStruct((own, count), jnp.bfloat16)] * groups,
        scratch_shapes=[pltpu.VMEM((groups, own, block), jnp.bfloat16)],
        compiler_params=pltpu.CompilerParams(vmem_limit_bytes=VMEM_FIRST),
    )(lens, resolved, pair, gain, w_right)


def make_left(normed, lens, resolved, w_left, right, rows, cols):
    groups = len(right)
    count, channels = normed.shape
    own = w_left.shape[1] // 2 // groups
    block = 512
    smem = pl.BlockSpec(memory_space=pltpu.SMEM)
    return pl.pallas_call(
        functools.partial(left_kernel, groups, rows, cols),
        grid=(pl.cdiv(count, block),),
        in_specs=[
            smem, smem,
            pl.BlockSpec((block, channels), lambda b: (b, 0)),
            pl.BlockSpec(w_left.shape, lambda b: (0, 0)),
        ]
        + [pl.BlockSpec((own, block), lambda b: (0, b))] * groups,
        out_specs=pl.BlockSpec((groups, 2 * own, block), lambda b: (0, 0, b)),
        out_shape=jax.ShapeDtypeStruct((groups, 2 * own, count), jnp.bfloat16),
        compiler_params=pltpu.CompilerParams(vmem_limit_bytes=VMEM_FIRST),
    )(lens, resolved, normed, w_left, *right)


def unpack(got_ref, held_refs, block, rows, cols, step):
    tiles = pl.cdiv(cols, LANES)
    flat = rows * cols
    height = got_ref.shape[0]
    ch = height // len(held_refs)
    lane = lax.broadcasted_iota(jnp.int32, (height, LANES), 1)
    seen = {}

    def tile_of(t):
        if t not in seen:
            width = min(LANES, flat - t * LANES)
            got = got_ref[:, pl.ds(t * LANES, width)].astype(jnp.float32)
            if width < LANES:
                got = jnp.concatenate([got, jnp.zeros((height, LANES - width), jnp.float32)], axis=1)
            seen[t] = got
        return seen[t]

    for i in range(rows):
        for tt in range(tiles):
            length = min(LANES, cols - LANES * tt)
            t0, off = divmod(cols * i + LANES * tt, LANES)
            piece = tile_of(t0)
            if off:
                piece = pltpu.roll(piece, LANES - off, 1)
            if off + length > LANES:
                piece = jnp.where(lane < LANES - off, piece, pltpu.roll(tile_of(t0 + 1), LANES - off, 1))
            if length < LANES:
                piece = jnp.where(lane < length, piece, 0.0)
            base = pl.multiple_of((block * rows + i) * step, 8)
            for n, held in enumerate(held_refs):
                held[tt, pl.ds(base, ch), :] = piece[n * ch:(n + 1) * ch]


def pack(held, store, block, rows, cols, step, ch):
    tiles = pl.cdiv(cols, LANES)
    flat = rows * cols
    lane = lax.broadcasted_iota(jnp.int32, (ch, LANES), 1)
    for t in range(pl.cdiv(flat, LANES)):
        tile = None
        for i in range(rows):
            for tt in range(tiles):
                shift = cols * i + LANES * tt - LANES * t
                length = min(LANES, cols - LANES * tt)
                if shift >= LANES or shift + length <= 0:
                    continue
                base = pl.multiple_of((block * rows + i) * step, 8)
                piece = held[tt, pl.ds(base, ch), :]
                if shift % LANES:
                    piece = pltpu.roll(piece, shift % LANES, 1)
                tile = piece if tile is None else jnp.where(lane < shift, tile, piece)
        width = min(LANES, flat - t * LANES)
        store(t, width, tile[:, :width].astype(jnp.bfloat16))


def channel_of(held, d, count, step):
    lines = [held[t, pl.ds(d, count, stride=step), :] for t in range(held.shape[0])]
    return jnp.concatenate(lines, axis=1)


def multiply(left_ref, right_s, prod_s, ch, step):
    count = left_ref.shape[1]
    pad = right_s.shape[0] * LANES - count
    for d in range(ch):
        right = channel_of(right_s, d, count, step)
        if pad:
            right = jnp.concatenate([right, jnp.zeros((pad, right.shape[1]), jnp.float32)], axis=0)
        prod = lax.dot_general(
            left_ref[d], right.astype(jnp.bfloat16), (((1,), (1,)), ((), ())), preferred_element_type=jnp.float32
        )
        for t in range(prod_s.shape[0]):
            prod_s[t, pl.ds(d, count, stride=step), :] = prod[:, t * LANES:(t + 1) * LANES]


def near_kernel(groups, rows, cols, got_ref, left_ref, near_ref, left_s, right_s, prod_s):
    mine = place_of(groups, rows, cols)[2]
    ch = near_ref.shape[1]
    step = left_s.shape[1] // (groups * rows)
    for u in range(groups):
        unpack(got_ref.at[u], (left_s, right_s), u, rows, cols, step)
    for d in range(ch):
        left_ref[d] = channel_of(left_s, d, groups * rows, step).astype(jnp.bfloat16)
    multiply(left_ref, right_s, prod_s, ch, step)
    for u in range(groups):
        def store(t, width, tile):
            near_ref[u, :, pl.ds(t * LANES, width)] = tile
        pack(prod_s, store, jnp.bitwise_xor(mine, u), rows, cols, step, ch)


def far_kernel(groups, rows, cols, left_ref, near_ref, *refs):
    got_refs = refs[:groups]
    keep_ref, send_ref, right_s, prod_s, pair_s = refs[groups:]
    ch = near_ref.shape[1]
    step = right_s.shape[1] // (groups * rows)
    _, _, mine, half, col = place_of(groups, rows, cols)
    far_at = (col == half).astype(jnp.int32)
    pair_s[1 - far_at] = near_ref[...]
    for u in range(groups):
        unpack(got_refs[u], (right_s,), jnp.bitwise_xor(mine, u), rows, cols, step)
    multiply(left_ref, right_s, prod_s, ch, step)
    for u in range(groups):
        def store(t, width, tile):
            pair_s[far_at, u, :, pl.ds(t * LANES, width)] = tile
        pack(prod_s, store, jnp.bitwise_xor(mine, u), rows, cols, step, ch)
    keep_ref[...] = pair_s[0]
    send_ref[...] = pair_s[1]


def make_near(got, rows, cols):
    groups, both, flat = got.shape
    ch = both // 2
    count = groups * rows
    tiles = pl.cdiv(cols, LANES)
    held = pltpu.VMEM((tiles, count * ceil_to(ch, 8), LANES), jnp.float32)
    whole = pl.BlockSpec(memory_space=pltpu.VMEM)
    return pl.pallas_call(
        functools.partial(near_kernel, groups, rows, cols),
        in_specs=[whole],
        out_specs=[whole] * 2,
        out_shape=[
            jax.ShapeDtypeStruct((ch, count, tiles * LANES), jnp.bfloat16),
            jax.ShapeDtypeStruct((groups, ch, flat), jnp.bfloat16),
        ],
        scratch_shapes=[held, held, held],
        compiler_params=pltpu.CompilerParams(vmem_limit_bytes=VMEM_LIMIT),
    )(got)


def make_far(got, left, near, rows, cols):
    groups = len(got)
    ch, flat = got[0].shape
    tiles = pl.cdiv(cols, LANES)
    held = pltpu.VMEM((tiles, groups * rows * ceil_to(ch, 8), LANES), jnp.float32)
    whole = pl.BlockSpec(memory_space=pltpu.VMEM)
    return pl.pallas_call(
        functools.partial(far_kernel, groups, rows, cols),
        in_specs=[whole] * (groups + 2),
        out_specs=[whole] * 2,
        out_shape=[jax.ShapeDtypeStruct((groups, ch, flat), jnp.bfloat16)] * 2,
        scratch_shapes=[held, held, pltpu.VMEM((2, groups, ch, flat), jnp.bfloat16)],
        compiler_params=pltpu.CompilerParams(vmem_limit_bytes=VMEM_LIMIT),
    )(left, near, *got)


def add_kernel(a_ref, b_ref, *out_refs):
    for u, out_ref in enumerate(out_refs):
        out_ref[...] = (a_ref[u].astype(jnp.float32) + b_ref[u].astype(jnp.float32)).astype(out_ref.dtype)


def make_sums(a, b):
    groups, ch, flat = a.shape
    whole = pl.BlockSpec(memory_space=pltpu.VMEM)
    return pl.pallas_call(
        add_kernel,
        in_specs=[whole] * 2,
        out_specs=[whole] * groups,
        out_shape=[jax.ShapeDtypeStruct((ch, flat), a.dtype)] * groups,
        compiler_params=pltpu.CompilerParams(vmem_limit_bytes=VMEM_LIMIT),
    )(a, b)


def update_kernel(groups, rows, cols, gain_ref, w_ref, gate_ref, *refs):
    prod_refs, out_ref, held = refs[:groups], refs[groups], refs[groups + 1]
    mine = place_of(groups, rows, cols)[2]
    for u in range(groups):
        held[jnp.bitwise_xor(mine, u)] = prod_refs[u][...].astype(jnp.float32)
    prod = held[...].reshape(-1, held.shape[2])
    mean = jnp.mean(prod, axis=0, keepdims=True)
    centred = prod - mean
    variance = jnp.mean(centred * centred, axis=0, keepdims=True)
    normed = (centred * lax.rsqrt(variance + EPS) * gain_ref[...]).astype(jnp.bfloat16)
    projected = lax.dot_general(normed, w_ref[...], (((0,), (0,)), ((), ())), preferred_element_type=jnp.float32)
    out_ref[...] = (gate_ref[...] * projected).astype(out_ref.dtype)


def make_update(prods, gain, w_out, gate, rows, cols):
    groups = len(prods)
    ch, count = prods[0].shape
    channels = w_out.shape[1]
    block = 512
    return pl.pallas_call(
        functools.partial(update_kernel, groups, rows, cols),
        grid=(pl.cdiv(count, block),),
        in_specs=[
            pl.BlockSpec((groups * ch, 1), lambda b: (0, 0)),
            pl.BlockSpec(w_out.shape, lambda b: (0, 0)),
            pl.BlockSpec((block, channels), lambda b: (b, 0)),
        ]
        + [pl.BlockSpec((ch, block), lambda b: (0, b))] * groups,
        out_specs=pl.BlockSpec((block, channels), lambda b: (b, 0)),
        out_shape=jax.ShapeDtypeStruct((count, channels), jnp.bfloat16),
        scratch_shapes=[pltpu.VMEM((groups, ch, block), jnp.float32)],
        compiler_params=pltpu.CompilerParams(vmem_limit_bytes=VMEM_LIMIT),
    )(gain, w_out, gate, *prods)


def swap(value, shift):
    return lax.ppermute(value, "row", [(r, r ^ shift) for r in range(lax.axis_size("row"))])


def shards(pair_act, chain_lengths, resolved, in_gain, out_gain, w_left, w_right, w_gate, w_out):
    rows, cols, channels = pair_act.shape
    hidden = w_out.shape[0]
    groups = lax.axis_size("row") // 2
    halves = [[h * groups + r for r in range(groups)] for h in range(2)]
    normed, *right = make_right(
        pair_act.reshape(rows * cols, channels), chain_lengths, resolved,
        in_gain.reshape(1, channels), w_right, groups, rows, cols,
    )
    far_got = [swap(right[u], groups + u) for u in range(groups)]
    both = make_left(normed, chain_lengths, resolved, w_left, right, rows, cols)
    near_got = lax.all_to_all(both, "row", split_axis=0, concat_axis=0, tiled=True, axis_index_groups=halves)
    gate = jax.nn.sigmoid(jnp.dot(normed, w_gate, preferred_element_type=jnp.float32))
    left, near = make_near(near_got, rows, cols)
    keep, send = make_far(far_got, left, near, rows, cols)
    sums = make_sums(keep, lax.ppermute(send, "col", [(0, 1), (1, 0)]))
    returned = [sums[0]] + [swap(sums[u], u) for u in range(1, groups)]
    update = make_update(returned, out_gain.reshape(hidden, 1), w_out, gate, rows, cols)
    return update.reshape(rows, cols, channels)


def solution(mesh):
    return jax.shard_map(
        shards,
        mesh=mesh,
        in_specs=(P(("grp", "row"), "col", None), P("grp"), P("grp"), P(), P(), P(), P(), P(), P()),
        out_specs=P(("grp", "row"), "col", None),
        check_vma=False,
    )
```

```python
import functools

import jax
import jax.numpy as jnp
from jax import lax
from jax.experimental import pallas as pl
from jax.experimental.pallas import tpu as pltpu
from jax.sharding import PartitionSpec as P

EPS = 1e-05
LANES = 128
VMEM_LIMIT = 32 * 1024 * 1024
VMEM_FIRST = 60 * 1024 * 1024


def ceil_to(n, m):
    return -(-n // m) * m


def place_of(groups, rows, cols):
    row, col = lax.axis_index("row"), lax.axis_index("col")
    return row * rows, col * cols, lax.rem(row, groups), row // groups, col


def sigmoid(x):
    return 0.5 + 0.5 * jnp.tanh(0.5 * x)


def mask_of(cols, first_row, first_col, lens_ref, res_ref, at, block):
    position = at + lax.broadcasted_iota(jnp.int32, (8, block), 1)
    i_here = jnp.floor((position.astype(jnp.float32) + 0.5) * (1.0 / cols)).astype(jnp.int32)
    i_at = first_row + i_here
    k_at = first_col + position - i_here * cols
    i_ok = jnp.zeros((8, block), jnp.float32)
    k_ok = jnp.zeros((8, block), jnp.float32)
    start = 0
    for q in range(lens_ref.shape[0]):
        length = lens_ref[q]
        stop = start + jnp.minimum(length, res_ref[q])
        i_ok = jnp.where((i_at >= start) & (i_at < stop), 1.0, i_ok)
        k_ok = jnp.where((k_at >= start) & (k_at < stop), 1.0, k_ok)
        start = start + length
    return i_ok * k_ok


def edge_of(normed, w_ref, mask, groups):
    hidden = w_ref.shape[1] // 2
    block = normed.shape[0]
    projected = lax.dot_general(w_ref[...], normed, (((0,), (1,)), ((), ())), preferred_element_type=jnp.float32)
    edge = sigmoid(projected[:hidden]) * projected[hidden:]
    edge = edge.reshape(hidden // 8, 8, block) * mask[None]
    return edge.reshape(groups, hidden // groups, block).astype(jnp.bfloat16)


def edges_kernel(groups, rows, cols, chunks, pair_ref, gain_ref, wl_ref, wr_ref, lens_ref, res_ref, normed_ref, *refs):
    both_refs, right_refs = refs[:groups], refs[groups:2 * groups]
    x_s, gain_s, wl_s, wr_s, lens_s, res_s, normed_s, held, in_sems, out_sems = refs[2 * groups:]
    count = rows * cols
    first_row, first_col, mine, _, _ = place_of(groups, rows, cols)
    own = wl_ref.shape[1] // 2 // groups
    loads = [
        pltpu.make_async_copy(src, dst, in_sems.at[n])
        for n, (src, dst) in enumerate(
            [(gain_ref, gain_s), (lens_ref, lens_s), (res_ref, res_s), (wr_ref, wr_s), (wl_ref, wl_s)]
        )
    ]
    pieces = [
        pltpu.make_async_copy(pair_ref.at[pl.ds(at, size)], x_s.at[pl.ds(at, size)], in_sems.at[len(loads) + n])
        for n, (at, size) in enumerate(chunks)
    ]
    for copy in pieces[:1] + loads + pieces[1:]:
        copy.start()
    block = chunks[0][1]
    spare = x_s.shape[0] - count
    if spare:
        x_s[pl.ds(count, spare)] = jnp.zeros((spare, x_s.shape[1]), x_s.dtype)
    stores = []
    for n, (at, size) in enumerate(chunks):
        pieces[n].wait()
        x = x_s[pl.ds(at, block)].astype(jnp.float32)
        mean = jnp.mean(x, axis=-1, keepdims=True)
        centred = x - mean
        variance = jnp.mean(centred * centred, axis=-1, keepdims=True)
        if n == 0:
            for copy in loads:
                copy.wait()
        normed = (centred * lax.rsqrt(variance + EPS) * gain_s[...]).astype(jnp.bfloat16)
        normed_s[pl.ds(at, block)] = normed
        mask = mask_of(cols, first_row, first_col, lens_s, res_s, at, block)
        lanes = pl.ds(at, block)
        held[:, own:, lanes] = edge_of(normed, wr_s, mask, groups)
        held[:, :own, lanes] = edge_of(normed, wl_s, mask, groups)
        sent = [(normed_s.at[pl.ds(at, size)], normed_ref.at[pl.ds(at, size)])]
        for u in range(groups):
            group = jnp.bitwise_xor(mine, u)
            sent.append((held.at[group, pl.ds(own, own), lanes], right_refs[u].at[:, lanes]))
            sent.append((held.at[group, :, lanes], both_refs[u].at[:, lanes]))
        for m, (src, dst) in enumerate(sent):
            stores.append(pltpu.make_async_copy(src, dst, out_sems.at[n, m]))
            stores[-1].start()
    for copy in stores:
        copy.wait()


def make_edges(pair, lens, resolved, gain, w_left, w_right, groups, rows, cols):
    count, channels = pair.shape
    own = w_left.shape[1] // 2 // groups
    block = 512
    flat = ceil_to(count, block)
    chunks = [(at, min(block, count - at)) for at in range(0, count, block)]
    here = pl.BlockSpec(memory_space=pltpu.HBM)
    return pl.pallas_call(
        functools.partial(edges_kernel, groups, rows, cols, chunks),
        in_specs=[here] * 6,
        out_specs=[here] * (1 + 2 * groups),
        out_shape=[jax.ShapeDtypeStruct((count, channels), jnp.bfloat16)]
        + [jax.ShapeDtypeStruct((2 * own, flat), jnp.bfloat16)] * groups
        + [jax.ShapeDtypeStruct((own, flat), jnp.bfloat16)] * groups,
        scratch_shapes=[
            pltpu.VMEM((flat, channels), pair.dtype),
            pltpu.VMEM(gain.shape, gain.dtype),
            pltpu.VMEM(w_left.shape, w_left.dtype),
            pltpu.VMEM(w_right.shape, w_right.dtype),
            pltpu.SMEM(lens.shape, lens.dtype),
            pltpu.SMEM(resolved.shape, resolved.dtype),
            pltpu.VMEM((flat, channels), jnp.bfloat16),
            pltpu.VMEM((groups, 2 * own, flat), jnp.bfloat16),
            pltpu.SemaphoreType.DMA((5 + len(chunks),)),
            pltpu.SemaphoreType.DMA((len(chunks), 1 + 2 * groups)),
        ],
        compiler_params=pltpu.CompilerParams(vmem_limit_bytes=VMEM_FIRST),
    )(pair, gain, w_left, w_right, lens, resolved)


def unpack(got_ref, held_refs, block, rows, cols, step):
    tiles = pl.cdiv(cols, LANES)
    ch = got_ref.shape[0] // len(held_refs)
    lane = lax.broadcasted_iota(jnp.int32, (ch, LANES), 1)
    for n, held in enumerate(held_refs):
        seen = {}

        def tile_of(t):
            if t not in seen:
                seen[t] = got_ref[n * ch:(n + 1) * ch, pl.ds(t * LANES, LANES)].astype(jnp.float32)
            return seen[t]

        for i in range(rows):
            for tt in range(tiles):
                length = min(LANES, cols - LANES * tt)
                t0, off = divmod(cols * i + LANES * tt, LANES)
                piece = tile_of(t0)
                if off:
                    piece = pltpu.roll(piece, LANES - off, 1)
                if off + length > LANES:
                    piece = jnp.where(lane < LANES - off, piece, pltpu.roll(tile_of(t0 + 1), LANES - off, 1))
                if length < LANES and n == 0:
                    piece = jnp.where(lane < length, piece, 0.0)
                base = pl.multiple_of((block * rows + i) * step, 8)
                held[tt, pl.ds(base, ch), :] = piece


def pack(held, out_ref, u, block, rows, cols, step):
    tiles = pl.cdiv(cols, LANES)
    ch = out_ref.shape[1]
    lane = lax.broadcasted_iota(jnp.int32, (ch, LANES), 1)
    for t in range(out_ref.shape[2] // LANES):
        tile = None
        for i in range(rows):
            for tt in range(tiles):
                shift = cols * i + LANES * tt - LANES * t
                length = min(LANES, cols - LANES * tt)
                if shift >= LANES or shift + length <= 0:
                    continue
                base = pl.multiple_of((block * rows + i) * step, 8)
                piece = held[tt, pl.ds(base, ch), :]
                if shift % LANES:
                    piece = pltpu.roll(piece, shift % LANES, 1)
                tile = piece if tile is None else jnp.where(lane < shift, tile, piece)
        if tile is None:
            tile = jnp.zeros((ch, LANES), jnp.float32)
        out_ref[u, :, pl.ds(t * LANES, LANES)] = tile.astype(jnp.bfloat16)


def channel_of(held, d, count, step):
    lines = [held[t, pl.ds(d, count, stride=step), :] for t in range(held.shape[0])]
    return jnp.concatenate(lines, axis=1).astype(jnp.bfloat16)


def near_kernel(groups, rows, cols, after_ref, *refs):
    got_refs = refs[:groups]
    left_ref, near_ref, left_s, right_s, prod_s = refs[groups:]
    mine = place_of(groups, rows, cols)[2]
    step = left_s.shape[1] // (groups * rows)
    for u in range(groups):
        unpack(got_refs[u], (left_s, right_s), jnp.bitwise_xor(mine, u), rows, cols, step)
    for d in range(near_ref.shape[1]):
        left_ref[d] = channel_of(left_s, d, groups * rows, step)
        multiply(left_ref[d], channel_of(right_s, d, groups * rows, step), prod_s, d, step)
    for u in range(groups):
        pack(prod_s, near_ref, u, jnp.bitwise_xor(mine, u), rows, cols, step)


def lines_kernel(groups, rows, cols, count, *refs):
    got_refs, lines_ref = refs[:count], refs[-1]
    mine = place_of(groups, rows, cols)[2]
    step = lines_ref.shape[1] // (count * rows)
    for u in range(count):
        block = jnp.bitwise_and(jnp.bitwise_xor(mine, u), count - 1)
        unpack(got_refs[u], (lines_ref,), block, rows, cols, step)


def multiply(left, right, prod_s, d, step):
    count = left.shape[0]
    pad = prod_s.shape[0] * LANES - count
    if pad:
        right = jnp.concatenate([right, jnp.zeros((pad, right.shape[1]), right.dtype)], axis=0)
    prod = lax.dot_general(left, right, (((1,), (1,)), ((), ())), preferred_element_type=jnp.float32)
    for t in range(prod_s.shape[0]):
        prod_s[t, pl.ds(d, count, stride=step), :] = prod[:, t * LANES:(t + 1) * LANES]


def cross_kernel(groups, rows, cols, left_ref, near_ref, early_ref, late_ref, keep_ref, send_ref, right_s, prod_s, pair_s):
    _, _, mine, half, col = place_of(groups, rows, cols)
    step = prod_s.shape[1] // (groups * rows)
    size = early_ref.shape[1]
    base = pl.multiple_of(mine // (groups // 2) * size, 8)
    right_s[:, pl.ds(base, size), :] = early_ref[...]
    right_s[:, pl.ds(pl.multiple_of(size - base, 8), size), :] = late_ref[...]
    for d in range(keep_ref.shape[1]):
        multiply(left_ref[d], channel_of(right_s, d, groups * rows, step), prod_s, d, step)
    for u in range(groups):
        pack(prod_s, pair_s, u, jnp.bitwise_xor(mine, u), rows, cols, step)
    near_kept = col == half
    keep_ref[...] = jnp.where(near_kept, near_ref[...], pair_s[...])
    send_ref[...] = jnp.where(near_kept, pair_s[...], near_ref[...])


def make_near(got, after, rows, cols):
    groups = len(got)
    both, flat = got[0].shape
    ch = both // 2
    count = groups * rows
    tiles = pl.cdiv(cols, LANES)
    held = pltpu.VMEM((tiles, count * ceil_to(ch, 8), LANES), jnp.float32)
    whole = pl.BlockSpec(memory_space=pltpu.VMEM)
    return pl.pallas_call(
        functools.partial(near_kernel, groups, rows, cols),
        in_specs=[pl.BlockSpec(memory_space=pl.ANY)] + [whole] * groups,
        out_specs=[whole] * 2,
        out_shape=[
            jax.ShapeDtypeStruct((ch, count, tiles * LANES), jnp.bfloat16),
            jax.ShapeDtypeStruct((groups, ch, flat), jnp.bfloat16),
        ],
        scratch_shapes=[held, held, held],
        compiler_params=pltpu.CompilerParams(vmem_limit_bytes=VMEM_LIMIT),
        cost_estimate=pl.CostEstimate(flops=10 ** 5, bytes_accessed=10 ** 5, transcendentals=0),
    )(after, *got)


def make_lines(got, groups, rows, cols, cost, after=()):
    ch = got[0].shape[0]
    whole = pl.BlockSpec(memory_space=pltpu.VMEM)
    lines = (pl.cdiv(cols, LANES), len(got) * rows * ceil_to(ch, 8), LANES)
    return pl.pallas_call(
        functools.partial(lines_kernel, groups, rows, cols, len(got)),
        in_specs=[whole] * len(got) + [pl.BlockSpec(memory_space=pl.ANY)] * len(after),
        out_specs=whole,
        out_shape=jax.ShapeDtypeStruct(lines, jnp.float32),
        compiler_params=pltpu.CompilerParams(vmem_limit_bytes=VMEM_LIMIT),
        cost_estimate=pl.CostEstimate(flops=10 ** 5, bytes_accessed=cost, transcendentals=0),
    )(*got, *after)


def make_cross(left, near, early, late, rows, cols):
    groups, ch, flat = near.shape
    whole = pl.BlockSpec(memory_space=pltpu.VMEM)
    held = pltpu.VMEM((pl.cdiv(cols, LANES), groups * rows * ceil_to(ch, 8), LANES), jnp.float32)
    return pl.pallas_call(
        functools.partial(cross_kernel, groups, rows, cols),
        in_specs=[whole] * 4,
        out_specs=[whole] * 2,
        out_shape=[jax.ShapeDtypeStruct(near.shape, near.dtype)] * 2,
        scratch_shapes=[held, held, pltpu.VMEM(near.shape, near.dtype)],
        compiler_params=pltpu.CompilerParams(vmem_limit_bytes=VMEM_LIMIT),
        cost_estimate=pl.CostEstimate(flops=10 ** 5, bytes_accessed=8 * 10 ** 6, transcendentals=0),
    )(left, near, early, late)


def add_kernel(a_ref, b_ref, *out_refs):
    for u, out_ref in enumerate(out_refs):
        out_ref[...] = (a_ref[u].astype(jnp.float32) + b_ref[u].astype(jnp.float32)).astype(out_ref.dtype)


def make_sums(a, b):
    groups, ch, flat = a.shape
    whole = pl.BlockSpec(memory_space=pltpu.VMEM)
    return pl.pallas_call(
        add_kernel,
        in_specs=[whole] * 2,
        out_specs=[whole] * groups,
        out_shape=[jax.ShapeDtypeStruct((ch, flat), a.dtype)] * groups,
        compiler_params=pltpu.CompilerParams(vmem_limit_bytes=VMEM_LIMIT),
        cost_estimate=pl.CostEstimate(flops=10 ** 5, bytes_accessed=10 ** 5, transcendentals=0),
    )(a, b)


def update_kernel(groups, rows, cols, chunks, gain_ref, w_ref, gate_ref, *refs):
    prod_refs = refs[:groups]
    out_ref, held, out_s, sems = refs[groups:]
    mine = place_of(groups, rows, cols)[2]
    ch = held.shape[1]
    block = held.shape[2]
    stores = []
    for n, (at, size) in enumerate(chunks):
        lanes = pl.ds(at, block)
        for u in range(groups):
            held[jnp.bitwise_xor(mine, u)] = prod_refs[u][:, lanes].astype(jnp.float32)
        prod = held[...].reshape(groups * ch, block)
        mean = jnp.mean(prod, axis=0, keepdims=True)
        centred = prod - mean
        variance = jnp.mean(centred * centred, axis=0, keepdims=True)
        normed = (centred * lax.rsqrt(variance + EPS) * gain_ref[...]).astype(jnp.bfloat16)
        projected = lax.dot_general(normed, w_ref[...], (((0,), (0,)), ((), ())), preferred_element_type=jnp.float32)
        out_s[pl.ds(at, size)] = (gate_ref[pl.ds(at, size)] * projected[:size]).astype(out_s.dtype)
        stores.append(pltpu.make_async_copy(out_s.at[pl.ds(at, size)], out_ref.at[pl.ds(at, size)], sems.at[n]))
        stores[-1].start()
    for copy in stores:
        copy.wait()


def make_update(prods, gain, w_out, gate, rows, cols):
    groups = len(prods)
    ch = prods[0].shape[0]
    count, channels = gate.shape
    block = 512
    chunks = [(at, min(block, count - at)) for at in range(0, count, block)]
    whole = pl.BlockSpec(memory_space=pltpu.VMEM)
    return pl.pallas_call(
        functools.partial(update_kernel, groups, rows, cols, chunks),
        in_specs=[whole] * (3 + groups),
        out_specs=pl.BlockSpec(memory_space=pltpu.HBM),
        out_shape=jax.ShapeDtypeStruct((count, channels), jnp.bfloat16),
        scratch_shapes=[
            pltpu.VMEM((groups, ch, block), jnp.float32),
            pltpu.VMEM((count, channels), jnp.bfloat16),
            pltpu.SemaphoreType.DMA((len(chunks),)),
        ],
        compiler_params=pltpu.CompilerParams(vmem_limit_bytes=VMEM_LIMIT),
    )(gain, w_out, gate, *prods)


def swap(value, shift):
    return lax.ppermute(value, "row", [(r, r ^ shift) for r in range(lax.axis_size("row"))])


def shards(pair_act, chain_lengths, resolved, in_gain, out_gain, w_left, w_right, w_gate, w_out):
    rows, cols, channels = pair_act.shape
    hidden = w_out.shape[0]
    groups = lax.axis_size("row") // 2
    normed, *edges = make_edges(
        pair_act.reshape(rows * cols, channels), chain_lengths, resolved,
        in_gain.reshape(1, channels), w_left, w_right, groups, rows, cols,
    )
    both, right = edges[:groups], edges[groups:]
    far_got = [swap(right[u], groups + u) for u in range(groups)]
    near_got = [both[0]] + [swap(both[u], u) for u in range(1, groups)]
    gate = jax.nn.sigmoid(jnp.dot(normed, w_gate, preferred_element_type=jnp.float32))
    half = groups // 2
    early = make_lines(far_got[:half], groups, rows, cols, 10 ** 8)
    left, near = make_near(near_got, early, rows, cols)
    late = make_lines(far_got[half:], groups, rows, cols, 10 ** 5, (left,))
    keep, send = make_cross(left, near, early, late, rows, cols)
    sums = make_sums(keep, lax.ppermute(send, "col", [(0, 1), (1, 0)]))
    returned = [sums[0]] + [swap(sums[u], u) for u in range(1, groups)]
    update = make_update(returned, out_gain.reshape(hidden, 1), w_out, gate, rows, cols)
    return update.reshape(rows, cols, channels)


def solution(mesh):
    return jax.shard_map(
        shards,
        mesh=mesh,
        in_specs=(P(("grp", "row"), "col", None), P("grp"), P("grp"), P(), P(), P(), P(), P(), P()),
        out_specs=P(("grp", "row"), "col", None),
        check_vma=False,
    )
```

```python
import functools

import jax
import jax.numpy as jnp
from jax import lax
from jax.experimental import pallas as pl
from jax.experimental.pallas import tpu as pltpu
from jax.sharding import PartitionSpec as P

EPS = 1e-05
LANES = 128
VMEM_LIMIT = 32 * 1024 * 1024
VMEM_FIRST = 60 * 1024 * 1024


def ceil_to(n, m):
    return -(-n // m) * m


def line_step(ch):
    return (ceil_to(ch, 8) // 8 | 1) * 8


def place_of(groups, rows, cols):
    row, col = lax.axis_index("row"), lax.axis_index("col")
    return row * rows, col * cols, lax.rem(row, groups), row // groups, col


def sigmoid(x):
    return 0.5 + 0.5 * jnp.tanh(0.5 * x)


def mask_of(cols, first_row, first_col, lens_ref, res_ref, at, block):
    position = at + lax.broadcasted_iota(jnp.int32, (8, block), 1)
    i_here = jnp.floor((position.astype(jnp.float32) + 0.5) * (1.0 / cols)).astype(jnp.int32)
    i_at = first_row + i_here
    k_at = first_col + position - i_here * cols
    i_ok = jnp.zeros((8, block), jnp.float32)
    k_ok = jnp.zeros((8, block), jnp.float32)
    start = 0
    for q in range(lens_ref.shape[0]):
        length = lens_ref[q]
        stop = start + jnp.minimum(length, res_ref[q])
        i_ok = jnp.where((i_at >= start) & (i_at < stop), 1.0, i_ok)
        k_ok = jnp.where((k_at >= start) & (k_at < stop), 1.0, k_ok)
        start = start + length
    return i_ok * k_ok


def edge_of(normed, w_ref, mask, groups):
    hidden = w_ref.shape[1] // 2
    block = normed.shape[0]
    projected = lax.dot_general(w_ref[...], normed, (((0,), (1,)), ((), ())), preferred_element_type=jnp.float32)
    edge = sigmoid(projected[:hidden]) * projected[hidden:]
    edge = edge.reshape(hidden // 8, 8, block) * mask[None]
    return edge.reshape(groups, hidden // groups, block).astype(jnp.bfloat16)


def edges_kernel(groups, rows, cols, chunks, pair_ref, gain_ref, wl_ref, wr_ref, lens_ref, res_ref, normed_ref, *refs):
    both_ref, right_refs = refs[0], refs[1:1 + groups]
    x_s, gain_s, wl_s, wr_s, lens_s, res_s, normed_s, held, in_sems, out_sems = refs[1 + groups:]
    count = rows * cols
    first_row, first_col, mine, _, _ = place_of(groups, rows, cols)
    own = wl_ref.shape[1] // 2 // groups
    loads = [
        pltpu.make_async_copy(src, dst, in_sems.at[n])
        for n, (src, dst) in enumerate(
            [(gain_ref, gain_s), (lens_ref, lens_s), (res_ref, res_s), (wr_ref, wr_s), (wl_ref, wl_s)]
        )
    ]
    pieces = [
        pltpu.make_async_copy(pair_ref.at[pl.ds(at, size)], x_s.at[pl.ds(at, size)], in_sems.at[len(loads) + n])
        for n, (at, size) in enumerate(chunks)
    ]
    for copy in pieces[:1] + loads + pieces[1:]:
        copy.start()
    block = chunks[0][1]
    channels = x_s.shape[1]
    average = jnp.full((2 * channels, channels), 1.0 / channels, jnp.bfloat16)
    spare = x_s.shape[0] - count
    if spare:
        x_s[pl.ds(count, spare)] = jnp.zeros((spare, x_s.shape[1]), x_s.dtype)
    stores = []
    for n, (at, size) in enumerate(chunks):
        pieces[n].wait()
        x = x_s[pl.ds(at, block)]
        centred = x.astype(jnp.float32) - jnp.dot(x, average[:channels], preferred_element_type=jnp.float32)
        square = centred * centred
        high = square.astype(jnp.bfloat16)
        low = (square - high.astype(jnp.float32)).astype(jnp.bfloat16)
        variance = jnp.dot(jnp.concatenate([high, low], axis=1), average, preferred_element_type=jnp.float32)
        if n == 0:
            for copy in loads:
                copy.wait()
        normed = (centred * lax.rsqrt(variance + EPS) * gain_s[...]).astype(jnp.bfloat16)
        normed_s[pl.ds(at, block)] = normed
        mask = mask_of(cols, first_row, first_col, lens_s, res_s, at, block)
        lanes = pl.ds(at, block)
        held[:, own:, lanes] = edge_of(normed, wr_s, mask, groups)
        held[:, :own, lanes] = edge_of(normed, wl_s, mask, groups)
        sent = [
            (held.at[jnp.bitwise_xor(mine, u), pl.ds(own, own), lanes], right_refs[u].at[:, lanes])
            for u in range(groups)
        ]
        sent.append((held.at[:, :, lanes], both_ref.at[:, :, lanes]))
        sent.append((normed_s.at[pl.ds(at, size)], normed_ref.at[pl.ds(at, size)]))
        for m, (src, dst) in enumerate(sent):
            stores.append(pltpu.make_async_copy(src, dst, out_sems.at[n, m]))
            stores[-1].start()
    for copy in stores:
        copy.wait()


def make_edges(pair, lens, resolved, gain, w_left, w_right, groups, rows, cols):
    count, channels = pair.shape
    own = w_left.shape[1] // 2 // groups
    block = 512
    flat = ceil_to(count, block)
    chunks = [(at, min(block, count - at)) for at in range(0, count, block)]
    here = pl.BlockSpec(memory_space=pltpu.HBM)
    return pl.pallas_call(
        functools.partial(edges_kernel, groups, rows, cols, chunks),
        in_specs=[here] * 6,
        out_specs=[here] * (2 + groups),
        out_shape=[jax.ShapeDtypeStruct((count, channels), jnp.bfloat16)]
        + [jax.ShapeDtypeStruct((groups, 2 * own, flat), jnp.bfloat16)]
        + [jax.ShapeDtypeStruct((own, flat), jnp.bfloat16)] * groups,
        scratch_shapes=[
            pltpu.VMEM((flat, channels), pair.dtype),
            pltpu.VMEM(gain.shape, gain.dtype),
            pltpu.VMEM(w_left.shape, w_left.dtype),
            pltpu.VMEM(w_right.shape, w_right.dtype),
            pltpu.SMEM(lens.shape, lens.dtype),
            pltpu.SMEM(resolved.shape, resolved.dtype),
            pltpu.VMEM((flat, channels), jnp.bfloat16),
            pltpu.VMEM((groups, 2 * own, flat), jnp.bfloat16),
            pltpu.SemaphoreType.DMA((5 + len(chunks),)),
            pltpu.SemaphoreType.DMA((len(chunks), 2 + groups)),
        ],
        compiler_params=pltpu.CompilerParams(vmem_limit_bytes=VMEM_FIRST),
    )(pair, gain, w_left, w_right, lens, resolved)


def unpack(got_ref, held_refs, block, rows, cols, step):
    tiles = pl.cdiv(cols, LANES)
    ch = got_ref.shape[0] // len(held_refs)
    lane = lax.broadcasted_iota(jnp.int32, (ch, LANES), 1)
    for n, held in enumerate(held_refs):
        seen = {}

        def tile_of(t):
            if t not in seen:
                seen[t] = got_ref[n * ch:(n + 1) * ch, pl.ds(t * LANES, LANES)].astype(jnp.float32)
            return seen[t]

        for i in range(rows):
            for tt in range(tiles):
                length = min(LANES, cols - LANES * tt)
                t0, off = divmod(cols * i + LANES * tt, LANES)
                piece = tile_of(t0)
                if off:
                    piece = pltpu.roll(piece, LANES - off, 1)
                if off + length > LANES:
                    piece = jnp.where(lane < LANES - off, piece, pltpu.roll(tile_of(t0 + 1), LANES - off, 1))
                if length < LANES and n == 0:
                    piece = jnp.where(lane < length, piece, 0.0)
                base = pl.multiple_of((block * rows + i) * step, 8)
                held[tt, pl.ds(base, ch), :] = piece


def pack(held, out_ref, u, block, rows, cols, step):
    tiles = pl.cdiv(cols, LANES)
    ch = out_ref.shape[1]
    lane = lax.broadcasted_iota(jnp.int32, (ch, LANES), 1)
    for t in range(out_ref.shape[2] // LANES):
        tile = None
        for i in range(rows):
            for tt in range(tiles):
                shift = cols * i + LANES * tt - LANES * t
                length = min(LANES, cols - LANES * tt)
                if shift >= LANES or shift + length <= 0:
                    continue
                base = pl.multiple_of((block * rows + i) * step, 8)
                piece = held[tt, pl.ds(base, ch), :]
                if shift % LANES:
                    piece = pltpu.roll(piece, shift % LANES, 1)
                tile = piece if tile is None else jnp.where(lane < shift, tile, piece)
        if tile is None:
            tile = jnp.zeros((ch, LANES), jnp.float32)
        out_ref[u, :, pl.ds(t * LANES, LANES)] = tile.astype(jnp.bfloat16)


def channel_of(held, d, count, step):
    lines = [held[t, pl.ds(d, count, stride=step), :] for t in range(held.shape[0])]
    return jnp.concatenate(lines, axis=1).astype(jnp.bfloat16)


def near_kernel(groups, rows, cols, after_ref, got_ref, left_ref, near_ref, left_s, right_s, prod_s):
    mine = place_of(groups, rows, cols)[2]
    step = left_s.shape[1] // (groups * rows)
    for u in range(groups):
        unpack(got_ref.at[u], (left_s, right_s), u, rows, cols, step)
    for d in range(near_ref.shape[1]):
        left_ref[d] = channel_of(left_s, d, groups * rows, step)
        multiply(left_ref[d], channel_of(right_s, d, groups * rows, step), prod_s, d, step)
    for u in range(groups):
        pack(prod_s, near_ref, u, jnp.bitwise_xor(mine, u), rows, cols, step)


def lines_kernel(groups, rows, cols, count, *refs):
    got_refs, lines_ref = refs[:count], refs[-1]
    mine = place_of(groups, rows, cols)[2]
    step = lines_ref.shape[1] // (count * rows)
    for u in range(count):
        block = jnp.bitwise_and(jnp.bitwise_xor(mine, u), count - 1)
        unpack(got_refs[u], (lines_ref,), block, rows, cols, step)


def multiply(left, right, prod_s, d, step):
    count = left.shape[0]
    pad = prod_s.shape[0] * LANES - count
    if pad:
        right = jnp.concatenate([right, jnp.zeros((pad, right.shape[1]), right.dtype)], axis=0)
    prod = lax.dot_general(left, right, (((1,), (1,)), ((), ())), preferred_element_type=jnp.float32)
    for t in range(prod_s.shape[0]):
        prod_s[t, pl.ds(d, count, stride=step), :] = prod[:, t * LANES:(t + 1) * LANES]


def cross_kernel(groups, rows, cols, left_ref, near_ref, early_ref, late_ref, keep_ref, send_ref, right_s, prod_s, pair_s):
    _, _, mine, half, col = place_of(groups, rows, cols)
    step = prod_s.shape[1] // (groups * rows)
    size = early_ref.shape[1]
    base = pl.multiple_of(mine // (groups // 2) * size, 8)
    right_s[:, pl.ds(base, size), :] = early_ref[...]
    right_s[:, pl.ds(pl.multiple_of(size - base, 8), size), :] = late_ref[...]
    for d in range(keep_ref.shape[1]):
        multiply(left_ref[d], channel_of(right_s, d, groups * rows, step), prod_s, d, step)
    for u in range(groups):
        pack(prod_s, pair_s, u, jnp.bitwise_xor(mine, u), rows, cols, step)
    near_kept = col == half
    keep_ref[...] = jnp.where(near_kept, near_ref[...], pair_s[...])
    send_ref[...] = jnp.where(near_kept, pair_s[...], near_ref[...])


def make_near(got, after, rows, cols):
    groups, both, flat = got.shape
    ch = both // 2
    count = groups * rows
    tiles = pl.cdiv(cols, LANES)
    held = pltpu.VMEM((tiles, count * line_step(ch), LANES), jnp.float32)
    whole = pl.BlockSpec(memory_space=pltpu.VMEM)
    return pl.pallas_call(
        functools.partial(near_kernel, groups, rows, cols),
        in_specs=[pl.BlockSpec(memory_space=pl.ANY), whole],
        out_specs=[whole] * 2,
        out_shape=[
            jax.ShapeDtypeStruct((ch, count, tiles * LANES), jnp.bfloat16),
            jax.ShapeDtypeStruct((groups, ch, flat), jnp.bfloat16),
        ],
        scratch_shapes=[held, held, held],
        compiler_params=pltpu.CompilerParams(vmem_limit_bytes=VMEM_LIMIT),
        cost_estimate=pl.CostEstimate(flops=10 ** 5, bytes_accessed=10 ** 5, transcendentals=0),
    )(after, got)


def make_lines(got, groups, rows, cols, cost, after=()):
    ch = got[0].shape[0]
    whole = pl.BlockSpec(memory_space=pltpu.VMEM)
    lines = (pl.cdiv(cols, LANES), len(got) * rows * line_step(ch), LANES)
    return pl.pallas_call(
        functools.partial(lines_kernel, groups, rows, cols, len(got)),
        in_specs=[whole] * len(got) + [pl.BlockSpec(memory_space=pl.ANY)] * len(after),
        out_specs=whole,
        out_shape=jax.ShapeDtypeStruct(lines, jnp.float32),
        compiler_params=pltpu.CompilerParams(vmem_limit_bytes=VMEM_LIMIT),
        cost_estimate=pl.CostEstimate(flops=10 ** 5, bytes_accessed=cost, transcendentals=0),
    )(*got, *after)


def make_cross(left, near, early, late, rows, cols):
    groups, ch, flat = near.shape
    whole = pl.BlockSpec(memory_space=pltpu.VMEM)
    held = pltpu.VMEM((pl.cdiv(cols, LANES), groups * rows * line_step(ch), LANES), jnp.float32)
    return pl.pallas_call(
        functools.partial(cross_kernel, groups, rows, cols),
        in_specs=[whole] * 4,
        out_specs=[whole] * 2,
        out_shape=[jax.ShapeDtypeStruct(near.shape, near.dtype)] * 2,
        scratch_shapes=[held, held, pltpu.VMEM(near.shape, near.dtype)],
        compiler_params=pltpu.CompilerParams(vmem_limit_bytes=VMEM_LIMIT),
        cost_estimate=pl.CostEstimate(flops=10 ** 5, bytes_accessed=8 * 10 ** 6, transcendentals=0),
    )(left, near, early, late)


def add_kernel(a_ref, b_ref, *out_refs):
    for u, out_ref in enumerate(out_refs):
        out_ref[...] = (a_ref[u].astype(jnp.float32) + b_ref[u].astype(jnp.float32)).astype(out_ref.dtype)


def make_sums(a, b):
    groups, ch, flat = a.shape
    whole = pl.BlockSpec(memory_space=pltpu.VMEM)
    return pl.pallas_call(
        add_kernel,
        in_specs=[whole] * 2,
        out_specs=[whole] * groups,
        out_shape=[jax.ShapeDtypeStruct((ch, flat), a.dtype)] * groups,
        compiler_params=pltpu.CompilerParams(vmem_limit_bytes=VMEM_LIMIT),
        cost_estimate=pl.CostEstimate(flops=10 ** 5, bytes_accessed=10 ** 5, transcendentals=0),
    )(a, b)


def update_kernel(groups, rows, cols, chunks, gain_ref, w_ref, gate_ref, *refs):
    prod_refs = refs[:groups]
    out_ref, held, out_s, sems = refs[groups:]
    mine = place_of(groups, rows, cols)[2]
    ch = held.shape[1]
    block = held.shape[2]
    stores = []
    for n, (at, size) in enumerate(chunks):
        lanes = pl.ds(at, block)
        for u in range(groups):
            held[jnp.bitwise_xor(mine, u)] = prod_refs[u][:, lanes].astype(jnp.float32)
        prod = held[...].reshape(groups * ch, block)
        mean = jnp.mean(prod, axis=0, keepdims=True)
        centred = prod - mean
        variance = jnp.mean(centred * centred, axis=0, keepdims=True)
        normed = (centred * lax.rsqrt(variance + EPS) * gain_ref[...]).astype(jnp.bfloat16)
        projected = lax.dot_general(normed, w_ref[...], (((0,), (0,)), ((), ())), preferred_element_type=jnp.float32)
        out_s[pl.ds(at, size)] = (gate_ref[pl.ds(at, size)] * projected[:size]).astype(out_s.dtype)
        stores.append(pltpu.make_async_copy(out_s.at[pl.ds(at, size)], out_ref.at[pl.ds(at, size)], sems.at[n]))
        stores[-1].start()
    for copy in stores:
        copy.wait()


def make_update(prods, gain, w_out, gate, rows, cols):
    groups = len(prods)
    ch = prods[0].shape[0]
    count, channels = gate.shape
    block = 512
    chunks = [(at, min(block, count - at)) for at in range(0, count, block)]
    whole = pl.BlockSpec(memory_space=pltpu.VMEM)
    return pl.pallas_call(
        functools.partial(update_kernel, groups, rows, cols, chunks),
        in_specs=[whole] * (3 + groups),
        out_specs=pl.BlockSpec(memory_space=pltpu.HBM),
        out_shape=jax.ShapeDtypeStruct((count, channels), jnp.bfloat16),
        scratch_shapes=[
            pltpu.VMEM((groups, ch, block), jnp.float32),
            pltpu.VMEM((count, channels), jnp.bfloat16),
            pltpu.SemaphoreType.DMA((len(chunks),)),
        ],
        compiler_params=pltpu.CompilerParams(vmem_limit_bytes=VMEM_LIMIT),
    )(gain, w_out, gate, *prods)


def swap(value, shift):
    return lax.ppermute(value, "row", [(r, r ^ shift) for r in range(lax.axis_size("row"))])


def shards(pair_act, chain_lengths, resolved, in_gain, out_gain, w_left, w_right, w_gate, w_out):
    rows, cols, channels = pair_act.shape
    hidden = w_out.shape[0]
    groups = lax.axis_size("row") // 2
    normed, *edges = make_edges(
        pair_act.reshape(rows * cols, channels), chain_lengths, resolved,
        in_gain.reshape(1, channels), w_left, w_right, groups, rows, cols,
    )
    both, right = edges[0], edges[1:]
    halves = [[h * groups + r for r in range(groups)] for h in range(2)]
    far_got = [swap(right[u], groups + u) for u in range(groups)]
    near_got = lax.all_to_all(both, "row", split_axis=0, concat_axis=0, tiled=True, axis_index_groups=halves)
    gate = jax.nn.sigmoid(jnp.dot(normed, w_gate, preferred_element_type=jnp.float32))
    half = groups // 2
    early = make_lines(far_got[:half], groups, rows, cols, 10 ** 8)
    left, near = make_near(near_got, early, rows, cols)
    late = make_lines(far_got[half:], groups, rows, cols, 10 ** 5, (left,))
    keep, send = make_cross(left, near, early, late, rows, cols)
    sums = make_sums(keep, lax.ppermute(send, "col", [(0, 1), (1, 0)]))
    returned = [sums[0]] + [swap(sums[u], u) for u in range(1, groups)]
    update = make_update(returned, out_gain.reshape(hidden, 1), w_out, gate, rows, cols)
    return update.reshape(rows, cols, channels)


def solution(mesh):
    return jax.shard_map(
        shards,
        mesh=mesh,
        in_specs=(P(("grp", "row"), "col", None), P("grp"), P("grp"), P(), P(), P(), P(), P(), P()),
        out_specs=P(("grp", "row"), "col", None),
        check_vma=False,
    )
```

```python
import functools

import jax
import jax.numpy as jnp
from jax import lax
from jax.experimental import pallas as pl
from jax.experimental.pallas import tpu as pltpu
from jax.sharding import PartitionSpec as P

EPS = 1e-05
LANES = 128
VMEM_LIMIT = 32 * 1024 * 1024
VMEM_FIRST = 60 * 1024 * 1024


def ceil_to(n, m):
    return -(-n // m) * m


def line_step(ch):
    return (ceil_to(ch, 8) // 8 | 1) * 8


def place_of(groups, rows, cols):
    row, col = lax.axis_index("row"), lax.axis_index("col")
    return row * rows, col * cols, lax.rem(row, groups), row // groups, col


def sigmoid(x):
    return 0.5 + 0.5 * jnp.tanh(0.5 * x)


def mask_of(cols, first_row, first_col, lens_ref, res_ref, at, block):
    position = at + lax.broadcasted_iota(jnp.int32, (8, block), 1)
    i_here = jnp.floor((position.astype(jnp.float32) + 0.5) * (1.0 / cols)).astype(jnp.int32)
    i_at = first_row + i_here
    k_at = first_col + position - i_here * cols
    i_ok = jnp.zeros((8, block), jnp.float32)
    k_ok = jnp.zeros((8, block), jnp.float32)
    start = 0
    for q in range(lens_ref.shape[0]):
        length = lens_ref[q]
        stop = start + jnp.minimum(length, res_ref[q])
        i_ok = jnp.where((i_at >= start) & (i_at < stop), 1.0, i_ok)
        k_ok = jnp.where((k_at >= start) & (k_at < stop), 1.0, k_ok)
        start = start + length
    return i_ok * k_ok


def edge_of(weights, normed, mask, groups):
    hidden = weights.shape[0] // 2
    block = normed.shape[1]
    projected = jnp.dot(weights, normed, preferred_element_type=jnp.float32)
    edge = sigmoid(projected[:hidden]) * projected[hidden:]
    edge = edge.reshape(hidden // 8, 8, block) * mask[None]
    return edge.reshape(groups, hidden // groups, block).astype(jnp.bfloat16)


def edges_kernel(groups, rows, cols, chunks, pair_ref, gain_ref, wl_ref, wr_ref, lens_ref, res_ref, normed_ref, *refs):
    both_refs, right_refs = refs[:groups], refs[groups:2 * groups]
    x_s, gain_s, wl_s, wr_s, lens_s, res_s, normed_s, held, in_sems, out_sems = refs[2 * groups:]
    count = rows * cols
    first_row, first_col, mine, _, _ = place_of(groups, rows, cols)
    own = wl_ref.shape[1] // 2 // groups
    loads = [
        pltpu.make_async_copy(src, dst, in_sems.at[n])
        for n, (src, dst) in enumerate(
            [(gain_ref, gain_s), (lens_ref, lens_s), (res_ref, res_s), (wr_ref, wr_s), (wl_ref, wl_s)]
        )
    ]
    pieces = [
        pltpu.make_async_copy(pair_ref.at[pl.ds(at, size)], x_s.at[pl.ds(at, size)], in_sems.at[len(loads) + n])
        for n, (at, size) in enumerate(chunks)
    ]
    for copy in pieces[:1] + loads + pieces[1:]:
        copy.start()
    block = chunks[0][1]
    channels = x_s.shape[1]
    spare = x_s.shape[0] - count
    if spare:
        x_s[pl.ds(count, spare)] = jnp.zeros((spare, x_s.shape[1]), x_s.dtype)
    stores = []
    for n, (at, size) in enumerate(chunks):
        pieces[n].wait()
        x = x_s[pl.ds(at, block)].T.astype(jnp.float32)
        centred = x - jnp.mean(x, axis=0, keepdims=True)
        variance = jnp.mean(centred * centred, axis=0, keepdims=True)
        if n == 0:
            for copy in loads:
                copy.wait()
            gain = jnp.broadcast_to(gain_s[...], (LANES, channels)).T
            gain = jnp.concatenate([gain] * (block // LANES), axis=1)
            right_w, left_w = wr_s[...].T, wl_s[...].T
        normed = (centred * lax.rsqrt(variance + EPS) * gain).astype(jnp.bfloat16)
        mask = mask_of(cols, first_row, first_col, lens_s, res_s, at, block)
        lanes = pl.ds(at, block)
        normed_s[:, lanes] = normed
        held[:, own:, lanes] = edge_of(right_w, normed, mask, groups)
        held[:, :own, lanes] = edge_of(left_w, normed, mask, groups)
        sent = []
        for u in range(groups):
            group = jnp.bitwise_xor(mine, u)
            sent.append((held.at[group, pl.ds(own, own), lanes], right_refs[u].at[:, lanes]))
            sent.append((held.at[group, :, lanes], both_refs[u].at[:, lanes]))
        sent.append((normed_s.at[:, lanes], normed_ref.at[:, lanes]))
        for m, (src, dst) in enumerate(sent):
            stores.append(pltpu.make_async_copy(src, dst, out_sems.at[n, m]))
            stores[-1].start()
    for copy in stores:
        copy.wait()


def make_edges(pair, lens, resolved, gain, w_left, w_right, groups, rows, cols):
    count, channels = pair.shape
    own = w_left.shape[1] // 2 // groups
    block = 512
    flat = ceil_to(count, block)
    chunks = [(at, min(block, count - at)) for at in range(0, count, block)]
    here = pl.BlockSpec(memory_space=pltpu.HBM)
    return pl.pallas_call(
        functools.partial(edges_kernel, groups, rows, cols, chunks),
        in_specs=[here] * 6,
        out_specs=[here] * (1 + 2 * groups),
        out_shape=[jax.ShapeDtypeStruct((channels, flat), jnp.bfloat16)]
        + [jax.ShapeDtypeStruct((2 * own, flat), jnp.bfloat16)] * groups
        + [jax.ShapeDtypeStruct((own, flat), jnp.bfloat16)] * groups,
        scratch_shapes=[
            pltpu.VMEM((flat, channels), pair.dtype),
            pltpu.VMEM(gain.shape, gain.dtype),
            pltpu.VMEM(w_left.shape, w_left.dtype),
            pltpu.VMEM(w_right.shape, w_right.dtype),
            pltpu.SMEM(lens.shape, lens.dtype),
            pltpu.SMEM(resolved.shape, resolved.dtype),
            pltpu.VMEM((channels, flat), jnp.bfloat16),
            pltpu.VMEM((groups, 2 * own, flat), jnp.bfloat16),
            pltpu.SemaphoreType.DMA((5 + len(chunks),)),
            pltpu.SemaphoreType.DMA((len(chunks), 1 + 2 * groups)),
        ],
        compiler_params=pltpu.CompilerParams(vmem_limit_bytes=VMEM_FIRST),
    )(pair, gain, w_left, w_right, lens, resolved)


def unpack(got_ref, held_refs, block, rows, cols, step):
    tiles = pl.cdiv(cols, LANES)
    ch = got_ref.shape[0] // len(held_refs)
    lane = lax.broadcasted_iota(jnp.int32, (ch, LANES), 1)
    for n, held in enumerate(held_refs):
        seen = {}

        def tile_of(t):
            if t not in seen:
                seen[t] = got_ref[n * ch:(n + 1) * ch, pl.ds(t * LANES, LANES)].astype(jnp.float32)
            return seen[t]

        for i in range(rows):
            for tt in range(tiles):
                length = min(LANES, cols - LANES * tt)
                t0, off = divmod(cols * i + LANES * tt, LANES)
                piece = tile_of(t0)
                if off:
                    piece = pltpu.roll(piece, LANES - off, 1)
                if off + length > LANES:
                    piece = jnp.where(lane < LANES - off, piece, pltpu.roll(tile_of(t0 + 1), LANES - off, 1))
                if length < LANES and n == 0:
                    piece = jnp.where(lane < length, piece, 0.0)
                base = pl.multiple_of((block * rows + i) * step, 8)
                held[tt, pl.ds(base, ch), :] = piece


def pack(held, out_ref, u, block, rows, cols, step):
    tiles = pl.cdiv(cols, LANES)
    ch = out_ref.shape[1]
    lane = lax.broadcasted_iota(jnp.int32, (ch, LANES), 1)
    for t in range(out_ref.shape[2] // LANES):
        tile = None
        for i in range(rows):
            for tt in range(tiles):
                shift = cols * i + LANES * tt - LANES * t
                length = min(LANES, cols - LANES * tt)
                if shift >= LANES or shift + length <= 0:
                    continue
                base = pl.multiple_of((block * rows + i) * step, 8)
                piece = held[tt, pl.ds(base, ch), :]
                if shift % LANES:
                    piece = pltpu.roll(piece, shift % LANES, 1)
                tile = piece if tile is None else jnp.where(lane < shift, tile, piece)
        if tile is None:
            tile = jnp.zeros((ch, LANES), jnp.float32)
        out_ref[u, :, pl.ds(t * LANES, LANES)] = tile.astype(jnp.bfloat16)


def channel_of(held, d, count, step):
    lines = [held[t, pl.ds(d, count, stride=step), :] for t in range(held.shape[0])]
    return jnp.concatenate(lines, axis=1).astype(jnp.bfloat16)


def early_kernel(groups, rows, cols, far_ref, near_ref, far_lines, left_lines, right_lines):
    step = far_lines.shape[1] // rows
    unpack(far_ref, (far_lines,), 0, rows, cols, step)
    unpack(near_ref, (left_lines, right_lines), 0, rows, cols, step)


def near_kernel(groups, rows, cols, left_lines, right_lines, *refs):
    got_refs = refs[:groups - 1]
    left_ref, near_ref, left_s, right_s, prod_s = refs[groups - 1:]
    mine = place_of(groups, rows, cols)[2]
    step = left_s.shape[1] // (groups * rows)
    size = rows * step
    there = pl.ds(pl.multiple_of(jnp.bitwise_xor(mine, 1) * size, 8), size)
    left_s[:, there, :] = left_lines[...]
    right_s[:, there, :] = right_lines[...]
    for got_ref, u in zip(got_refs, [0] + list(range(2, groups))):
        unpack(got_ref, (left_s, right_s), jnp.bitwise_xor(mine, u), rows, cols, step)
    for d in range(near_ref.shape[1]):
        left_ref[d] = channel_of(left_s, d, groups * rows, step)
        multiply(left_ref[d], channel_of(right_s, d, groups * rows, step), prod_s, d, step)
    for u in range(groups):
        pack(prod_s, near_ref, u, jnp.bitwise_xor(mine, u), rows, cols, step)


def late_kernel(groups, rows, cols, after_ref, far_lines, *refs):
    got_refs, lines_ref = refs[:-1], refs[-1]
    mine = place_of(groups, rows, cols)[2]
    step = lines_ref.shape[1] // (groups * rows)
    size = rows * step
    lines_ref[:, pl.ds(pl.multiple_of(mine * size, 8), size), :] = far_lines[...]
    for u in range(1, groups):
        unpack(got_refs[u - 1], (lines_ref,), jnp.bitwise_xor(mine, u), rows, cols, step)


def multiply(left, right, prod_s, d, step):
    count = left.shape[0]
    pad = prod_s.shape[0] * LANES - count
    if pad:
        right = jnp.concatenate([right, jnp.zeros((pad, right.shape[1]), right.dtype)], axis=0)
    prod = lax.dot_general(left, right, (((1,), (1,)), ((), ())), preferred_element_type=jnp.float32)
    for t in range(prod_s.shape[0]):
        prod_s[t, pl.ds(d, count, stride=step), :] = prod[:, t * LANES:(t + 1) * LANES]


def cross_kernel(groups, rows, cols, left_ref, near_ref, lines_ref, *refs):
    keep_refs, send_refs = refs[:2], refs[2:4]
    prod_s, pair_s = refs[4:]
    _, _, mine, half, col = place_of(groups, rows, cols)
    step = prod_s.shape[1] // (groups * rows)
    for d in range(left_ref.shape[0]):
        multiply(left_ref[d], channel_of(lines_ref, d, groups * rows, step), prod_s, d, step)
    for u in range(groups):
        pack(prod_s, pair_s, u, jnp.bitwise_xor(mine, u), rows, cols, step)
    near_kept = col == half
    for part in range(2):
        pieces = pl.ds(part * (groups // 2), groups // 2)
        keep_refs[part][...] = jnp.where(near_kept, near_ref[pieces], pair_s[pieces])
        send_refs[part][...] = jnp.where(near_kept, pair_s[pieces], near_ref[pieces])


def lines_of(blocks, ch, cols):
    return (pl.cdiv(cols, LANES), blocks * line_step(ch), LANES)


def make_early(far, near, groups, rows, cols):
    ch = far.shape[0]
    whole = pl.BlockSpec(memory_space=pltpu.VMEM)
    return pl.pallas_call(
        functools.partial(early_kernel, groups, rows, cols),
        in_specs=[whole] * 2,
        out_specs=[whole] * 3,
        out_shape=[jax.ShapeDtypeStruct(lines_of(rows, ch, cols), jnp.float32)] * 3,
        compiler_params=pltpu.CompilerParams(vmem_limit_bytes=VMEM_LIMIT),
        cost_estimate=pl.CostEstimate(flops=10 ** 5, bytes_accessed=10 ** 8, transcendentals=0),
    )(far, near)


def make_late(after, far_lines, got, groups, rows, cols):
    ch = got[0].shape[0]
    whole = pl.BlockSpec(memory_space=pltpu.VMEM)
    return pl.pallas_call(
        functools.partial(late_kernel, groups, rows, cols),
        in_specs=[pl.BlockSpec(memory_space=pl.ANY)] + [whole] * (1 + len(got)),
        out_specs=whole,
        out_shape=jax.ShapeDtypeStruct(lines_of(groups * rows, ch, cols), jnp.float32),
        compiler_params=pltpu.CompilerParams(vmem_limit_bytes=VMEM_LIMIT),
        cost_estimate=pl.CostEstimate(flops=10 ** 5, bytes_accessed=10 ** 5, transcendentals=0),
    )(after, far_lines, *got)


def make_near(left_lines, right_lines, got, rows, cols):
    groups = len(got) + 1
    both, flat = got[0].shape
    ch = both // 2
    count = groups * rows
    held = pltpu.VMEM(lines_of(count, ch, cols), jnp.float32)
    whole = pl.BlockSpec(memory_space=pltpu.VMEM)
    return pl.pallas_call(
        functools.partial(near_kernel, groups, rows, cols),
        in_specs=[whole] * (2 + len(got)),
        out_specs=[whole] * 2,
        out_shape=[
            jax.ShapeDtypeStruct((ch, count, pl.cdiv(cols, LANES) * LANES), jnp.bfloat16),
            jax.ShapeDtypeStruct((groups, ch, flat), jnp.bfloat16),
        ],
        scratch_shapes=[held, held, held],
        compiler_params=pltpu.CompilerParams(vmem_limit_bytes=VMEM_LIMIT),
        cost_estimate=pl.CostEstimate(flops=10 ** 5, bytes_accessed=10 ** 5, transcendentals=0),
    )(left_lines, right_lines, *got)


def make_cross(left, near, lines, rows, cols):
    groups, ch, flat = near.shape
    whole = pl.BlockSpec(memory_space=pltpu.VMEM)
    return pl.pallas_call(
        functools.partial(cross_kernel, groups, rows, cols),
        in_specs=[whole] * 3,
        out_specs=[whole] * 4,
        out_shape=[jax.ShapeDtypeStruct((groups // 2, ch, flat), near.dtype)] * 4,
        scratch_shapes=[
            pltpu.VMEM(lines_of(groups * rows, ch, cols), jnp.float32),
            pltpu.VMEM(near.shape, near.dtype),
        ],
        compiler_params=pltpu.CompilerParams(vmem_limit_bytes=VMEM_LIMIT),
        cost_estimate=pl.CostEstimate(flops=10 ** 5, bytes_accessed=8 * 10 ** 6, transcendentals=0),
    )(left, near, lines)


def add_kernel(a_ref, b_ref, *out_refs):
    for u, out_ref in enumerate(out_refs):
        out_ref[...] = (a_ref[u].astype(jnp.float32) + b_ref[u].astype(jnp.float32)).astype(out_ref.dtype)


def make_sums(a, b):
    groups, ch, flat = a.shape
    whole = pl.BlockSpec(memory_space=pltpu.VMEM)
    return pl.pallas_call(
        add_kernel,
        in_specs=[whole] * 2,
        out_specs=[whole] * groups,
        out_shape=[jax.ShapeDtypeStruct((ch, flat), a.dtype)] * groups,
        compiler_params=pltpu.CompilerParams(vmem_limit_bytes=VMEM_LIMIT),
        cost_estimate=pl.CostEstimate(flops=10 ** 5, bytes_accessed=10 ** 5, transcendentals=0),
    )(a, b)


def update_kernel(groups, rows, cols, chunks, gain_ref, w_ref, gate_ref, *refs):
    prod_refs = refs[:groups]
    out_ref, held, out_s, sems = refs[groups:]
    mine = place_of(groups, rows, cols)[2]
    ch = held.shape[1]
    block = held.shape[2]
    stores = []
    for n, (at, size) in enumerate(chunks):
        lanes = pl.ds(at, block)
        for u in range(groups):
            held[jnp.bitwise_xor(mine, u)] = prod_refs[u][:, lanes].astype(jnp.float32)
        prod = held[...].reshape(groups * ch, block)
        mean = jnp.mean(prod, axis=0, keepdims=True)
        centred = prod - mean
        variance = jnp.mean(centred * centred, axis=0, keepdims=True)
        normed = (centred * lax.rsqrt(variance + EPS) * gain_ref[...]).astype(jnp.bfloat16)
        projected = lax.dot_general(normed, w_ref[...], (((0,), (0,)), ((), ())), preferred_element_type=jnp.float32)
        out_s[pl.ds(at, size)] = (gate_ref[pl.ds(at, size)] * projected[:size]).astype(out_s.dtype)
        stores.append(pltpu.make_async_copy(out_s.at[pl.ds(at, size)], out_ref.at[pl.ds(at, size)], sems.at[n]))
        stores[-1].start()
    for copy in stores:
        copy.wait()


def make_update(prods, gain, w_out, gate, rows, cols):
    groups = len(prods)
    ch = prods[0].shape[0]
    count, channels = gate.shape
    block = 512
    chunks = [(at, min(block, count - at)) for at in range(0, count, block)]
    whole = pl.BlockSpec(memory_space=pltpu.VMEM)
    return pl.pallas_call(
        functools.partial(update_kernel, groups, rows, cols, chunks),
        in_specs=[whole] * (3 + groups),
        out_specs=pl.BlockSpec(memory_space=pltpu.HBM),
        out_shape=jax.ShapeDtypeStruct((count, channels), jnp.bfloat16),
        scratch_shapes=[
            pltpu.VMEM((groups, ch, block), jnp.float32),
            pltpu.VMEM((count, channels), jnp.bfloat16),
            pltpu.SemaphoreType.DMA((len(chunks),)),
        ],
        compiler_params=pltpu.CompilerParams(vmem_limit_bytes=VMEM_LIMIT),
    )(gain, w_out, gate, *prods)


def swap(value, shift):
    return lax.ppermute(value, "row", [(r, r ^ shift) for r in range(lax.axis_size("row"))])


def shards(pair_act, chain_lengths, resolved, in_gain, out_gain, w_left, w_right, w_gate, w_out):
    rows, cols, channels = pair_act.shape
    hidden = w_out.shape[0]
    groups = lax.axis_size("row") // 2
    normed, *edges = make_edges(
        pair_act.reshape(rows * cols, channels), chain_lengths, resolved,
        in_gain.reshape(1, channels), w_left, w_right, groups, rows, cols,
    )
    both, right = edges[:groups], edges[groups:]
    far_got = [swap(right[u], groups + u) for u in range(groups)]
    near_got = [both[0]] + [swap(both[u], u) for u in range(1, groups)]
    gate = jax.nn.sigmoid(
        jnp.einsum("cp,cd->pd", normed[:, :rows * cols], w_gate, preferred_element_type=jnp.float32)
    )
    far_lines, *near_lines = make_early(far_got[0], near_got[1], groups, rows, cols)
    left, near = make_near(*near_lines, near_got[:1] + near_got[2:], rows, cols)
    lines = make_late(left, far_lines, far_got[1:], groups, rows, cols)
    parts = make_cross(left, near, lines, rows, cols)
    sums = [[], []]
    for part in (1, 0):
        other = lax.ppermute(parts[2 + part], "col", [(0, 1), (1, 0)])
        sums[part] = make_sums(parts[part], other)
    sums = sums[0] + sums[1]
    returned = [sums[0]] + [swap(sums[u], u) for u in range(1, groups)]
    update = make_update(returned, out_gain.reshape(hidden, 1), w_out, gate, rows, cols)
    return update.reshape(rows, cols, channels)


def solution(mesh):
    return jax.shard_map(
        shards,
        mesh=mesh,
        in_specs=(P(("grp", "row"), "col", None), P("grp"), P("grp"), P(), P(), P(), P(), P(), P()),
        out_specs=P(("grp", "row"), "col", None),
        check_vma=False,
    )
```

```python
import functools

import jax
import jax.numpy as jnp
from jax import lax
from jax.experimental import pallas as pl
from jax.experimental.pallas import tpu as pltpu
from jax.sharding import PartitionSpec as P

EPS = 1e-05
LANES = 128
VMEM_LIMIT = 32 * 1024 * 1024
VMEM_FIRST = 60 * 1024 * 1024


def ceil_to(n, m):
    return -(-n // m) * m


def line_step(ch):
    return (ceil_to(ch, 8) // 8 | 1) * 8


def place_of(groups, rows, cols):
    row, col = lax.axis_index("row"), lax.axis_index("col")
    return row * rows, col * cols, lax.rem(row, groups), row // groups, col


def sigmoid(x):
    return 0.5 + 0.5 * jnp.tanh(0.5 * x)


def mask_of(cols, first_row, first_col, lens_ref, res_ref, at, block):
    position = at + lax.broadcasted_iota(jnp.int32, (8, block), 1)
    i_here = jnp.floor((position.astype(jnp.float32) + 0.5) * (1.0 / cols)).astype(jnp.int32)
    i_at = first_row + i_here
    k_at = first_col + position - i_here * cols
    i_ok = jnp.zeros((8, block), jnp.float32)
    k_ok = jnp.zeros((8, block), jnp.float32)
    start = 0
    for q in range(lens_ref.shape[0]):
        length = lens_ref[q]
        stop = start + jnp.minimum(length, res_ref[q])
        i_ok = jnp.where((i_at >= start) & (i_at < stop), 1.0, i_ok)
        k_ok = jnp.where((k_at >= start) & (k_at < stop), 1.0, k_ok)
        start = start + length
    return i_ok * k_ok


def edge_of(weights, normed, mask, groups):
    hidden = weights.shape[0] // 2
    block = normed.shape[1]
    projected = jnp.dot(weights, normed, preferred_element_type=jnp.float32)
    edge = sigmoid(projected[:hidden]) * projected[hidden:]
    edge = edge.reshape(hidden // 8, 8, block) * mask[None]
    return edge.reshape(groups, hidden // groups, block).astype(jnp.bfloat16)


def edges_kernel(groups, rows, cols, chunks, pair_ref, gain_ref, wl_ref, wr_ref, lens_ref, res_ref, normed_ref, *refs):
    both_ref, right_refs = refs[0], refs[1:1 + groups]
    x_s, gain_s, wl_s, wr_s, lens_s, res_s, normed_s, held, in_sems, out_sems = refs[1 + groups:]
    count = rows * cols
    first_row, first_col, mine, _, _ = place_of(groups, rows, cols)
    own = wl_ref.shape[1] // 2 // groups
    loads = [
        pltpu.make_async_copy(src, dst, in_sems.at[n])
        for n, (src, dst) in enumerate(
            [(gain_ref, gain_s), (lens_ref, lens_s), (res_ref, res_s), (wr_ref, wr_s), (wl_ref, wl_s)]
        )
    ]
    pieces = [
        pltpu.make_async_copy(pair_ref.at[pl.ds(at, size)], x_s.at[pl.ds(at, size)], in_sems.at[len(loads) + n])
        for n, (at, size) in enumerate(chunks)
    ]
    for copy in pieces[:1] + loads + pieces[1:]:
        copy.start()
    block = chunks[0][1]
    channels = x_s.shape[1]
    spare = x_s.shape[0] - count
    if spare:
        x_s[pl.ds(count, spare)] = jnp.zeros((spare, x_s.shape[1]), x_s.dtype)
    stores = []
    for n, (at, size) in enumerate(chunks):
        pieces[n].wait()
        x = x_s[pl.ds(at, block)].T.astype(jnp.float32)
        centred = x - jnp.mean(x, axis=0, keepdims=True)
        variance = jnp.mean(centred * centred, axis=0, keepdims=True)
        if n == 0:
            for copy in loads:
                copy.wait()
            gain = jnp.broadcast_to(gain_s[...], (LANES, channels)).T
            gain = jnp.concatenate([gain] * (block // LANES), axis=1)
            right_w, left_w = wr_s[...].T, wl_s[...].T
        normed = (centred * lax.rsqrt(variance + EPS) * gain).astype(jnp.bfloat16)
        mask = mask_of(cols, first_row, first_col, lens_s, res_s, at, block)
        lanes = pl.ds(at, block)
        normed_s[:, lanes] = normed
        held[:, own:, lanes] = edge_of(right_w, normed, mask, groups)
        held[:, :own, lanes] = edge_of(left_w, normed, mask, groups)
        sent = [
            (held.at[jnp.bitwise_xor(mine, u), pl.ds(own, own), lanes], right_refs[u].at[:, lanes])
            for u in range(groups)
        ]
        sent.append((held.at[:, :, lanes], both_ref.at[:, :, lanes]))
        sent.append((normed_s.at[:, lanes], normed_ref.at[:, lanes]))
        for m, (src, dst) in enumerate(sent):
            stores.append(pltpu.make_async_copy(src, dst, out_sems.at[n, m]))
            stores[-1].start()
    for copy in stores:
        copy.wait()


def make_edges(pair, lens, resolved, gain, w_left, w_right, groups, rows, cols):
    count, channels = pair.shape
    own = w_left.shape[1] // 2 // groups
    block = 512
    flat = ceil_to(count, block)
    chunks = [(at, min(block, count - at)) for at in range(0, count, block)]
    here = pl.BlockSpec(memory_space=pltpu.HBM)
    return pl.pallas_call(
        functools.partial(edges_kernel, groups, rows, cols, chunks),
        in_specs=[here] * 6,
        out_specs=[here] * (2 + groups),
        out_shape=[jax.ShapeDtypeStruct((channels, flat), jnp.bfloat16)]
        + [jax.ShapeDtypeStruct((groups, 2 * own, flat), jnp.bfloat16)]
        + [jax.ShapeDtypeStruct((own, flat), jnp.bfloat16)] * groups,
        scratch_shapes=[
            pltpu.VMEM((flat, channels), pair.dtype),
            pltpu.VMEM(gain.shape, gain.dtype),
            pltpu.VMEM(w_left.shape, w_left.dtype),
            pltpu.VMEM(w_right.shape, w_right.dtype),
            pltpu.SMEM(lens.shape, lens.dtype),
            pltpu.SMEM(resolved.shape, resolved.dtype),
            pltpu.VMEM((channels, flat), jnp.bfloat16),
            pltpu.VMEM((groups, 2 * own, flat), jnp.bfloat16),
            pltpu.SemaphoreType.DMA((5 + len(chunks),)),
            pltpu.SemaphoreType.DMA((len(chunks), 2 + groups)),
        ],
        compiler_params=pltpu.CompilerParams(vmem_limit_bytes=VMEM_FIRST),
    )(pair, gain, w_left, w_right, lens, resolved)


def unpack(got_ref, held_refs, block, rows, cols, step):
    tiles = pl.cdiv(cols, LANES)
    ch = got_ref.shape[0] // len(held_refs)
    lane = lax.broadcasted_iota(jnp.int32, (ch, LANES), 1)
    for n, held in enumerate(held_refs):
        seen = {}

        def tile_of(t):
            if t not in seen:
                seen[t] = got_ref[n * ch:(n + 1) * ch, pl.ds(t * LANES, LANES)].astype(jnp.float32)
            return seen[t]

        for i in range(rows):
            for tt in range(tiles):
                length = min(LANES, cols - LANES * tt)
                t0, off = divmod(cols * i + LANES * tt, LANES)
                piece = tile_of(t0)
                if off:
                    piece = pltpu.roll(piece, LANES - off, 1)
                if off + length > LANES:
                    piece = jnp.where(lane < LANES - off, piece, pltpu.roll(tile_of(t0 + 1), LANES - off, 1))
                if length < LANES and n == 0:
                    piece = jnp.where(lane < length, piece, 0.0)
                base = pl.multiple_of((block * rows + i) * step, 8)
                held[tt, pl.ds(base, ch), :] = piece


def pack(held, out_ref, u, block, rows, cols, step):
    tiles = pl.cdiv(cols, LANES)
    ch = out_ref.shape[1]
    lane = lax.broadcasted_iota(jnp.int32, (ch, LANES), 1)
    for t in range(out_ref.shape[2] // LANES):
        tile = None
        for i in range(rows):
            for tt in range(tiles):
                shift = cols * i + LANES * tt - LANES * t
                length = min(LANES, cols - LANES * tt)
                if shift >= LANES or shift + length <= 0:
                    continue
                base = pl.multiple_of((block * rows + i) * step, 8)
                piece = held[tt, pl.ds(base, ch), :]
                if shift % LANES:
                    piece = pltpu.roll(piece, shift % LANES, 1)
                tile = piece if tile is None else jnp.where(lane < shift, tile, piece)
        if tile is None:
            tile = jnp.zeros((ch, LANES), jnp.float32)
        out_ref[u, :, pl.ds(t * LANES, LANES)] = tile.astype(jnp.bfloat16)


def channel_of(held, d, count, step):
    lines = [held[t, pl.ds(d, count, stride=step), :] for t in range(held.shape[0])]
    return jnp.concatenate(lines, axis=1).astype(jnp.bfloat16)


def near_kernel(groups, rows, cols, after_ref, got_ref, left_ref, near_ref, left_s, right_s, prod_s):
    mine = place_of(groups, rows, cols)[2]
    step = left_s.shape[1] // (groups * rows)
    for u in range(groups):
        unpack(got_ref.at[u], (left_s, right_s), u, rows, cols, step)
    for d in range(near_ref.shape[1]):
        left_ref[d] = channel_of(left_s, d, groups * rows, step)
        multiply(left_ref[d], channel_of(right_s, d, groups * rows, step), prod_s, d, step)
    for u in range(groups):
        pack(prod_s, near_ref, u, jnp.bitwise_xor(mine, u), rows, cols, step)


def lines_kernel(groups, rows, cols, count, *refs):
    got_refs, lines_ref = refs[:count], refs[-1]
    mine = place_of(groups, rows, cols)[2]
    step = lines_ref.shape[1] // (count * rows)
    for u in range(count):
        block = jnp.bitwise_and(jnp.bitwise_xor(mine, u), count - 1)
        unpack(got_refs[u], (lines_ref,), block, rows, cols, step)


def multiply(left, right, prod_s, d, step):
    count = left.shape[0]
    pad = prod_s.shape[0] * LANES - count
    if pad:
        right = jnp.concatenate([right, jnp.zeros((pad, right.shape[1]), right.dtype)], axis=0)
    prod = lax.dot_general(left, right, (((1,), (1,)), ((), ())), preferred_element_type=jnp.float32)
    for t in range(prod_s.shape[0]):
        prod_s[t, pl.ds(d, count, stride=step), :] = prod[:, t * LANES:(t + 1) * LANES]


def cross_kernel(groups, rows, cols, left_ref, near_ref, early_ref, late_ref, *refs):
    keep_refs, send_refs = refs[:2], refs[2:4]
    right_s, prod_s, pair_s = refs[4:]
    _, _, mine, half, col = place_of(groups, rows, cols)
    step = prod_s.shape[1] // (groups * rows)
    size = early_ref.shape[1]
    base = pl.multiple_of(mine // (groups // 2) * size, 8)
    right_s[:, pl.ds(base, size), :] = early_ref[...]
    right_s[:, pl.ds(pl.multiple_of(size - base, 8), size), :] = late_ref[...]
    for d in range(left_ref.shape[0]):
        multiply(left_ref[d], channel_of(right_s, d, groups * rows, step), prod_s, d, step)
    for u in range(groups):
        pack(prod_s, pair_s, u, jnp.bitwise_xor(mine, u), rows, cols, step)
    near_kept = col == half
    for part in range(2):
        pieces = pl.ds(part * (groups // 2), groups // 2)
        keep_refs[part][...] = jnp.where(near_kept, near_ref[pieces], pair_s[pieces])
        send_refs[part][...] = jnp.where(near_kept, pair_s[pieces], near_ref[pieces])


def make_near(got, after, rows, cols):
    groups, both, flat = got.shape
    ch = both // 2
    count = groups * rows
    tiles = pl.cdiv(cols, LANES)
    held = pltpu.VMEM((tiles, count * line_step(ch), LANES), jnp.float32)
    whole = pl.BlockSpec(memory_space=pltpu.VMEM)
    return pl.pallas_call(
        functools.partial(near_kernel, groups, rows, cols),
        in_specs=[pl.BlockSpec(memory_space=pl.ANY), whole],
        out_specs=[whole] * 2,
        out_shape=[
            jax.ShapeDtypeStruct((ch, count, tiles * LANES), jnp.bfloat16),
            jax.ShapeDtypeStruct((groups, ch, flat), jnp.bfloat16),
        ],
        scratch_shapes=[held, held, held],
        compiler_params=pltpu.CompilerParams(vmem_limit_bytes=VMEM_LIMIT),
        cost_estimate=pl.CostEstimate(flops=10 ** 5, bytes_accessed=10 ** 5, transcendentals=0),
    )(after, got)


def make_lines(got, groups, rows, cols, cost, after=()):
    ch = got[0].shape[0]
    whole = pl.BlockSpec(memory_space=pltpu.VMEM)
    lines = (pl.cdiv(cols, LANES), len(got) * rows * line_step(ch), LANES)
    return pl.pallas_call(
        functools.partial(lines_kernel, groups, rows, cols, len(got)),
        in_specs=[whole] * len(got) + [pl.BlockSpec(memory_space=pl.ANY)] * len(after),
        out_specs=whole,
        out_shape=jax.ShapeDtypeStruct(lines, jnp.float32),
        compiler_params=pltpu.CompilerParams(vmem_limit_bytes=VMEM_LIMIT),
        cost_estimate=pl.CostEstimate(flops=10 ** 5, bytes_accessed=cost, transcendentals=0),
    )(*got, *after)


def make_cross(left, near, early, late, rows, cols):
    groups, ch, flat = near.shape
    whole = pl.BlockSpec(memory_space=pltpu.VMEM)
    held = pltpu.VMEM((pl.cdiv(cols, LANES), groups * rows * line_step(ch), LANES), jnp.float32)
    return pl.pallas_call(
        functools.partial(cross_kernel, groups, rows, cols),
        in_specs=[whole] * 4,
        out_specs=[whole] * 4,
        out_shape=[jax.ShapeDtypeStruct((groups // 2, ch, flat), near.dtype)] * 4,
        scratch_shapes=[held, held, pltpu.VMEM(near.shape, near.dtype)],
        compiler_params=pltpu.CompilerParams(vmem_limit_bytes=VMEM_LIMIT),
        cost_estimate=pl.CostEstimate(flops=10 ** 5, bytes_accessed=8 * 10 ** 6, transcendentals=0),
    )(left, near, early, late)


def add_kernel(a_ref, b_ref, *out_refs):
    for u, out_ref in enumerate(out_refs):
        out_ref[...] = (a_ref[u].astype(jnp.float32) + b_ref[u].astype(jnp.float32)).astype(out_ref.dtype)


def make_sums(a, b):
    groups, ch, flat = a.shape
    whole = pl.BlockSpec(memory_space=pltpu.VMEM)
    return pl.pallas_call(
        add_kernel,
        in_specs=[whole] * 2,
        out_specs=[whole] * groups,
        out_shape=[jax.ShapeDtypeStruct((ch, flat), a.dtype)] * groups,
        compiler_params=pltpu.CompilerParams(vmem_limit_bytes=VMEM_LIMIT),
        cost_estimate=pl.CostEstimate(flops=10 ** 5, bytes_accessed=10 ** 5, transcendentals=0),
    )(a, b)


def update_kernel(groups, rows, cols, chunks, gain_ref, w_ref, gate_ref, *refs):
    prod_refs = refs[:groups]
    out_ref, held, out_s, sems = refs[groups:]
    mine = place_of(groups, rows, cols)[2]
    ch = held.shape[1]
    block = held.shape[2]
    stores = []
    for n, (at, size) in enumerate(chunks):
        lanes = pl.ds(at, block)
        for u in range(groups):
            held[jnp.bitwise_xor(mine, u)] = prod_refs[u][:, lanes].astype(jnp.float32)
        prod = held[...].reshape(groups * ch, block)
        mean = jnp.mean(prod, axis=0, keepdims=True)
        centred = prod - mean
        variance = jnp.mean(centred * centred, axis=0, keepdims=True)
        normed = (centred * lax.rsqrt(variance + EPS) * gain_ref[...]).astype(jnp.bfloat16)
        projected = lax.dot_general(normed, w_ref[...], (((0,), (0,)), ((), ())), preferred_element_type=jnp.float32)
        out_s[pl.ds(at, size)] = (gate_ref[pl.ds(at, size)] * projected[:size]).astype(out_s.dtype)
        stores.append(pltpu.make_async_copy(out_s.at[pl.ds(at, size)], out_ref.at[pl.ds(at, size)], sems.at[n]))
        stores[-1].start()
    for copy in stores:
        copy.wait()


def make_update(prods, gain, w_out, gate, rows, cols):
    groups = len(prods)
    ch = prods[0].shape[0]
    count, channels = gate.shape
    block = 512
    chunks = [(at, min(block, count - at)) for at in range(0, count, block)]
    whole = pl.BlockSpec(memory_space=pltpu.VMEM)
    return pl.pallas_call(
        functools.partial(update_kernel, groups, rows, cols, chunks),
        in_specs=[whole] * (3 + groups),
        out_specs=pl.BlockSpec(memory_space=pltpu.HBM),
        out_shape=jax.ShapeDtypeStruct((count, channels), jnp.bfloat16),
        scratch_shapes=[
            pltpu.VMEM((groups, ch, block), jnp.float32),
            pltpu.VMEM((count, channels), jnp.bfloat16),
            pltpu.SemaphoreType.DMA((len(chunks),)),
        ],
        compiler_params=pltpu.CompilerParams(vmem_limit_bytes=VMEM_LIMIT),
    )(gain, w_out, gate, *prods)


def swap(value, shift):
    return lax.ppermute(value, "row", [(r, r ^ shift) for r in range(lax.axis_size("row"))])


def shards(pair_act, chain_lengths, resolved, in_gain, out_gain, w_left, w_right, w_gate, w_out):
    rows, cols, channels = pair_act.shape
    hidden = w_out.shape[0]
    groups = lax.axis_size("row") // 2
    normed, *edges = make_edges(
        pair_act.reshape(rows * cols, channels), chain_lengths, resolved,
        in_gain.reshape(1, channels), w_left, w_right, groups, rows, cols,
    )
    both, right = edges[0], edges[1:]
    halves = [[h * groups + r for r in range(groups)] for h in range(2)]
    far_got = [swap(right[u], groups + u) for u in range(groups)]
    near_got = lax.all_to_all(both, "row", split_axis=0, concat_axis=0, tiled=True, axis_index_groups=halves)
    gate = jax.nn.sigmoid(
        jnp.einsum("cp,cd->pd", normed[:, :rows * cols], w_gate, preferred_element_type=jnp.float32)
    )
    half = groups // 2
    early = make_lines(far_got[:half], groups, rows, cols, 10 ** 8)
    left, near = make_near(near_got, early, rows, cols)
    late = make_lines(far_got[half:], groups, rows, cols, 10 ** 5, (left,))
    parts = make_cross(left, near, early, late, rows, cols)
    sums = [[], []]
    for part in (1, 0):
        other = lax.ppermute(parts[2 + part], "col", [(0, 1), (1, 0)])
        sums[part] = make_sums(parts[part], other)
    sums = sums[0] + sums[1]
    returned = [sums[0]] + [swap(sums[u], u) for u in range(1, groups)]
    update = make_update(returned, out_gain.reshape(hidden, 1), w_out, gate, rows, cols)
    return update.reshape(rows, cols, channels)


def solution(mesh):
    return jax.shard_map(
        shards,
        mesh=mesh,
        in_specs=(P(("grp", "row"), "col", None), P("grp"), P("grp"), P(), P(), P(), P(), P(), P()),
        out_specs=P(("grp", "row"), "col", None),
        check_vma=False,
    )
```

```python
import functools

import jax
import jax.numpy as jnp
from jax import lax
from jax.experimental import pallas as pl
from jax.experimental.pallas import tpu as pltpu
from jax.sharding import PartitionSpec as P

EPS = 1e-05
LANES = 128
VMEM_LIMIT = 32 * 1024 * 1024
VMEM_FIRST = 60 * 1024 * 1024


def ceil_to(n, m):
    return -(-n // m) * m


def line_step(ch):
    return (ceil_to(ch, 8) // 8 | 1) * 8


def place_of(groups, rows, cols):
    row, col = lax.axis_index("row"), lax.axis_index("col")
    return row * rows, col * cols, lax.rem(row, groups), row // groups, col


def sigmoid(x):
    return 0.5 + 0.5 * jnp.tanh(0.5 * x)


def mask_of(cols, first_row, first_col, lens_ref, res_ref, at, block):
    position = at + lax.broadcasted_iota(jnp.int32, (8, block), 1)
    i_here = jnp.floor((position.astype(jnp.float32) + 0.5) * (1.0 / cols)).astype(jnp.int32)
    i_at = first_row + i_here
    k_at = first_col + position - i_here * cols
    i_ok = jnp.zeros((8, block), jnp.float32)
    k_ok = jnp.zeros((8, block), jnp.float32)
    start = 0
    for q in range(lens_ref.shape[0]):
        length = lens_ref[q]
        stop = start + jnp.minimum(length, res_ref[q])
        i_ok = jnp.where((i_at >= start) & (i_at < stop), 1.0, i_ok)
        k_ok = jnp.where((k_at >= start) & (k_at < stop), 1.0, k_ok)
        start = start + length
    return i_ok * k_ok


def edge_of(weights, normed, mask, groups):
    hidden = weights.shape[0] // 2
    block = normed.shape[1]
    projected = jnp.dot(weights, normed, preferred_element_type=jnp.float32)
    edge = sigmoid(projected[:hidden]) * projected[hidden:]
    edge = edge.reshape(hidden // 8, 8, block) * mask[None]
    return edge.reshape(groups, hidden // groups, block).astype(jnp.bfloat16)


def edges_kernel(groups, rows, cols, chunks, pair_ref, gain_ref, wl_ref, wr_ref, lens_ref, res_ref, normed_ref, *refs):
    both_refs, right_refs = refs[:groups], refs[groups:2 * groups]
    x_s, gain_s, wl_s, wr_s, lens_s, res_s, normed_s, held, in_sems, out_sems = refs[2 * groups:]
    count = rows * cols
    first_row, first_col, mine, _, _ = place_of(groups, rows, cols)
    own = wl_ref.shape[1] // 2 // groups
    loads = [
        pltpu.make_async_copy(src, dst, in_sems.at[n])
        for n, (src, dst) in enumerate(
            [(gain_ref, gain_s), (lens_ref, lens_s), (res_ref, res_s), (wr_ref, wr_s), (wl_ref, wl_s)]
        )
    ]
    pieces = [
        pltpu.make_async_copy(pair_ref.at[pl.ds(at, size)], x_s.at[pl.ds(at, size)], in_sems.at[len(loads) + n])
        for n, (at, size) in enumerate(chunks)
    ]
    for copy in pieces[:1] + loads + pieces[1:]:
        copy.start()
    block = chunks[0][1]
    channels = x_s.shape[1]
    spare = x_s.shape[0] - count
    if spare:
        x_s[pl.ds(count, spare)] = jnp.zeros((spare, x_s.shape[1]), x_s.dtype)
    stores = []
    for n, (at, size) in enumerate(chunks):
        pieces[n].wait()
        x = x_s[pl.ds(at, block)].T.astype(jnp.float32)
        centred = x - jnp.mean(x, axis=0, keepdims=True)
        variance = jnp.mean(centred * centred, axis=0, keepdims=True)
        if n == 0:
            for copy in loads:
                copy.wait()
            gain = jnp.broadcast_to(gain_s[...], (LANES, channels)).T
            gain = jnp.concatenate([gain] * (block // LANES), axis=1)
            right_w, left_w = wr_s[...].T, wl_s[...].T
        normed = (centred * lax.rsqrt(variance + EPS) * gain).astype(jnp.bfloat16)
        mask = mask_of(cols, first_row, first_col, lens_s, res_s, at, block)
        lanes = pl.ds(at, block)
        normed_s[:, lanes] = normed
        held[:, own:, lanes] = edge_of(right_w, normed, mask, groups)
        held[:, :own, lanes] = edge_of(left_w, normed, mask, groups)
        sent = []
        for u in range(groups):
            group = jnp.bitwise_xor(mine, u)
            sent.append((held.at[group, pl.ds(own, own), lanes], right_refs[u].at[:, lanes]))
            sent.append((held.at[group, :, lanes], both_refs[u].at[:, lanes]))
        sent.append((normed_s.at[:, lanes], normed_ref.at[:, lanes]))
        for m, (src, dst) in enumerate(sent):
            stores.append(pltpu.make_async_copy(src, dst, out_sems.at[n, m]))
            stores[-1].start()
    for copy in stores:
        copy.wait()


def make_edges(pair, lens, resolved, gain, w_left, w_right, groups, rows, cols):
    count, channels = pair.shape
    own = w_left.shape[1] // 2 // groups
    block = 512
    flat = ceil_to(count, block)
    chunks = [(at, min(block, count - at)) for at in range(0, count, block)]
    here = pl.BlockSpec(memory_space=pltpu.HBM)
    return pl.pallas_call(
        functools.partial(edges_kernel, groups, rows, cols, chunks),
        in_specs=[here] * 6,
        out_specs=[here] * (1 + 2 * groups),
        out_shape=[jax.ShapeDtypeStruct((channels, flat), jnp.bfloat16)]
        + [jax.ShapeDtypeStruct((2 * own, flat), jnp.bfloat16)] * groups
        + [jax.ShapeDtypeStruct((own, flat), jnp.bfloat16)] * groups,
        scratch_shapes=[
            pltpu.VMEM((flat, channels), pair.dtype),
            pltpu.VMEM(gain.shape, gain.dtype),
            pltpu.VMEM(w_left.shape, w_left.dtype),
            pltpu.VMEM(w_right.shape, w_right.dtype),
            pltpu.SMEM(lens.shape, lens.dtype),
            pltpu.SMEM(resolved.shape, resolved.dtype),
            pltpu.VMEM((channels, flat), jnp.bfloat16),
            pltpu.VMEM((groups, 2 * own, flat), jnp.bfloat16),
            pltpu.SemaphoreType.DMA((5 + len(chunks),)),
            pltpu.SemaphoreType.DMA((len(chunks), 1 + 2 * groups)),
        ],
        compiler_params=pltpu.CompilerParams(vmem_limit_bytes=VMEM_FIRST),
    )(pair, gain, w_left, w_right, lens, resolved)


def unpack(got_ref, held_refs, block, rows, cols, step):
    tiles = pl.cdiv(cols, LANES)
    ch = got_ref.shape[0] // len(held_refs)
    lane = lax.broadcasted_iota(jnp.int32, (ch, LANES), 1)
    for n, held in enumerate(held_refs):
        seen = {}

        def tile_of(t):
            if t not in seen:
                seen[t] = got_ref[n * ch:(n + 1) * ch, pl.ds(t * LANES, LANES)].astype(jnp.float32)
            return seen[t]

        for i in range(rows):
            for tt in range(tiles):
                length = min(LANES, cols - LANES * tt)
                t0, off = divmod(cols * i + LANES * tt, LANES)
                piece = tile_of(t0)
                if off:
                    piece = pltpu.roll(piece, LANES - off, 1)
                if off + length > LANES:
                    piece = jnp.where(lane < LANES - off, piece, pltpu.roll(tile_of(t0 + 1), LANES - off, 1))
                if length < LANES and n == 0:
                    piece = jnp.where(lane < length, piece, 0.0)
                base = pl.multiple_of((block * rows + i) * step, 8)
                held[tt, pl.ds(base, ch), :] = piece


def pack(held, out_ref, u, block, rows, cols, step):
    tiles = pl.cdiv(cols, LANES)
    ch = out_ref.shape[1]
    lane = lax.broadcasted_iota(jnp.int32, (ch, LANES), 1)
    for t in range(out_ref.shape[2] // LANES):
        tile = None
        for i in range(rows):
            for tt in range(tiles):
                shift = cols * i + LANES * tt - LANES * t
                length = min(LANES, cols - LANES * tt)
                if shift >= LANES or shift + length <= 0:
                    continue
                base = pl.multiple_of((block * rows + i) * step, 8)
                piece = held[tt, pl.ds(base, ch), :]
                if shift % LANES:
                    piece = pltpu.roll(piece, shift % LANES, 1)
                tile = piece if tile is None else jnp.where(lane < shift, tile, piece)
        if tile is None:
            tile = jnp.zeros((ch, LANES), jnp.float32)
        out_ref[u, :, pl.ds(t * LANES, LANES)] = tile.astype(jnp.bfloat16)


def channel_of(held, d, count, step):
    lines = [held[t, pl.ds(d, count, stride=step), :] for t in range(held.shape[0])]
    return jnp.concatenate(lines, axis=1).astype(jnp.bfloat16)


def near_kernel(groups, rows, cols, after_ref, *refs):
    got_refs = refs[:groups]
    left_ref, near_ref, left_s, right_s, prod_s = refs[groups:]
    mine = place_of(groups, rows, cols)[2]
    step = left_s.shape[1] // (groups * rows)
    for u in range(groups):
        unpack(got_refs[u], (left_s, right_s), jnp.bitwise_xor(mine, u), rows, cols, step)
    for d in range(near_ref.shape[1]):
        left_ref[d] = channel_of(left_s, d, groups * rows, step)
        multiply(left_ref[d], channel_of(right_s, d, groups * rows, step), prod_s, d, step)
    for u in range(groups):
        pack(prod_s, near_ref, u, jnp.bitwise_xor(mine, u), rows, cols, step)


def lines_kernel(groups, rows, cols, count, *refs):
    got_refs, lines_ref = refs[:count], refs[-1]
    mine = place_of(groups, rows, cols)[2]
    step = lines_ref.shape[1] // (count * rows)
    for u in range(count):
        block = jnp.bitwise_and(jnp.bitwise_xor(mine, u), count - 1)
        unpack(got_refs[u], (lines_ref,), block, rows, cols, step)


def multiply(left, right, prod_s, d, step):
    count = left.shape[0]
    pad = prod_s.shape[0] * LANES - count
    if pad:
        right = jnp.concatenate([right, jnp.zeros((pad, right.shape[1]), right.dtype)], axis=0)
    prod = lax.dot_general(left, right, (((1,), (1,)), ((), ())), preferred_element_type=jnp.float32)
    for t in range(prod_s.shape[0]):
        prod_s[t, pl.ds(d, count, stride=step), :] = prod[:, t * LANES:(t + 1) * LANES]


def cross_kernel(groups, rows, cols, left_ref, near_ref, early_ref, late_ref, *refs):
    keep_refs, send_refs = refs[:2], refs[2:4]
    right_s, prod_s, pair_s = refs[4:]
    _, _, mine, half, col = place_of(groups, rows, cols)
    step = prod_s.shape[1] // (groups * rows)
    size = early_ref.shape[1]
    base = pl.multiple_of(mine // (groups // 2) * size, 8)
    right_s[:, pl.ds(base, size), :] = early_ref[...]
    right_s[:, pl.ds(pl.multiple_of(size - base, 8), size), :] = late_ref[...]
    for d in range(left_ref.shape[0]):
        multiply(left_ref[d], channel_of(right_s, d, groups * rows, step), prod_s, d, step)
    for u in range(groups):
        pack(prod_s, pair_s, u, jnp.bitwise_xor(mine, u), rows, cols, step)
    near_kept = col == half
    for part in range(2):
        pieces = pl.ds(part * (groups // 2), groups // 2)
        keep_refs[part][...] = jnp.where(near_kept, near_ref[pieces], pair_s[pieces])
        send_refs[part][...] = jnp.where(near_kept, pair_s[pieces], near_ref[pieces])


def make_near(got, after, rows, cols):
    groups = len(got)
    both, flat = got[0].shape
    ch = both // 2
    count = groups * rows
    tiles = pl.cdiv(cols, LANES)
    held = pltpu.VMEM((tiles, count * line_step(ch), LANES), jnp.float32)
    whole = pl.BlockSpec(memory_space=pltpu.VMEM)
    return pl.pallas_call(
        functools.partial(near_kernel, groups, rows, cols),
        in_specs=[pl.BlockSpec(memory_space=pl.ANY)] + [whole] * groups,
        out_specs=[whole] * 2,
        out_shape=[
            jax.ShapeDtypeStruct((ch, count, tiles * LANES), jnp.bfloat16),
            jax.ShapeDtypeStruct((groups, ch, flat), jnp.bfloat16),
        ],
        scratch_shapes=[held, held, held],
        compiler_params=pltpu.CompilerParams(vmem_limit_bytes=VMEM_LIMIT),
        cost_estimate=pl.CostEstimate(flops=10 ** 5, bytes_accessed=10 ** 5, transcendentals=0),
    )(after, *got)


def make_lines(got, groups, rows, cols, cost, after=()):
    ch = got[0].shape[0]
    whole = pl.BlockSpec(memory_space=pltpu.VMEM)
    lines = (pl.cdiv(cols, LANES), len(got) * rows * line_step(ch), LANES)
    return pl.pallas_call(
        functools.partial(lines_kernel, groups, rows, cols, len(got)),
        in_specs=[whole] * len(got) + [pl.BlockSpec(memory_space=pl.ANY)] * len(after),
        out_specs=whole,
        out_shape=jax.ShapeDtypeStruct(lines, jnp.float32),
        compiler_params=pltpu.CompilerParams(vmem_limit_bytes=VMEM_LIMIT),
        cost_estimate=pl.CostEstimate(flops=10 ** 5, bytes_accessed=cost, transcendentals=0),
    )(*got, *after)


def make_cross(left, near, early, late, rows, cols):
    groups, ch, flat = near.shape
    whole = pl.BlockSpec(memory_space=pltpu.VMEM)
    held = pltpu.VMEM((pl.cdiv(cols, LANES), groups * rows * line_step(ch), LANES), jnp.float32)
    return pl.pallas_call(
        functools.partial(cross_kernel, groups, rows, cols),
        in_specs=[whole] * 4,
        out_specs=[whole] * 4,
        out_shape=[jax.ShapeDtypeStruct((groups // 2, ch, flat), near.dtype)] * 4,
        scratch_shapes=[held, held, pltpu.VMEM(near.shape, near.dtype)],
        compiler_params=pltpu.CompilerParams(vmem_limit_bytes=VMEM_LIMIT),
        cost_estimate=pl.CostEstimate(flops=10 ** 5, bytes_accessed=8 * 10 ** 6, transcendentals=0),
    )(left, near, early, late)


def add_kernel(a_ref, b_ref, *out_refs):
    for u, out_ref in enumerate(out_refs):
        out_ref[...] = (a_ref[u].astype(jnp.float32) + b_ref[u].astype(jnp.float32)).astype(out_ref.dtype)


def make_sums(a, b):
    groups, ch, flat = a.shape
    whole = pl.BlockSpec(memory_space=pltpu.VMEM)
    return pl.pallas_call(
        add_kernel,
        in_specs=[whole] * 2,
        out_specs=[whole] * groups,
        out_shape=[jax.ShapeDtypeStruct((ch, flat), a.dtype)] * groups,
        compiler_params=pltpu.CompilerParams(vmem_limit_bytes=VMEM_LIMIT),
        cost_estimate=pl.CostEstimate(flops=10 ** 5, bytes_accessed=10 ** 5, transcendentals=0),
    )(a, b)


def update_kernel(groups, rows, cols, chunks, gain_ref, w_ref, gate_ref, *refs):
    prod_refs = refs[:groups]
    out_ref, held, out_s, sems = refs[groups:]
    mine = place_of(groups, rows, cols)[2]
    ch = held.shape[1]
    block = held.shape[2]
    stores = []
    for n, (at, size) in enumerate(chunks):
        lanes = pl.ds(at, block)
        for u in range(groups):
            held[jnp.bitwise_xor(mine, u)] = prod_refs[u][:, lanes].astype(jnp.float32)
        prod = held[...].reshape(groups * ch, block)
        mean = jnp.mean(prod, axis=0, keepdims=True)
        centred = prod - mean
        variance = jnp.mean(centred * centred, axis=0, keepdims=True)
        normed = (centred * lax.rsqrt(variance + EPS) * gain_ref[...]).astype(jnp.bfloat16)
        projected = lax.dot_general(normed, w_ref[...], (((0,), (0,)), ((), ())), preferred_element_type=jnp.float32)
        out_s[pl.ds(at, size)] = (gate_ref[pl.ds(at, size)] * projected[:size]).astype(out_s.dtype)
        stores.append(pltpu.make_async_copy(out_s.at[pl.ds(at, size)], out_ref.at[pl.ds(at, size)], sems.at[n]))
        stores[-1].start()
    for copy in stores:
        copy.wait()


def make_update(prods, gain, w_out, gate, rows, cols):
    groups = len(prods)
    ch = prods[0].shape[0]
    count, channels = gate.shape
    block = 512
    chunks = [(at, min(block, count - at)) for at in range(0, count, block)]
    whole = pl.BlockSpec(memory_space=pltpu.VMEM)
    return pl.pallas_call(
        functools.partial(update_kernel, groups, rows, cols, chunks),
        in_specs=[whole] * (3 + groups),
        out_specs=pl.BlockSpec(memory_space=pltpu.HBM),
        out_shape=jax.ShapeDtypeStruct((count, channels), jnp.bfloat16),
        scratch_shapes=[
            pltpu.VMEM((groups, ch, block), jnp.float32),
            pltpu.VMEM((count, channels), jnp.bfloat16),
            pltpu.SemaphoreType.DMA((len(chunks),)),
        ],
        compiler_params=pltpu.CompilerParams(vmem_limit_bytes=VMEM_LIMIT),
    )(gain, w_out, gate, *prods)


def swap(value, shift):
    return lax.ppermute(value, "row", [(r, r ^ shift) for r in range(lax.axis_size("row"))])


def shards(pair_act, chain_lengths, resolved, in_gain, out_gain, w_left, w_right, w_gate, w_out):
    rows, cols, channels = pair_act.shape
    hidden = w_out.shape[0]
    groups = lax.axis_size("row") // 2
    normed, *edges = make_edges(
        pair_act.reshape(rows * cols, channels), chain_lengths, resolved,
        in_gain.reshape(1, channels), w_left, w_right, groups, rows, cols,
    )
    both, right = edges[:groups], edges[groups:]
    far_got = [swap(right[u], groups + u) for u in range(groups)]
    near_got = [both[0]] + [swap(both[u], u) for u in range(1, groups)]
    gate = jax.nn.sigmoid(
        jnp.einsum("cp,cd->pd", normed[:, :rows * cols], w_gate, preferred_element_type=jnp.float32)
    )
    half = groups // 2
    early = make_lines(far_got[:half], groups, rows, cols, 10 ** 8)
    left, near = make_near(near_got, early, rows, cols)
    late = make_lines(far_got[half:], groups, rows, cols, 10 ** 5)
    parts = make_cross(left, near, early, late, rows, cols)
    sums = [[], []]
    for part in (1, 0):
        other = lax.ppermute(parts[2 + part], "col", [(0, 1), (1, 0)])
        sums[part] = make_sums(parts[part], other)
    sums = sums[0] + sums[1]
    returned = [sums[0]] + [swap(sums[u], u) for u in range(1, groups)]
    update = make_update(returned, out_gain.reshape(hidden, 1), w_out, gate, rows, cols)
    return update.reshape(rows, cols, channels)


def solution(mesh):
    return jax.shard_map(
        shards,
        mesh=mesh,
        in_specs=(P(("grp", "row"), "col", None), P("grp"), P("grp"), P(), P(), P(), P(), P(), P()),
        out_specs=P(("grp", "row"), "col", None),
        check_vma=False,
    )
```

```python
import functools

import jax
import jax.numpy as jnp
from jax import lax
from jax.experimental import pallas as pl
from jax.experimental.pallas import tpu as pltpu
from jax.sharding import PartitionSpec as P

EPS = 1e-05
LANES = 128
VMEM_LIMIT = 32 * 1024 * 1024
VMEM_FIRST = 60 * 1024 * 1024


def ceil_to(n, m):
    return -(-n // m) * m


def line_step(ch):
    return (ceil_to(ch, 8) // 8 | 1) * 8


def place_of(groups, rows, cols):
    row, col = lax.axis_index("row"), lax.axis_index("col")
    return row * rows, col * cols, lax.rem(row, groups), row // groups, col


def sigmoid(x):
    return 0.5 + 0.5 * jnp.tanh(0.5 * x)


def mask_of(cols, first_row, first_col, lens_ref, res_ref, at, block):
    position = at + lax.broadcasted_iota(jnp.int32, (8, block), 1)
    i_here = jnp.floor((position.astype(jnp.float32) + 0.5) * (1.0 / cols)).astype(jnp.int32)
    i_at = first_row + i_here
    k_at = first_col + position - i_here * cols
    i_ok = jnp.zeros((8, block), jnp.float32)
    k_ok = jnp.zeros((8, block), jnp.float32)
    start = 0
    for q in range(lens_ref.shape[0]):
        length = lens_ref[q]
        stop = start + jnp.minimum(length, res_ref[q])
        i_ok = jnp.where((i_at >= start) & (i_at < stop), 1.0, i_ok)
        k_ok = jnp.where((k_at >= start) & (k_at < stop), 1.0, k_ok)
        start = start + length
    return i_ok * k_ok


def edge_of(weights, normed, mask, groups):
    hidden = weights.shape[0] // 2
    block = normed.shape[1]
    projected = jnp.dot(weights, normed, preferred_element_type=jnp.float32)
    edge = sigmoid(projected[:hidden]) * projected[hidden:]
    edge = edge.reshape(hidden // 8, 8, block) * mask[None]
    return edge.reshape(groups, hidden // groups, block).astype(jnp.bfloat16)


def edges_kernel(groups, rows, cols, chunks, pair_ref, gain_ref, wl_ref, wr_ref, lens_ref, res_ref, normed_ref, *refs):
    both_refs, right_refs = refs[:groups], refs[groups:2 * groups]
    x_s, gain_s, wl_s, wr_s, lens_s, res_s, normed_s, held, in_sems, out_sems = refs[2 * groups:]
    count = rows * cols
    first_row, first_col, mine, _, _ = place_of(groups, rows, cols)
    own = wl_ref.shape[1] // 2 // groups
    loads = [
        pltpu.make_async_copy(src, dst, in_sems.at[n])
        for n, (src, dst) in enumerate(
            [(gain_ref, gain_s), (lens_ref, lens_s), (res_ref, res_s), (wr_ref, wr_s), (wl_ref, wl_s)]
        )
    ]
    pieces = [
        pltpu.make_async_copy(pair_ref.at[pl.ds(at, size)], x_s.at[pl.ds(at, size)], in_sems.at[len(loads) + n])
        for n, (at, size) in enumerate(chunks)
    ]
    for copy in pieces[:1] + loads + pieces[1:]:
        copy.start()
    block = chunks[0][1]
    channels = x_s.shape[1]
    spare = x_s.shape[0] - count
    if spare:
        x_s[pl.ds(count, spare)] = jnp.zeros((spare, x_s.shape[1]), x_s.dtype)
    stores = []
    for n, (at, size) in enumerate(chunks):
        pieces[n].wait()
        x = x_s[pl.ds(at, block)].T.astype(jnp.float32)
        centred = x - jnp.mean(x, axis=0, keepdims=True)
        variance = jnp.mean(centred * centred, axis=0, keepdims=True)
        if n == 0:
            for copy in loads:
                copy.wait()
            gain = jnp.broadcast_to(gain_s[...], (LANES, channels)).T
            gain = jnp.concatenate([gain] * (block // LANES), axis=1)
            right_w, left_w = wr_s[...].T, wl_s[...].T
        normed = (centred * lax.rsqrt(variance + EPS) * gain).astype(jnp.bfloat16)
        mask = mask_of(cols, first_row, first_col, lens_s, res_s, at, block)
        lanes = pl.ds(at, block)
        normed_s[:, lanes] = normed
        held[:, own:, lanes] = edge_of(right_w, normed, mask, groups)
        held[:, :own, lanes] = edge_of(left_w, normed, mask, groups)
        sent = []
        for u in range(groups):
            group = jnp.bitwise_xor(mine, u)
            sent.append((held.at[group, pl.ds(own, own), lanes], right_refs[u].at[:, lanes]))
            sent.append((held.at[group, :, lanes], both_refs[u].at[:, lanes]))
        sent.append((normed_s.at[:, lanes], normed_ref.at[:, lanes]))
        for m, (src, dst) in enumerate(sent):
            stores.append(pltpu.make_async_copy(src, dst, out_sems.at[n, m]))
            stores[-1].start()
    for copy in stores:
        copy.wait()


def make_edges(pair, lens, resolved, gain, w_left, w_right, groups, rows, cols):
    count, channels = pair.shape
    own = w_left.shape[1] // 2 // groups
    block = 512
    flat = ceil_to(count, block)
    chunks = [(at, min(block, count - at)) for at in range(0, count, block)]
    here = pl.BlockSpec(memory_space=pltpu.HBM)
    return pl.pallas_call(
        functools.partial(edges_kernel, groups, rows, cols, chunks),
        in_specs=[here] * 6,
        out_specs=[here] * (1 + 2 * groups),
        out_shape=[jax.ShapeDtypeStruct((channels, flat), jnp.bfloat16)]
        + [jax.ShapeDtypeStruct((2 * own, flat), jnp.bfloat16)] * groups
        + [jax.ShapeDtypeStruct((own, flat), jnp.bfloat16)] * groups,
        scratch_shapes=[
            pltpu.VMEM((flat, channels), pair.dtype),
            pltpu.VMEM(gain.shape, gain.dtype),
            pltpu.VMEM(w_left.shape, w_left.dtype),
            pltpu.VMEM(w_right.shape, w_right.dtype),
            pltpu.SMEM(lens.shape, lens.dtype),
            pltpu.SMEM(resolved.shape, resolved.dtype),
            pltpu.VMEM((channels, flat), jnp.bfloat16),
            pltpu.VMEM((groups, 2 * own, flat), jnp.bfloat16),
            pltpu.SemaphoreType.DMA((5 + len(chunks),)),
            pltpu.SemaphoreType.DMA((len(chunks), 1 + 2 * groups)),
        ],
        compiler_params=pltpu.CompilerParams(vmem_limit_bytes=VMEM_FIRST),
    )(pair, gain, w_left, w_right, lens, resolved)


def unpack(got_ref, held_refs, block, rows, cols, step):
    tiles = pl.cdiv(cols, LANES)
    ch = got_ref.shape[0] // len(held_refs)
    lane = lax.broadcasted_iota(jnp.int32, (ch, LANES), 1)
    for n, held in enumerate(held_refs):
        seen = {}

        def tile_of(t):
            if t not in seen:
                seen[t] = got_ref[n * ch:(n + 1) * ch, pl.ds(t * LANES, LANES)].astype(jnp.float32)
            return seen[t]

        for i in range(rows):
            for tt in range(tiles):
                length = min(LANES, cols - LANES * tt)
                t0, off = divmod(cols * i + LANES * tt, LANES)
                piece = tile_of(t0)
                if off:
                    piece = pltpu.roll(piece, LANES - off, 1)
                if off + length > LANES:
                    piece = jnp.where(lane < LANES - off, piece, pltpu.roll(tile_of(t0 + 1), LANES - off, 1))
                if length < LANES and n == 0:
                    piece = jnp.where(lane < length, piece, 0.0)
                base = pl.multiple_of((block * rows + i) * step, 8)
                held[tt, pl.ds(base, ch), :] = piece


def packed_tile(held, first, t, block, rows, cols, step, ch):
    tiles = pl.cdiv(cols, LANES)
    lane = lax.broadcasted_iota(jnp.int32, (ch, LANES), 1)
    tile = None
    for i in range(rows):
        for tt in range(tiles):
            shift = cols * i + LANES * tt - LANES * t
            length = min(LANES, cols - LANES * tt)
            if shift >= LANES or shift + length <= 0:
                continue
            base = pl.multiple_of((block * rows + i) * step, 8)
            piece = held[first + tt, pl.ds(base, ch), :]
            if shift % LANES:
                piece = pltpu.roll(piece, shift % LANES, 1)
            tile = piece if tile is None else jnp.where(lane < shift, tile, piece)
    return jnp.zeros((ch, LANES), jnp.float32) if tile is None else tile


def channel_of(held, d, count, step):
    return jnp.concatenate([held[t, pl.ds(d, count, stride=step), :] for t in range(held.shape[0])], axis=1)


def lines_kernel(groups, rows, cols, *refs):
    got_refs, lines_ref = refs[:-1], refs[-1]
    mine = place_of(groups, rows, cols)[2]
    count = len(got_refs)
    step = lines_ref.shape[1] // (count * rows)
    for u in range(count):
        block = jnp.bitwise_and(jnp.bitwise_xor(mine, u), count - 1)
        unpack(got_refs[u], (lines_ref,), block, rows, cols, step)


def products_kernel(groups, rows, cols, parts, lines_ref, *refs):
    half = groups // 2
    near_refs, far_refs = refs[:groups], refs[groups:groups + half]
    keep_refs, send_refs = refs[groups + half:groups + half + 2], refs[groups + half + 2:groups + half + 4]
    left_s, right_s, far_s, prod_s = refs[groups + half + 4:]
    _, _, mine, own_half, col = place_of(groups, rows, cols)
    ch = far_refs[0].shape[0]
    step = left_s.shape[1] // (groups * rows)
    count = groups * rows
    tiles = left_s.shape[0]
    size = lines_ref.shape[1]
    far_s[:, pl.ds(pl.multiple_of((1 - mine // half) * size, 8), size), :] = lines_ref[...]
    for u in range(groups):
        unpack(near_refs[u], (left_s, right_s), jnp.bitwise_xor(mine, u), rows, cols, step)
    for u in range(half):
        unpack(far_refs[u], (far_s,), jnp.bitwise_xor(mine, u), rows, cols, step)
    pad = [jnp.zeros((tiles * LANES - count, tiles * LANES), jnp.float32)] if count % LANES else []
    for d in range(ch):
        left = channel_of(left_s, d, count, step)
        right = jnp.concatenate(
            [channel_of(right_s, d, count, step)] + pad + [channel_of(far_s, d, count, step)] + pad, axis=0
        )
        prod = lax.dot_general(
            left.astype(jnp.bfloat16), right.astype(jnp.bfloat16), (((1,), (1,)), ((), ())),
            preferred_element_type=jnp.float32,
        )
        for t in range(2 * tiles):
            prod_s[t, pl.ds(d, count, stride=step), :] = prod[:, t * LANES:(t + 1) * LANES]
    near_kept = col == own_half
    for part, pieces in enumerate(parts):
        for n, u in enumerate(pieces):
            block = jnp.bitwise_xor(mine, u)
            for t in range(keep_refs[part].shape[2] // LANES):
                near = packed_tile(prod_s, 0, t, block, rows, cols, step, ch)
                far = packed_tile(prod_s, tiles, t, block, rows, cols, step, ch)
                lanes = pl.ds(t * LANES, LANES)
                keep_refs[part][n, :, lanes] = jnp.where(near_kept, near, far).astype(jnp.bfloat16)
                send_refs[part][n, :, lanes] = jnp.where(near_kept, far, near).astype(jnp.bfloat16)


def lines_of(blocks, ch, cols):
    return (pl.cdiv(cols, LANES), blocks * line_step(ch), LANES)


def make_lines(got, groups, rows, cols):
    ch = got[0].shape[0]
    whole = pl.BlockSpec(memory_space=pltpu.VMEM)
    return pl.pallas_call(
        functools.partial(lines_kernel, groups, rows, cols),
        in_specs=[whole] * len(got),
        out_specs=whole,
        out_shape=jax.ShapeDtypeStruct(lines_of(len(got) * rows, ch, cols), jnp.float32),
        compiler_params=pltpu.CompilerParams(vmem_limit_bytes=VMEM_LIMIT),
        cost_estimate=pl.CostEstimate(flops=10 ** 5, bytes_accessed=10 ** 8, transcendentals=0),
    )(*got)


def make_products(lines, near, far, parts, rows, cols):
    groups = len(near)
    ch, flat = far[0].shape
    whole = pl.BlockSpec(memory_space=pltpu.VMEM)
    tiles, held, _ = lines_of(groups * rows, ch, cols)
    one = pltpu.VMEM((tiles, held, LANES), jnp.float32)
    sizes = [len(pieces) for pieces in parts] * 2
    return pl.pallas_call(
        functools.partial(products_kernel, groups, rows, cols, parts),
        in_specs=[whole] * (1 + len(near) + len(far)),
        out_specs=[whole] * 4,
        out_shape=[jax.ShapeDtypeStruct((n, ch, flat), jnp.bfloat16) for n in sizes],
        scratch_shapes=[one, one, one, pltpu.VMEM((2 * tiles, held, LANES), jnp.float32)],
        compiler_params=pltpu.CompilerParams(vmem_limit_bytes=VMEM_LIMIT),
        cost_estimate=pl.CostEstimate(flops=10 ** 5, bytes_accessed=10 ** 7, transcendentals=0),
    )(lines, *near, *far)


def add_kernel(a_ref, b_ref, *out_refs):
    for u, out_ref in enumerate(out_refs):
        out_ref[...] = (a_ref[u].astype(jnp.float32) + b_ref[u].astype(jnp.float32)).astype(out_ref.dtype)


def make_sums(a, b):
    groups, ch, flat = a.shape
    whole = pl.BlockSpec(memory_space=pltpu.VMEM)
    return pl.pallas_call(
        add_kernel,
        in_specs=[whole] * 2,
        out_specs=[whole] * groups,
        out_shape=[jax.ShapeDtypeStruct((ch, flat), a.dtype)] * groups,
        compiler_params=pltpu.CompilerParams(vmem_limit_bytes=VMEM_LIMIT),
        cost_estimate=pl.CostEstimate(flops=10 ** 5, bytes_accessed=10 ** 5, transcendentals=0),
    )(a, b)


def update_kernel(groups, rows, cols, chunks, gain_ref, w_ref, gate_ref, *refs):
    prod_refs = refs[:groups]
    out_ref, held, out_s, sems = refs[groups:]
    mine = place_of(groups, rows, cols)[2]
    ch = held.shape[1]
    block = held.shape[2]
    stores = []
    for n, (at, size) in enumerate(chunks):
        lanes = pl.ds(at, block)
        for u in range(groups):
            held[jnp.bitwise_xor(mine, u)] = prod_refs[u][:, lanes].astype(jnp.float32)
        prod = held[...].reshape(groups * ch, block)
        mean = jnp.mean(prod, axis=0, keepdims=True)
        centred = prod - mean
        variance = jnp.mean(centred * centred, axis=0, keepdims=True)
        normed = (centred * lax.rsqrt(variance + EPS) * gain_ref[...]).astype(jnp.bfloat16)
        projected = lax.dot_general(normed, w_ref[...], (((0,), (0,)), ((), ())), preferred_element_type=jnp.float32)
        out_s[pl.ds(at, size)] = (gate_ref[pl.ds(at, size)] * projected[:size]).astype(out_s.dtype)
        stores.append(pltpu.make_async_copy(out_s.at[pl.ds(at, size)], out_ref.at[pl.ds(at, size)], sems.at[n]))
        stores[-1].start()
    for copy in stores:
        copy.wait()


def make_update(prods, gain, w_out, gate, rows, cols):
    groups = len(prods)
    ch = prods[0].shape[0]
    count, channels = gate.shape
    block = 512
    chunks = [(at, min(block, count - at)) for at in range(0, count, block)]
    whole = pl.BlockSpec(memory_space=pltpu.VMEM)
    return pl.pallas_call(
        functools.partial(update_kernel, groups, rows, cols, chunks),
        in_specs=[whole] * (3 + groups),
        out_specs=pl.BlockSpec(memory_space=pltpu.HBM),
        out_shape=jax.ShapeDtypeStruct((count, channels), jnp.bfloat16),
        scratch_shapes=[
            pltpu.VMEM((groups, ch, block), jnp.float32),
            pltpu.VMEM((count, channels), jnp.bfloat16),
            pltpu.SemaphoreType.DMA((len(chunks),)),
        ],
        compiler_params=pltpu.CompilerParams(vmem_limit_bytes=VMEM_LIMIT),
    )(gain, w_out, gate, *prods)


def swap(value, shift):
    return lax.ppermute(value, "row", [(r, r ^ shift) for r in range(lax.axis_size("row"))])


def shards(pair_act, chain_lengths, resolved, in_gain, out_gain, w_left, w_right, w_gate, w_out):
    rows, cols, channels = pair_act.shape
    hidden = w_out.shape[0]
    groups = lax.axis_size("row") // 2
    normed, *edges = make_edges(
        pair_act.reshape(rows * cols, channels), chain_lengths, resolved,
        in_gain.reshape(1, channels), w_left, w_right, groups, rows, cols,
    )
    both, right = edges[:groups], edges[groups:]
    far_got = [swap(right[u], groups + u) for u in range(groups)]
    near_got = [both[0]] + [swap(both[u], u) for u in range(1, groups)]
    gate = jax.nn.sigmoid(
        jnp.einsum("cp,cd->pd", normed[:, :rows * cols], w_gate, preferred_element_type=jnp.float32)
    )
    half = groups // 2
    lines = make_lines(far_got[half:], groups, rows, cols)
    parts = [list(range(1, half + 1)), [0] + list(range(half + 1, groups))]
    made = make_products(lines, near_got, far_got[:half], parts, rows, cols)
    sums = {}
    for part, pieces in enumerate(parts):
        other = lax.ppermute(made[2 + part], "col", [(0, 1), (1, 0)])
        sums.update(zip(pieces, make_sums(made[part], other)))
    returned = [sums[0]] + [swap(sums[u], u) for u in range(1, groups)]
    update = make_update(returned, out_gain.reshape(hidden, 1), w_out, gate, rows, cols)
    return update.reshape(rows, cols, channels)


def solution(mesh):
    return jax.shard_map(
        shards,
        mesh=mesh,
        in_specs=(P(("grp", "row"), "col", None), P("grp"), P("grp"), P(), P(), P(), P(), P(), P()),
        out_specs=P(("grp", "row"), "col", None),
        check_vma=False,
    )
```

```python
import functools

import jax
import jax.numpy as jnp
from jax import lax
from jax.experimental import pallas as pl
from jax.experimental.pallas import tpu as pltpu
from jax.sharding import PartitionSpec as P

EPS = 1e-05
LANES = 128
VMEM_LIMIT = 32 * 1024 * 1024
VMEM_FIRST = 60 * 1024 * 1024


def ceil_to(n, m):
    return -(-n // m) * m


def line_step(ch):
    return (ceil_to(ch, 8) // 8 | 1) * 8


def place_of(groups, rows, cols):
    row, col = lax.axis_index("row"), lax.axis_index("col")
    return row * rows, col * cols, lax.rem(row, groups), row // groups, col


def sigmoid(x):
    return 0.5 + 0.5 * jnp.tanh(0.5 * x)


def mask_of(cols, first_row, first_col, lens_ref, res_ref, at, block):
    position = at + lax.broadcasted_iota(jnp.int32, (8, block), 1)
    i_here = jnp.floor((position.astype(jnp.float32) + 0.5) * (1.0 / cols)).astype(jnp.int32)
    i_at = first_row + i_here
    k_at = first_col + position - i_here * cols
    i_ok = jnp.zeros((8, block), jnp.float32)
    k_ok = jnp.zeros((8, block), jnp.float32)
    start = 0
    for q in range(lens_ref.shape[0]):
        length = lens_ref[q]
        stop = start + jnp.minimum(length, res_ref[q])
        i_ok = jnp.where((i_at >= start) & (i_at < stop), 1.0, i_ok)
        k_ok = jnp.where((k_at >= start) & (k_at < stop), 1.0, k_ok)
        start = start + length
    return i_ok * k_ok


def edge_of(weights, normed, mask, groups):
    hidden = weights.shape[0] // 2
    block = normed.shape[1]
    projected = jnp.dot(weights, normed, preferred_element_type=jnp.float32)
    edge = sigmoid(projected[:hidden]) * projected[hidden:]
    edge = edge.reshape(hidden // 8, 8, block) * mask[None]
    return edge.reshape(groups, hidden // groups, block).astype(jnp.bfloat16)


def edges_kernel(groups, rows, cols, chunks, pair_ref, gain_ref, wl_ref, wr_ref, lens_ref, res_ref, normed_ref, *refs):
    both_refs, right_refs = refs[:groups], refs[groups:2 * groups]
    x_s, gain_s, wl_s, wr_s, lens_s, res_s, normed_s, held, in_sems, out_sems = refs[2 * groups:]
    count = rows * cols
    first_row, first_col, mine, _, _ = place_of(groups, rows, cols)
    own = wl_ref.shape[1] // 2 // groups
    loads = [
        pltpu.make_async_copy(src, dst, in_sems.at[n])
        for n, (src, dst) in enumerate(
            [(gain_ref, gain_s), (lens_ref, lens_s), (res_ref, res_s), (wr_ref, wr_s), (wl_ref, wl_s)]
        )
    ]
    pieces = [
        pltpu.make_async_copy(pair_ref.at[pl.ds(at, size)], x_s.at[pl.ds(at, size)], in_sems.at[len(loads) + n])
        for n, (at, size) in enumerate(chunks)
    ]
    for copy in pieces[:1] + loads + pieces[1:]:
        copy.start()
    block = chunks[0][1]
    channels = x_s.shape[1]
    spare = x_s.shape[0] - count
    if spare:
        x_s[pl.ds(count, spare)] = jnp.zeros((spare, x_s.shape[1]), x_s.dtype)
    stores = []
    for n, (at, size) in enumerate(chunks):
        pieces[n].wait()
        x = x_s[pl.ds(at, block)].T.astype(jnp.float32)
        centred = x - jnp.mean(x, axis=0, keepdims=True)
        variance = jnp.mean(centred * centred, axis=0, keepdims=True)
        if n == 0:
            for copy in loads:
                copy.wait()
            gain = jnp.broadcast_to(gain_s[...], (LANES, channels)).T
            gain = jnp.concatenate([gain] * (block // LANES), axis=1)
            right_w, left_w = wr_s[...].T, wl_s[...].T
        normed = (centred * lax.rsqrt(variance + EPS) * gain).astype(jnp.bfloat16)
        mask = mask_of(cols, first_row, first_col, lens_s, res_s, at, block)
        lanes = pl.ds(at, block)
        normed_s[:, lanes] = normed
        held[:, own:, lanes] = edge_of(right_w, normed, mask, groups)
        held[:, :own, lanes] = edge_of(left_w, normed, mask, groups)
        sent = []
        for u in range(groups):
            group = jnp.bitwise_xor(mine, u)
            sent.append((held.at[group, pl.ds(own, own), lanes], right_refs[u].at[:, lanes]))
            sent.append((held.at[group, :, lanes], both_refs[u].at[:, lanes]))
        sent.append((normed_s.at[:, lanes], normed_ref.at[:, lanes]))
        for m, (src, dst) in enumerate(sent):
            stores.append(pltpu.make_async_copy(src, dst, out_sems.at[n, m]))
            stores[-1].start()
    for copy in stores:
        copy.wait()


def make_edges(pair, lens, resolved, gain, w_left, w_right, groups, rows, cols):
    count, channels = pair.shape
    own = w_left.shape[1] // 2 // groups
    block = 256
    flat = ceil_to(count, block)
    chunks = [(at, min(block, count - at)) for at in range(0, count, block)]
    here = pl.BlockSpec(memory_space=pltpu.HBM)
    return pl.pallas_call(
        functools.partial(edges_kernel, groups, rows, cols, chunks),
        in_specs=[here] * 6,
        out_specs=[here] * (1 + 2 * groups),
        out_shape=[jax.ShapeDtypeStruct((channels, flat), jnp.bfloat16)]
        + [jax.ShapeDtypeStruct((2 * own, flat), jnp.bfloat16)] * groups
        + [jax.ShapeDtypeStruct((own, flat), jnp.bfloat16)] * groups,
        scratch_shapes=[
            pltpu.VMEM((flat, channels), pair.dtype),
            pltpu.VMEM(gain.shape, gain.dtype),
            pltpu.VMEM(w_left.shape, w_left.dtype),
            pltpu.VMEM(w_right.shape, w_right.dtype),
            pltpu.SMEM(lens.shape, lens.dtype),
            pltpu.SMEM(resolved.shape, resolved.dtype),
            pltpu.VMEM((channels, flat), jnp.bfloat16),
            pltpu.VMEM((groups, 2 * own, flat), jnp.bfloat16),
            pltpu.SemaphoreType.DMA((5 + len(chunks),)),
            pltpu.SemaphoreType.DMA((len(chunks), 1 + 2 * groups)),
        ],
        compiler_params=pltpu.CompilerParams(vmem_limit_bytes=VMEM_FIRST),
    )(pair, gain, w_left, w_right, lens, resolved)


def unpack(got_ref, held_refs, block, rows, cols, step):
    tiles = pl.cdiv(cols, LANES)
    ch = got_ref.shape[0] // len(held_refs)
    lane = lax.broadcasted_iota(jnp.int32, (ch, LANES), 1)
    for n, held in enumerate(held_refs):
        seen = {}

        def tile_of(t):
            if t not in seen:
                seen[t] = got_ref[n * ch:(n + 1) * ch, pl.ds(t * LANES, LANES)].astype(jnp.float32)
            return seen[t]

        for i in range(rows):
            for tt in range(tiles):
                length = min(LANES, cols - LANES * tt)
                t0, off = divmod(cols * i + LANES * tt, LANES)
                piece = tile_of(t0)
                if off:
                    piece = pltpu.roll(piece, LANES - off, 1)
                if off + length > LANES:
                    piece = jnp.where(lane < LANES - off, piece, pltpu.roll(tile_of(t0 + 1), LANES - off, 1))
                if length < LANES and n == 0:
                    piece = jnp.where(lane < length, piece, 0.0)
                base = pl.multiple_of((block * rows + i) * step, 8)
                held[tt, pl.ds(base, ch), :] = piece


def packed_tile(held, first, t, block, rows, cols, step, ch):
    tiles = pl.cdiv(cols, LANES)
    lane = lax.broadcasted_iota(jnp.int32, (ch, LANES), 1)
    tile = None
    for i in range(rows):
        for tt in range(tiles):
            shift = cols * i + LANES * tt - LANES * t
            length = min(LANES, cols - LANES * tt)
            if shift >= LANES or shift + length <= 0:
                continue
            base = pl.multiple_of((block * rows + i) * step, 8)
            piece = held[first + tt, pl.ds(base, ch), :]
            if shift % LANES:
                piece = pltpu.roll(piece, shift % LANES, 1)
            tile = piece if tile is None else jnp.where(lane < shift, tile, piece)
    return jnp.zeros((ch, LANES), jnp.float32) if tile is None else tile


def channel_of(held, d, count, step):
    return jnp.concatenate([held[t, pl.ds(d, count, stride=step), :] for t in range(held.shape[0])], axis=1)


def lines_kernel(rows, cols, *refs):
    count = len(refs) // 2
    for got_ref, lines_ref in zip(refs[:count], refs[count:]):
        unpack(got_ref, (lines_ref,), 0, rows, cols, lines_ref.shape[1] // rows)


def products_kernel(groups, rows, cols, parts, early, late, *refs):
    lines_refs, near_refs, far_refs = refs[:len(early)], refs[len(early):][:groups], refs[len(early) + groups:][:len(late)]
    keep_refs, send_refs = refs[2 * groups:2 * groups + 2], refs[2 * groups + 2:2 * groups + 4]
    left_s, right_s, far_s, prod_s = refs[2 * groups + 4:]
    _, _, mine, own_half, col = place_of(groups, rows, cols)
    ch = keep_refs[0].shape[1]
    step = left_s.shape[1] // (groups * rows)
    count = groups * rows
    tiles = left_s.shape[0]
    for u, lines_ref in zip(early, lines_refs):
        far_s[:, pl.ds(pl.multiple_of(jnp.bitwise_xor(mine, u) * rows * step, 8), rows * step), :] = lines_ref[...]
    for u in range(groups):
        unpack(near_refs[u], (left_s, right_s), jnp.bitwise_xor(mine, u), rows, cols, step)
    for u, far_ref in zip(late, far_refs):
        unpack(far_ref, (far_s,), jnp.bitwise_xor(mine, u), rows, cols, step)
    pad = [jnp.zeros((tiles * LANES - count, tiles * LANES), jnp.float32)] if count % LANES else []
    for d in range(ch):
        left = channel_of(left_s, d, count, step)
        right = jnp.concatenate(
            [channel_of(right_s, d, count, step)] + pad + [channel_of(far_s, d, count, step)] + pad, axis=0
        )
        prod = lax.dot_general(
            left.astype(jnp.bfloat16), right.astype(jnp.bfloat16), (((1,), (1,)), ((), ())),
            preferred_element_type=jnp.float32,
        )
        for t in range(2 * tiles):
            prod_s[t, pl.ds(d, count, stride=step), :] = prod[:, t * LANES:(t + 1) * LANES]
    near_kept = col == own_half
    for part, pieces in enumerate(parts):
        for n, u in enumerate(pieces):
            block = jnp.bitwise_xor(mine, u)
            for t in range(keep_refs[part].shape[2] // LANES):
                near = packed_tile(prod_s, 0, t, block, rows, cols, step, ch)
                far = packed_tile(prod_s, tiles, t, block, rows, cols, step, ch)
                lanes = pl.ds(t * LANES, LANES)
                keep_refs[part][n, :, lanes] = jnp.where(near_kept, near, far).astype(jnp.bfloat16)
                send_refs[part][n, :, lanes] = jnp.where(near_kept, far, near).astype(jnp.bfloat16)


def lines_of(blocks, ch, cols):
    return (pl.cdiv(cols, LANES), blocks * line_step(ch), LANES)


def make_lines(got, rows, cols):
    ch = got[0].shape[0]
    whole = pl.BlockSpec(memory_space=pltpu.VMEM)
    return pl.pallas_call(
        functools.partial(lines_kernel, rows, cols),
        in_specs=[whole] * len(got),
        out_specs=[whole] * len(got),
        out_shape=[jax.ShapeDtypeStruct(lines_of(rows, ch, cols), jnp.float32)] * len(got),
        compiler_params=pltpu.CompilerParams(vmem_limit_bytes=VMEM_LIMIT),
        cost_estimate=pl.CostEstimate(flops=10 ** 5, bytes_accessed=10 ** 8, transcendentals=0),
    )(*got)


def make_products(lines, near, far, parts, early, late, rows, cols):
    groups = len(near)
    ch, flat = near[0].shape[0] // 2, near[0].shape[1]
    whole = pl.BlockSpec(memory_space=pltpu.VMEM)
    tiles, held, _ = lines_of(groups * rows, ch, cols)
    one = pltpu.VMEM((tiles, held, LANES), jnp.float32)
    sizes = [len(pieces) for pieces in parts] * 2
    return pl.pallas_call(
        functools.partial(products_kernel, groups, rows, cols, parts, early, late),
        in_specs=[whole] * (2 * groups),
        out_specs=[whole] * 4,
        out_shape=[jax.ShapeDtypeStruct((n, ch, flat), jnp.bfloat16) for n in sizes],
        scratch_shapes=[one, one, one, pltpu.VMEM((2 * tiles, held, LANES), jnp.float32)],
        compiler_params=pltpu.CompilerParams(vmem_limit_bytes=VMEM_LIMIT),
        cost_estimate=pl.CostEstimate(flops=10 ** 5, bytes_accessed=10 ** 7, transcendentals=0),
    )(*lines, *near, *far)


def add_kernel(a_ref, b_ref, *out_refs):
    for u, out_ref in enumerate(out_refs):
        out_ref[...] = (a_ref[u].astype(jnp.float32) + b_ref[u].astype(jnp.float32)).astype(out_ref.dtype)


def make_sums(a, b):
    groups, ch, flat = a.shape
    whole = pl.BlockSpec(memory_space=pltpu.VMEM)
    return pl.pallas_call(
        add_kernel,
        in_specs=[whole] * 2,
        out_specs=[whole] * groups,
        out_shape=[jax.ShapeDtypeStruct((ch, flat), a.dtype)] * groups,
        compiler_params=pltpu.CompilerParams(vmem_limit_bytes=VMEM_LIMIT),
        cost_estimate=pl.CostEstimate(flops=10 ** 5, bytes_accessed=10 ** 5, transcendentals=0),
    )(a, b)


def update_kernel(groups, rows, cols, chunks, gain_ref, w_ref, gate_ref, *refs):
    prod_refs = refs[:groups]
    out_ref, gain_s, w_s, out_s, sems = refs[groups:]
    mine = place_of(groups, rows, cols)[2]
    ch = prod_refs[0].shape[0]
    block = chunks[0][1]
    for u in range(groups):
        there = pl.ds(pl.multiple_of(jnp.bitwise_xor(mine, u) * ch, 8), ch)
        gain_s[u * ch:(u + 1) * ch] = gain_ref[there]
        w_s[u * ch:(u + 1) * ch] = w_ref[there]
    gain, weights = gain_s[...], w_s[...].astype(jnp.bfloat16)
    stores = []
    for n, (at, size) in enumerate(chunks):
        lanes = pl.ds(at, block)
        prod = jnp.concatenate([ref[:, lanes].astype(jnp.float32) for ref in prod_refs], axis=0)
        mean = jnp.mean(prod, axis=0, keepdims=True)
        centred = prod - mean
        variance = jnp.mean(centred * centred, axis=0, keepdims=True)
        normed = (centred * lax.rsqrt(variance + EPS) * gain).astype(jnp.bfloat16)
        projected = lax.dot_general(normed, weights, (((0,), (0,)), ((), ())), preferred_element_type=jnp.float32)
        out_s[pl.ds(at, size)] = (gate_ref[pl.ds(at, size)] * projected[:size]).astype(out_s.dtype)
        stores.append(pltpu.make_async_copy(out_s.at[pl.ds(at, size)], out_ref.at[pl.ds(at, size)], sems.at[n]))
        stores[-1].start()
    for copy in stores:
        copy.wait()


def make_update(prods, gain, w_out, gate, rows, cols):
    groups = len(prods)
    ch = prods[0].shape[0]
    count, channels = gate.shape
    block = 256
    chunks = [(at, min(block, count - at)) for at in range(0, count, block)]
    whole = pl.BlockSpec(memory_space=pltpu.VMEM)
    return pl.pallas_call(
        functools.partial(update_kernel, groups, rows, cols, chunks),
        in_specs=[whole] * (3 + groups),
        out_specs=pl.BlockSpec(memory_space=pltpu.HBM),
        out_shape=jax.ShapeDtypeStruct((count, channels), jnp.bfloat16),
        scratch_shapes=[
            pltpu.VMEM(gain.shape, jnp.float32),
            pltpu.VMEM(w_out.shape, jnp.float32),
            pltpu.VMEM((count, channels), jnp.bfloat16),
            pltpu.SemaphoreType.DMA((len(chunks),)),
        ],
        compiler_params=pltpu.CompilerParams(vmem_limit_bytes=VMEM_LIMIT),
    )(gain, w_out, gate, *prods)


def swap(value, shift):
    return lax.ppermute(value, "row", [(r, r ^ shift) for r in range(lax.axis_size("row"))])


def shards(pair_act, chain_lengths, resolved, in_gain, out_gain, w_left, w_right, w_gate, w_out):
    rows, cols, channels = pair_act.shape
    hidden = w_out.shape[0]
    groups = lax.axis_size("row") // 2
    normed, *edges = make_edges(
        pair_act.reshape(rows * cols, channels), chain_lengths, resolved,
        in_gain.reshape(1, channels), w_left, w_right, groups, rows, cols,
    )
    both, right = edges[:groups], edges[groups:]
    far_got = [swap(right[u], groups + u) for u in range(groups)]
    near_got = [both[0]] + [swap(both[u], u) for u in range(1, groups)]
    gate = jax.nn.sigmoid(
        jnp.einsum("cp,cd->pd", normed[:, :rows * cols], w_gate, preferred_element_type=jnp.float32)
    )
    half = groups // 2
    early, late = list(range(half, groups)) + [0], list(range(1, half))
    lines = make_lines([far_got[u] for u in early], rows, cols)
    parts = [list(range(1, half + 1)), [0] + list(range(half + 1, groups))]
    made = make_products(lines, near_got, [far_got[u] for u in late], parts, early, late, rows, cols)
    sums = {}
    for part, pieces in enumerate(parts):
        other = lax.ppermute(made[2 + part], "col", [(0, 1), (1, 0)])
        sums.update(zip(pieces, make_sums(made[part], other)))
    returned = [sums[0]] + [swap(sums[u], u) for u in range(1, groups)]
    update = make_update(returned, out_gain.reshape(hidden, 1), w_out.astype(jnp.float32), gate, rows, cols)
    return update.reshape(rows, cols, channels)


def solution(mesh):
    return jax.shard_map(
        shards,
        mesh=mesh,
        in_specs=(P(("grp", "row"), "col", None), P("grp"), P("grp"), P(), P(), P(), P(), P(), P()),
        out_specs=P(("grp", "row"), "col", None),
        check_vma=False,
    )
```

```python
import functools

import jax
import jax.numpy as jnp
from jax import lax
from jax.experimental import pallas as pl
from jax.experimental.pallas import tpu as pltpu
from jax.sharding import PartitionSpec as P

EPS = 1e-05
LANES = 128
VMEM_LIMIT = 32 * 1024 * 1024
VMEM_FIRST = 60 * 1024 * 1024


def ceil_to(n, m):
    return -(-n // m) * m


def line_step(ch):
    return (ceil_to(ch, 8) // 8 | 1) * 8


def place_of(groups, rows, cols):
    row, col = lax.axis_index("row"), lax.axis_index("col")
    return row * rows, col * cols, lax.rem(row, groups), row // groups, col


def sigmoid(x):
    return 0.5 + 0.5 * jnp.tanh(0.5 * x)


def mask_of(cols, first_row, first_col, lens_ref, res_ref, at, block):
    position = at + lax.broadcasted_iota(jnp.int32, (8, block), 1)
    i_here = jnp.floor((position.astype(jnp.float32) + 0.5) * (1.0 / cols)).astype(jnp.int32)
    i_at = first_row + i_here
    k_at = first_col + position - i_here * cols
    i_ok = jnp.zeros((8, block), jnp.float32)
    k_ok = jnp.zeros((8, block), jnp.float32)
    start = 0
    for q in range(lens_ref.shape[0]):
        length = lens_ref[q]
        stop = start + jnp.minimum(length, res_ref[q])
        i_ok = jnp.where((i_at >= start) & (i_at < stop), 1.0, i_ok)
        k_ok = jnp.where((k_at >= start) & (k_at < stop), 1.0, k_ok)
        start = start + length
    return i_ok * k_ok


def edge_of(weights, normed, mask, groups):
    hidden = weights.shape[0] // 2
    block = normed.shape[1]
    projected = jnp.dot(weights, normed, preferred_element_type=jnp.float32)
    edge = sigmoid(projected[:hidden]) * projected[hidden:]
    edge = edge.reshape(hidden // 8, 8, block) * mask[None]
    return edge.reshape(groups, hidden // groups, block).astype(jnp.bfloat16)


def edges_kernel(groups, rows, cols, chunks, pair_ref, gain_ref, wl_ref, wr_ref, lens_ref, res_ref, normed_ref, *refs):
    both_refs, right_refs = refs[:groups], refs[groups:2 * groups]
    x_s, gain_s, wl_s, wr_s, lens_s, res_s, normed_s, held, in_sems, out_sems = refs[2 * groups:]
    count = rows * cols
    first_row, first_col, mine, _, _ = place_of(groups, rows, cols)
    own = wl_ref.shape[1] // 2 // groups
    loads = [
        pltpu.make_async_copy(src, dst, in_sems.at[n])
        for n, (src, dst) in enumerate(
            [(gain_ref, gain_s), (lens_ref, lens_s), (res_ref, res_s), (wr_ref, wr_s), (wl_ref, wl_s)]
        )
    ]
    pieces = [
        pltpu.make_async_copy(pair_ref.at[pl.ds(at, size)], x_s.at[pl.ds(at, size)], in_sems.at[len(loads) + n])
        for n, (at, size) in enumerate(chunks)
    ]
    for copy in pieces[:1] + loads + pieces[1:]:
        copy.start()
    block = chunks[0][1]
    channels = x_s.shape[1]
    spare = x_s.shape[0] - count
    if spare:
        x_s[pl.ds(count, spare)] = jnp.zeros((spare, x_s.shape[1]), x_s.dtype)
    stores = []
    for n, (at, size) in enumerate(chunks):
        pieces[n].wait()
        x = x_s[pl.ds(at, block)].T.astype(jnp.float32)
        centred = x - jnp.mean(x, axis=0, keepdims=True)
        variance = jnp.mean(centred * centred, axis=0, keepdims=True)
        if n == 0:
            for copy in loads:
                copy.wait()
            gain = jnp.broadcast_to(gain_s[...], (LANES, channels)).T
            gain = jnp.concatenate([gain] * (block // LANES), axis=1)
            right_w, left_w = wr_s[...].T, wl_s[...].T
        normed = (centred * lax.rsqrt(variance + EPS) * gain).astype(jnp.bfloat16)
        mask = mask_of(cols, first_row, first_col, lens_s, res_s, at, block)
        lanes = pl.ds(at, block)
        normed_s[:, lanes] = normed
        held[:, own:, lanes] = edge_of(right_w, normed, mask, groups)
        held[:, :own, lanes] = edge_of(left_w, normed, mask, groups)
        sent = []
        for u in range(groups):
            group = jnp.bitwise_xor(mine, u)
            sent.append((held.at[group, pl.ds(own, own), lanes], right_refs[u].at[:, lanes]))
            sent.append((held.at[group, :, lanes], both_refs[u].at[:, lanes]))
        sent.append((normed_s.at[:, lanes], normed_ref.at[:, lanes]))
        for m, (src, dst) in enumerate(sent):
            stores.append(pltpu.make_async_copy(src, dst, out_sems.at[n, m]))
            stores[-1].start()
    for copy in stores:
        copy.wait()


def make_edges(pair, lens, resolved, gain, w_left, w_right, groups, rows, cols):
    count, channels = pair.shape
    own = w_left.shape[1] // 2 // groups
    block = 1024
    flat = ceil_to(count, block)
    chunks = [(at, min(block, count - at)) for at in range(0, count, block)]
    here = pl.BlockSpec(memory_space=pltpu.HBM)
    return pl.pallas_call(
        functools.partial(edges_kernel, groups, rows, cols, chunks),
        in_specs=[here] * 6,
        out_specs=[here] * (1 + 2 * groups),
        out_shape=[jax.ShapeDtypeStruct((channels, flat), jnp.bfloat16)]
        + [jax.ShapeDtypeStruct((2 * own, flat), jnp.bfloat16)] * groups
        + [jax.ShapeDtypeStruct((own, flat), jnp.bfloat16)] * groups,
        scratch_shapes=[
            pltpu.VMEM((flat, channels), pair.dtype),
            pltpu.VMEM(gain.shape, gain.dtype),
            pltpu.VMEM(w_left.shape, w_left.dtype),
            pltpu.VMEM(w_right.shape, w_right.dtype),
            pltpu.SMEM(lens.shape, lens.dtype),
            pltpu.SMEM(resolved.shape, resolved.dtype),
            pltpu.VMEM((channels, flat), jnp.bfloat16),
            pltpu.VMEM((groups, 2 * own, flat), jnp.bfloat16),
            pltpu.SemaphoreType.DMA((5 + len(chunks),)),
            pltpu.SemaphoreType.DMA((len(chunks), 1 + 2 * groups)),
        ],
        compiler_params=pltpu.CompilerParams(vmem_limit_bytes=VMEM_FIRST),
    )(pair, gain, w_left, w_right, lens, resolved)


def unpack(got_ref, held_refs, block, rows, cols, step):
    tiles = pl.cdiv(cols, LANES)
    ch = got_ref.shape[0] // len(held_refs)
    lane = lax.broadcasted_iota(jnp.int32, (ch, LANES), 1)
    for n, held in enumerate(held_refs):
        seen = {}

        def tile_of(t):
            if t not in seen:
                seen[t] = got_ref[n * ch:(n + 1) * ch, pl.ds(t * LANES, LANES)].astype(jnp.float32)
            return seen[t]

        for i in range(rows):
            for tt in range(tiles):
                length = min(LANES, cols - LANES * tt)
                t0, off = divmod(cols * i + LANES * tt, LANES)
                piece = tile_of(t0)
                if off:
                    piece = pltpu.roll(piece, LANES - off, 1)
                if off + length > LANES:
                    piece = jnp.where(lane < LANES - off, piece, pltpu.roll(tile_of(t0 + 1), LANES - off, 1))
                if length < LANES and n == 0:
                    piece = jnp.where(lane < length, piece, 0.0)
                base = pl.multiple_of((block * rows + i) * step, 8)
                held[tt, pl.ds(base, ch), :] = piece


def packed_tile(held, first, t, block, rows, cols, step, ch):
    tiles = pl.cdiv(cols, LANES)
    lane = lax.broadcasted_iota(jnp.int32, (ch, LANES), 1)
    tile = None
    for i in range(rows):
        for tt in range(tiles):
            shift = cols * i + LANES * tt - LANES * t
            length = min(LANES, cols - LANES * tt)
            if shift >= LANES or shift + length <= 0:
                continue
            base = pl.multiple_of((block * rows + i) * step, 8)
            piece = held[first + tt, pl.ds(base, ch), :]
            if shift % LANES:
                piece = pltpu.roll(piece, shift % LANES, 1)
            tile = piece if tile is None else jnp.where(lane < shift, tile, piece)
    return jnp.zeros((ch, LANES), jnp.float32) if tile is None else tile


def channel_of(held, d, count, step):
    return jnp.concatenate([held[t, pl.ds(d, count, stride=step), :] for t in range(held.shape[0])], axis=1)


def lines_kernel(rows, cols, *refs):
    count = len(refs) // 2
    for got_ref, lines_ref in zip(refs[:count], refs[count:]):
        unpack(got_ref, (lines_ref,), 0, rows, cols, lines_ref.shape[1] // rows)


def products_kernel(groups, rows, cols, parts, early, late, *refs):
    lines_refs, near_refs, far_refs = refs[:len(early)], refs[len(early):][:groups], refs[len(early) + groups:][:len(late)]
    keep_refs, send_refs = refs[2 * groups:2 * groups + 2], refs[2 * groups + 2:2 * groups + 4]
    left_s, right_s, far_s, prod_s = refs[2 * groups + 4:]
    _, _, mine, own_half, col = place_of(groups, rows, cols)
    ch = keep_refs[0].shape[1]
    step = left_s.shape[1] // (groups * rows)
    count = groups * rows
    tiles = left_s.shape[0]
    for u, lines_ref in zip(early, lines_refs):
        far_s[:, pl.ds(pl.multiple_of(jnp.bitwise_xor(mine, u) * rows * step, 8), rows * step), :] = lines_ref[...]
    for u in range(groups):
        unpack(near_refs[u], (left_s, right_s), jnp.bitwise_xor(mine, u), rows, cols, step)
    for u, far_ref in zip(late, far_refs):
        unpack(far_ref, (far_s,), jnp.bitwise_xor(mine, u), rows, cols, step)
    pad = [jnp.zeros((tiles * LANES - count, tiles * LANES), jnp.float32)] if count % LANES else []
    for d in range(ch):
        left = channel_of(left_s, d, count, step)
        right = jnp.concatenate(
            [channel_of(right_s, d, count, step)] + pad + [channel_of(far_s, d, count, step)] + pad, axis=0
        )
        prod = lax.dot_general(
            left.astype(jnp.bfloat16), right.astype(jnp.bfloat16), (((1,), (1,)), ((), ())),
            preferred_element_type=jnp.float32,
        )
        for t in range(2 * tiles):
            prod_s[t, pl.ds(d, count, stride=step), :] = prod[:, t * LANES:(t + 1) * LANES]
    near_kept = col == own_half
    for part, pieces in enumerate(parts):
        for n, u in enumerate(pieces):
            block = jnp.bitwise_xor(mine, u)
            for t in range(keep_refs[part].shape[2] // LANES):
                near = packed_tile(prod_s, 0, t, block, rows, cols, step, ch)
                far = packed_tile(prod_s, tiles, t, block, rows, cols, step, ch)
                lanes = pl.ds(t * LANES, LANES)
                keep_refs[part][n, :, lanes] = jnp.where(near_kept, near, far).astype(jnp.bfloat16)
                send_refs[part][n, :, lanes] = jnp.where(near_kept, far, near).astype(jnp.bfloat16)


def lines_of(blocks, ch, cols):
    return (pl.cdiv(cols, LANES), blocks * line_step(ch), LANES)


def make_lines(got, rows, cols):
    ch = got[0].shape[0]
    whole = pl.BlockSpec(memory_space=pltpu.VMEM)
    return pl.pallas_call(
        functools.partial(lines_kernel, rows, cols),
        in_specs=[whole] * len(got),
        out_specs=[whole] * len(got),
        out_shape=[jax.ShapeDtypeStruct(lines_of(rows, ch, cols), jnp.float32)] * len(got),
        compiler_params=pltpu.CompilerParams(vmem_limit_bytes=VMEM_LIMIT),
        cost_estimate=pl.CostEstimate(flops=10 ** 5, bytes_accessed=10 ** 8, transcendentals=0),
    )(*got)


def make_products(lines, near, far, parts, early, late, rows, cols):
    groups = len(near)
    ch, flat = near[0].shape[0] // 2, near[0].shape[1]
    whole = pl.BlockSpec(memory_space=pltpu.VMEM)
    tiles, held, _ = lines_of(groups * rows, ch, cols)
    one = pltpu.VMEM((tiles, held, LANES), jnp.float32)
    sizes = [len(pieces) for pieces in parts] * 2
    return pl.pallas_call(
        functools.partial(products_kernel, groups, rows, cols, parts, early, late),
        in_specs=[whole] * (2 * groups),
        out_specs=[whole] * 4,
        out_shape=[jax.ShapeDtypeStruct((n, ch, flat), jnp.bfloat16) for n in sizes],
        scratch_shapes=[one, one, one, pltpu.VMEM((2 * tiles, held, LANES), jnp.float32)],
        compiler_params=pltpu.CompilerParams(vmem_limit_bytes=VMEM_LIMIT),
        cost_estimate=pl.CostEstimate(flops=10 ** 5, bytes_accessed=10 ** 7, transcendentals=0),
    )(*lines, *near, *far)


def add_kernel(a_ref, b_ref, *out_refs):
    for u, out_ref in enumerate(out_refs):
        out_ref[...] = (a_ref[u].astype(jnp.float32) + b_ref[u].astype(jnp.float32)).astype(out_ref.dtype)


def make_sums(a, b):
    groups, ch, flat = a.shape
    whole = pl.BlockSpec(memory_space=pltpu.VMEM)
    return pl.pallas_call(
        add_kernel,
        in_specs=[whole] * 2,
        out_specs=[whole] * groups,
        out_shape=[jax.ShapeDtypeStruct((ch, flat), a.dtype)] * groups,
        compiler_params=pltpu.CompilerParams(vmem_limit_bytes=VMEM_LIMIT),
        cost_estimate=pl.CostEstimate(flops=10 ** 5, bytes_accessed=10 ** 5, transcendentals=0),
    )(a, b)


def update_kernel(groups, rows, cols, chunks, gain_ref, w_ref, gate_ref, *refs):
    prod_refs = refs[:groups]
    out_ref, gain_s, w_s, out_s, sems = refs[groups:]
    mine = place_of(groups, rows, cols)[2]
    ch = prod_refs[0].shape[0]
    block = chunks[0][1]
    for u in range(groups):
        there = pl.ds(pl.multiple_of(jnp.bitwise_xor(mine, u) * ch, 8), ch)
        gain_s[u * ch:(u + 1) * ch] = gain_ref[there]
        w_s[u * ch:(u + 1) * ch] = w_ref[there]
    gain, weights = gain_s[...], w_s[...].astype(jnp.bfloat16)
    stores = []
    for n, (at, size) in enumerate(chunks):
        lanes = pl.ds(at, block)
        prod = jnp.concatenate([ref[:, lanes].astype(jnp.float32) for ref in prod_refs], axis=0)
        mean = jnp.mean(prod, axis=0, keepdims=True)
        centred = prod - mean
        variance = jnp.mean(centred * centred, axis=0, keepdims=True)
        normed = (centred * lax.rsqrt(variance + EPS) * gain).astype(jnp.bfloat16)
        projected = lax.dot_general(normed, weights, (((0,), (0,)), ((), ())), preferred_element_type=jnp.float32)
        out_s[pl.ds(at, size)] = (gate_ref[pl.ds(at, size)] * projected[:size]).astype(out_s.dtype)
        stores.append(pltpu.make_async_copy(out_s.at[pl.ds(at, size)], out_ref.at[pl.ds(at, size)], sems.at[n]))
        stores[-1].start()
    for copy in stores:
        copy.wait()


def make_update(prods, gain, w_out, gate, rows, cols):
    groups = len(prods)
    ch = prods[0].shape[0]
    count, channels = gate.shape
    block = 512
    chunks = [(at, min(block, count - at)) for at in range(0, count, block)]
    whole = pl.BlockSpec(memory_space=pltpu.VMEM)
    return pl.pallas_call(
        functools.partial(update_kernel, groups, rows, cols, chunks),
        in_specs=[whole] * (3 + groups),
        out_specs=pl.BlockSpec(memory_space=pltpu.HBM),
        out_shape=jax.ShapeDtypeStruct((count, channels), jnp.bfloat16),
        scratch_shapes=[
            pltpu.VMEM(gain.shape, jnp.float32),
            pltpu.VMEM(w_out.shape, jnp.float32),
            pltpu.VMEM((count, channels), jnp.bfloat16),
            pltpu.SemaphoreType.DMA((len(chunks),)),
        ],
        compiler_params=pltpu.CompilerParams(vmem_limit_bytes=VMEM_LIMIT),
    )(gain, w_out, gate, *prods)


def swap(value, shift):
    return lax.ppermute(value, "row", [(r, r ^ shift) for r in range(lax.axis_size("row"))])


def shards(pair_act, chain_lengths, resolved, in_gain, out_gain, w_left, w_right, w_gate, w_out):
    rows, cols, channels = pair_act.shape
    hidden = w_out.shape[0]
    groups = lax.axis_size("row") // 2
    normed, *edges = make_edges(
        pair_act.reshape(rows * cols, channels), chain_lengths, resolved,
        in_gain.reshape(1, channels), w_left, w_right, groups, rows, cols,
    )
    both, right = edges[:groups], edges[groups:]
    far_got = [swap(right[u], groups + u) for u in range(groups)]
    near_got = [both[0]] + [swap(both[u], u) for u in range(1, groups)]
    gate = jax.nn.sigmoid(
        jnp.einsum("cp,cd->pd", normed[:, :rows * cols], w_gate, preferred_element_type=jnp.float32)
    )
    half = groups // 2
    early, late = list(range(half, groups)) + [0], list(range(1, half))
    lines = make_lines([far_got[u] for u in early], rows, cols)
    parts = [list(range(1, half + 1)), [0] + list(range(half + 1, groups))]
    made = make_products(lines, near_got, [far_got[u] for u in late], parts, early, late, rows, cols)
    sums = {}
    for part, pieces in enumerate(parts):
        other = lax.ppermute(made[2 + part], "col", [(0, 1), (1, 0)])
        sums.update(zip(pieces, make_sums(made[part], other)))
    returned = [sums[0]] + [swap(sums[u], u) for u in range(1, groups)]
    update = make_update(returned, out_gain.reshape(hidden, 1), w_out.astype(jnp.float32), gate, rows, cols)
    return update.reshape(rows, cols, channels)


def solution(mesh):
    return jax.shard_map(
        shards,
        mesh=mesh,
        in_specs=(P(("grp", "row"), "col", None), P("grp"), P("grp"), P(), P(), P(), P(), P(), P()),
        out_specs=P(("grp", "row"), "col", None),
        check_vma=False,
    )
```

```python
import functools

import jax
import jax.numpy as jnp
from jax import lax
from jax.experimental import pallas as pl
from jax.experimental.pallas import tpu as pltpu
from jax.sharding import PartitionSpec as P

EPS = 1e-05
LANES = 128
VMEM_LIMIT = 32 * 1024 * 1024
STRIP = 16
VMEM_FIRST = 60 * 1024 * 1024


def ceil_to(n, m):
    return -(-n // m) * m


def line_step(ch):
    return (ceil_to(ch, 8) // 8 | 1) * 8


def place_of(groups, rows, cols):
    row, col = lax.axis_index("row"), lax.axis_index("col")
    return row * rows, col * cols, lax.rem(row, groups), row // groups, col


def sigmoid(x):
    return 0.5 + 0.5 * jnp.tanh(0.5 * x)


def mask_of(cols, first_row, first_col, lens_ref, res_ref, at, block):
    position = at + lax.broadcasted_iota(jnp.int32, (8, block), 1)
    i_here = jnp.floor((position.astype(jnp.float32) + 0.5) * (1.0 / cols)).astype(jnp.int32)
    i_at = first_row + i_here
    k_at = first_col + position - i_here * cols
    i_ok = jnp.zeros((8, block), jnp.float32)
    k_ok = jnp.zeros((8, block), jnp.float32)
    start = 0
    for q in range(lens_ref.shape[0]):
        length = lens_ref[q]
        stop = start + jnp.minimum(length, res_ref[q])
        i_ok = jnp.where((i_at >= start) & (i_at < stop), 1.0, i_ok)
        k_ok = jnp.where((k_at >= start) & (k_at < stop), 1.0, k_ok)
        start = start + length
    return i_ok * k_ok


def edge_of(weights, normed, mask, groups):
    hidden = weights.shape[0] // 2
    block = normed.shape[1]
    projected = jnp.dot(weights, normed, preferred_element_type=jnp.float32)
    edge = sigmoid(projected[:hidden]) * projected[hidden:]
    edge = edge.reshape(hidden // 8, 8, block) * mask[None]
    return edge.reshape(groups, hidden // groups, block)


def edges_kernel(groups, rows, cols, chunks, pair_ref, gain_ref, wl_ref, wr_ref, lens_ref, res_ref, normed_ref, *refs):
    both_refs, right_refs = refs[:groups], refs[groups:2 * groups]
    x_s, gain_s, wl_s, wr_s, lens_s, res_s, normed_s, both_s, right_s, in_sems, out_sems = refs[2 * groups:]
    count = rows * cols
    first_row, first_col, mine, _, _ = place_of(groups, rows, cols)
    own = wl_ref.shape[1] // 2 // groups
    loads = [
        pltpu.make_async_copy(src, dst, in_sems.at[n])
        for n, (src, dst) in enumerate(
            [(gain_ref, gain_s), (lens_ref, lens_s), (res_ref, res_s), (wr_ref, wr_s), (wl_ref, wl_s)]
        )
    ]
    pieces = [
        pltpu.make_async_copy(pair_ref.at[pl.ds(at, size)], x_s.at[pl.ds(at, size)], in_sems.at[len(loads) + n])
        for n, (at, size) in enumerate(chunks)
    ]
    for copy in pieces[:1] + loads + pieces[1:]:
        copy.start()
    block = chunks[0][1]
    whole, over = tiles_of(rows, cols)
    channels = x_s.shape[1]
    spare = x_s.shape[0] - count
    if spare:
        x_s[pl.ds(count, spare)] = jnp.zeros((spare, x_s.shape[1]), x_s.dtype)
    stores = []
    for n, (at, size) in enumerate(chunks):
        pieces[n].wait()
        x = x_s[pl.ds(at, block)].T.astype(jnp.float32)
        centred = x - jnp.mean(x, axis=0, keepdims=True)
        variance = jnp.mean(centred * centred, axis=0, keepdims=True)
        if n == 0:
            for copy in loads:
                copy.wait()
            gain = jnp.broadcast_to(gain_s[...], (LANES, channels)).T
            gain = jnp.concatenate([gain] * (block // LANES), axis=1)
            right_w, left_w = wr_s[...].T, wl_s[...].T
        normed = (centred * lax.rsqrt(variance + EPS) * gain).astype(jnp.bfloat16)
        mask = mask_of(cols, first_row, first_col, lens_s, res_s, at, block)
        lanes = pl.ds(at, block)
        normed_s[:, lanes] = normed
        right = edge_of(right_w, normed, mask, groups)
        left = edge_of(left_w, normed, mask, groups)
        begin, end = at // LANES, min((at + block) // LANES, whole)
        for t in range(begin, end):
            here = slice(t * LANES - at, (t + 1) * LANES - at)
            both_s[:, 2 * own * t:2 * own * t + own] = left[:, :, here].astype(jnp.bfloat16)
            both_s[:, 2 * own * t + own:2 * own * (t + 1)] = right[:, :, here].astype(jnp.bfloat16)
            right_s[:, own * t:own * (t + 1)] = right[:, :, here].astype(jnp.bfloat16)
        strip = STRIP if end == whole else 0
        if strip and over:
            here = slice(whole * LANES - at, (whole + 1) * LANES - at)
            for g in range(groups):
                pair = jnp.concatenate([left[g, :, here], right[g, :, here]], axis=0)
                both_s[g, 2 * own * whole:2 * own * whole + 8] = strip_of(pair, over).astype(jnp.bfloat16)
                right_s[g, own * whole:own * whole + 8] = strip_of(right[g, :, here], over).astype(jnp.bfloat16)
        both_rows = pl.ds(2 * own * begin, 2 * own * (end - begin) + strip)
        right_rows = pl.ds(own * begin, own * (end - begin) + strip)
        sent = []
        for u in range(groups):
            group = jnp.bitwise_xor(mine, u)
            sent.append((right_s.at[group, right_rows], right_refs[u].at[right_rows]))
            sent.append((both_s.at[group, both_rows], both_refs[u].at[both_rows]))
        sent.append((normed_s.at[:, lanes], normed_ref.at[:, lanes]))
        for m, (src, dst) in enumerate(sent):
            stores.append(pltpu.make_async_copy(src, dst, out_sems.at[n, m]))
            stores[-1].start()
    for copy in stores:
        copy.wait()


def make_edges(pair, lens, resolved, gain, w_left, w_right, groups, rows, cols):
    count, channels = pair.shape
    own = w_left.shape[1] // 2 // groups
    block = 1024
    flat = ceil_to(count, block)
    chunks = [(at, min(block, count - at)) for at in range(0, count, block)]
    here = pl.BlockSpec(memory_space=pltpu.HBM)
    return pl.pallas_call(
        functools.partial(edges_kernel, groups, rows, cols, chunks),
        in_specs=[here] * 6,
        out_specs=[here] * (1 + 2 * groups),
        out_shape=[jax.ShapeDtypeStruct((channels, flat), jnp.bfloat16)]
        + [jax.ShapeDtypeStruct((travel_rows(2 * own, rows, cols), LANES), jnp.bfloat16)] * groups
        + [jax.ShapeDtypeStruct((travel_rows(own, rows, cols), LANES), jnp.bfloat16)] * groups,
        scratch_shapes=[
            pltpu.VMEM((flat, channels), pair.dtype),
            pltpu.VMEM(gain.shape, gain.dtype),
            pltpu.VMEM(w_left.shape, w_left.dtype),
            pltpu.VMEM(w_right.shape, w_right.dtype),
            pltpu.SMEM(lens.shape, lens.dtype),
            pltpu.SMEM(resolved.shape, resolved.dtype),
            pltpu.VMEM((channels, flat), jnp.bfloat16),
            pltpu.VMEM((groups, travel_rows(2 * own, rows, cols), LANES), jnp.bfloat16),
            pltpu.VMEM((groups, travel_rows(own, rows, cols), LANES), jnp.bfloat16),
            pltpu.SemaphoreType.DMA((5 + len(chunks),)),
            pltpu.SemaphoreType.DMA((len(chunks), 1 + 2 * groups)),
        ],
        compiler_params=pltpu.CompilerParams(vmem_limit_bytes=VMEM_FIRST),
    )(pair, gain, w_left, w_right, lens, resolved)


def tiles_of(rows, cols):
    return divmod(rows * cols, LANES)


def travel_rows(ch, rows, cols):
    return tiles_of(rows, cols)[0] * ch + STRIP


def strip_of(tile, left):
    lane = lax.broadcasted_iota(jnp.int32, (8, LANES), 1)
    strip = jnp.zeros((8, LANES), jnp.float32)
    for g in range(tile.shape[0] // 8):
        piece = tile[8 * g:8 * g + 8]
        if g:
            piece = pltpu.roll(piece, g * left, 1)
        strip = jnp.where((lane >= g * left) & (lane < (g + 1) * left), piece, strip)
    return strip


def tile_at(ref, t, total, first, ch, rows, cols):
    whole, left = tiles_of(rows, cols)
    if t < whole:
        return ref[t * total + first:t * total + first + ch].astype(jnp.float32)
    strip = ref[whole * total:whole * total + 8].astype(jnp.float32)
    pieces = []
    for g in range(first // 8, (first + ch) // 8):
        pieces.append(pltpu.roll(strip, LANES - g * left, 1) if g else strip)
    return jnp.concatenate(pieces, axis=0)


def unpack(got_ref, held_refs, block, rows, cols, step):
    tiles = pl.cdiv(cols, LANES)
    total = (got_ref.shape[0] - STRIP) // tiles_of(rows, cols)[0]
    ch = total // len(held_refs)
    lane = lax.broadcasted_iota(jnp.int32, (ch, LANES), 1)
    for n, held in enumerate(held_refs):
        seen = {}

        def tile_of(t):
            if t not in seen:
                seen[t] = tile_at(got_ref, t, total, n * ch, ch, rows, cols)
            return seen[t]

        for i in range(rows):
            for tt in range(tiles):
                length = min(LANES, cols - LANES * tt)
                t0, off = divmod(cols * i + LANES * tt, LANES)
                piece = tile_of(t0)
                if off:
                    piece = pltpu.roll(piece, LANES - off, 1)
                if off + length > LANES:
                    piece = jnp.where(lane < LANES - off, piece, pltpu.roll(tile_of(t0 + 1), LANES - off, 1))
                if length < LANES and n == 0:
                    piece = jnp.where(lane < length, piece, 0.0)
                base = pl.multiple_of((block * rows + i) * step, 8)
                held[tt, pl.ds(base, ch), :] = piece


def packed_tile(held, first, t, block, rows, cols, step, ch):
    tiles = pl.cdiv(cols, LANES)
    lane = lax.broadcasted_iota(jnp.int32, (ch, LANES), 1)
    tile = None
    for i in range(rows):
        for tt in range(tiles):
            shift = cols * i + LANES * tt - LANES * t
            length = min(LANES, cols - LANES * tt)
            if shift >= LANES or shift + length <= 0:
                continue
            base = pl.multiple_of((block * rows + i) * step, 8)
            piece = held[first + tt, pl.ds(base, ch), :]
            if shift % LANES:
                piece = pltpu.roll(piece, shift % LANES, 1)
            tile = piece if tile is None else jnp.where(lane < shift, tile, piece)
    return jnp.zeros((ch, LANES), jnp.float32) if tile is None else tile


def channel_of(held, d, count, step):
    return jnp.concatenate([held[t, pl.ds(d, count, stride=step), :] for t in range(held.shape[0])], axis=1)


def lines_kernel(rows, cols, *refs):
    count = len(refs) // 2
    for got_ref, lines_ref in zip(refs[:count], refs[count:]):
        unpack(got_ref, (lines_ref,), 0, rows, cols, lines_ref.shape[1] // rows)


def products_kernel(groups, rows, cols, parts, early, late, *refs):
    lines_refs, near_refs, far_refs = refs[:len(early)], refs[len(early):][:groups], refs[len(early) + groups:][:len(late)]
    keep_refs, send_refs = refs[2 * groups:2 * groups + 2], refs[2 * groups + 2:2 * groups + 4]
    left_s, right_s, far_s, prod_s = refs[2 * groups + 4:]
    _, _, mine, own_half, col = place_of(groups, rows, cols)
    full, over = tiles_of(rows, cols)
    ch = (keep_refs[0].shape[1] - STRIP) // full
    step = left_s.shape[1] // (groups * rows)
    count = groups * rows
    tiles = left_s.shape[0]
    for u, lines_ref in zip(early, lines_refs):
        far_s[:, pl.ds(pl.multiple_of(jnp.bitwise_xor(mine, u) * rows * step, 8), rows * step), :] = lines_ref[...]
    for u in range(groups):
        unpack(near_refs[u], (left_s, right_s), jnp.bitwise_xor(mine, u), rows, cols, step)
    for u, far_ref in zip(late, far_refs):
        unpack(far_ref, (far_s,), jnp.bitwise_xor(mine, u), rows, cols, step)
    pad = [jnp.zeros((tiles * LANES - count, tiles * LANES), jnp.float32)] if count % LANES else []
    for d in range(ch):
        left = channel_of(left_s, d, count, step)
        right = jnp.concatenate(
            [channel_of(right_s, d, count, step)] + pad + [channel_of(far_s, d, count, step)] + pad, axis=0
        )
        prod = lax.dot_general(
            left.astype(jnp.bfloat16), right.astype(jnp.bfloat16), (((1,), (1,)), ((), ())),
            preferred_element_type=jnp.float32,
        )
        for t in range(2 * tiles):
            prod_s[t, pl.ds(d, count, stride=step), :] = prod[:, t * LANES:(t + 1) * LANES]
    near_kept = col == own_half
    for part, pieces in enumerate(parts):
        for n, u in enumerate(pieces):
            block = jnp.bitwise_xor(mine, u)
            for t in range(full + (over > 0)):
                near = packed_tile(prod_s, 0, t, block, rows, cols, step, ch)
                far = packed_tile(prod_s, tiles, t, block, rows, cols, step, ch)
                if t == full:
                    near, far = strip_of(near, over), strip_of(far, over)
                there = pl.ds(t * ch, near.shape[0])
                keep_refs[part][n, there] = jnp.where(near_kept, near, far).astype(jnp.bfloat16)
                send_refs[part][n, there] = jnp.where(near_kept, far, near).astype(jnp.bfloat16)


def lines_of(blocks, ch, cols):
    return (pl.cdiv(cols, LANES), blocks * line_step(ch), LANES)


def make_lines(got, rows, cols):
    ch = (got[0].shape[0] - STRIP) // tiles_of(rows, cols)[0]
    whole = pl.BlockSpec(memory_space=pltpu.VMEM)
    return pl.pallas_call(
        functools.partial(lines_kernel, rows, cols),
        in_specs=[whole] * len(got),
        out_specs=[whole] * len(got),
        out_shape=[jax.ShapeDtypeStruct(lines_of(rows, ch, cols), jnp.float32)] * len(got),
        compiler_params=pltpu.CompilerParams(vmem_limit_bytes=VMEM_LIMIT),
        cost_estimate=pl.CostEstimate(flops=10 ** 5, bytes_accessed=10 ** 8, transcendentals=0),
    )(*got)


def make_products(lines, near, far, parts, early, late, rows, cols):
    groups = len(near)
    ch = (near[0].shape[0] - STRIP) // tiles_of(rows, cols)[0] // 2
    whole = pl.BlockSpec(memory_space=pltpu.VMEM)
    tiles, held, _ = lines_of(groups * rows, ch, cols)
    one = pltpu.VMEM((tiles, held, LANES), jnp.float32)
    sizes = [len(pieces) for pieces in parts] * 2
    return pl.pallas_call(
        functools.partial(products_kernel, groups, rows, cols, parts, early, late),
        in_specs=[whole] * (2 * groups),
        out_specs=[whole] * 4,
        out_shape=[jax.ShapeDtypeStruct((n, travel_rows(ch, rows, cols), LANES), jnp.bfloat16) for n in sizes],
        scratch_shapes=[one, one, one, pltpu.VMEM((2 * tiles, held, LANES), jnp.float32)],
        compiler_params=pltpu.CompilerParams(vmem_limit_bytes=VMEM_LIMIT),
        cost_estimate=pl.CostEstimate(flops=10 ** 5, bytes_accessed=10 ** 7, transcendentals=0),
    )(*lines, *near, *far)


def add_kernel(a_ref, b_ref, *out_refs):
    for u, out_ref in enumerate(out_refs):
        out_ref[...] = (a_ref[u].astype(jnp.float32) + b_ref[u].astype(jnp.float32)).astype(out_ref.dtype)


def make_sums(a, b):
    groups, ch, flat = a.shape
    whole = pl.BlockSpec(memory_space=pltpu.VMEM)
    return pl.pallas_call(
        add_kernel,
        in_specs=[whole] * 2,
        out_specs=[whole] * groups,
        out_shape=[jax.ShapeDtypeStruct((ch, flat), a.dtype)] * groups,
        compiler_params=pltpu.CompilerParams(vmem_limit_bytes=VMEM_LIMIT),
        cost_estimate=pl.CostEstimate(flops=10 ** 5, bytes_accessed=10 ** 5, transcendentals=0),
    )(a, b)


def update_kernel(groups, rows, cols, chunks, gain_ref, w_ref, gate_ref, *refs):
    prod_refs = refs[:groups]
    out_ref, gain_s, w_s, out_s, sems = refs[groups:]
    mine = place_of(groups, rows, cols)[2]
    ch = w_ref.shape[0] // groups
    block = chunks[0][1]
    for u in range(groups):
        there = pl.ds(pl.multiple_of(jnp.bitwise_xor(mine, u) * ch, 8), ch)
        gain_s[u * ch:(u + 1) * ch] = gain_ref[there]
        w_s[u * ch:(u + 1) * ch] = w_ref[there]
    gain, weights = gain_s[...], w_s[...].astype(jnp.bfloat16)
    stores = []
    for n, (at, size) in enumerate(chunks):
        prod = jnp.concatenate(
            [
                jnp.concatenate([tile_at(ref, t, ch, 0, ch, rows, cols) for ref in prod_refs], axis=0)
                for t in range(at // LANES, pl.cdiv(at + size, LANES))
            ],
            axis=1,
        )
        mean = jnp.mean(prod, axis=0, keepdims=True)
        centred = prod - mean
        variance = jnp.mean(centred * centred, axis=0, keepdims=True)
        normed = (centred * lax.rsqrt(variance + EPS) * gain).astype(jnp.bfloat16)
        projected = lax.dot_general(normed, weights, (((0,), (0,)), ((), ())), preferred_element_type=jnp.float32)
        out_s[pl.ds(at, size)] = (gate_ref[pl.ds(at, size)] * projected[:size]).astype(out_s.dtype)
        stores.append(pltpu.make_async_copy(out_s.at[pl.ds(at, size)], out_ref.at[pl.ds(at, size)], sems.at[n]))
        stores[-1].start()
    for copy in stores:
        copy.wait()


def make_update(prods, gain, w_out, gate, rows, cols):
    groups = len(prods)
    count, channels = gate.shape
    block = 512
    chunks = [(at, min(block, count - at)) for at in range(0, count, block)]
    whole = pl.BlockSpec(memory_space=pltpu.VMEM)
    return pl.pallas_call(
        functools.partial(update_kernel, groups, rows, cols, chunks),
        in_specs=[whole] * (3 + groups),
        out_specs=pl.BlockSpec(memory_space=pltpu.HBM),
        out_shape=jax.ShapeDtypeStruct((count, channels), jnp.bfloat16),
        scratch_shapes=[
            pltpu.VMEM(gain.shape, jnp.float32),
            pltpu.VMEM(w_out.shape, jnp.float32),
            pltpu.VMEM((count, channels), jnp.bfloat16),
            pltpu.SemaphoreType.DMA((len(chunks),)),
        ],
        compiler_params=pltpu.CompilerParams(vmem_limit_bytes=VMEM_LIMIT),
    )(gain, w_out, gate, *prods)


def swap(value, shift):
    return lax.ppermute(value, "row", [(r, r ^ shift) for r in range(lax.axis_size("row"))])


def shards(pair_act, chain_lengths, resolved, in_gain, out_gain, w_left, w_right, w_gate, w_out):
    rows, cols, channels = pair_act.shape
    hidden = w_out.shape[0]
    groups = lax.axis_size("row") // 2
    normed, *edges = make_edges(
        pair_act.reshape(rows * cols, channels), chain_lengths, resolved,
        in_gain.reshape(1, channels), w_left, w_right, groups, rows, cols,
    )
    both, right = edges[:groups], edges[groups:]
    far_got = [swap(right[u], groups + u) for u in range(groups)]
    near_got = [both[0]] + [swap(both[u], u) for u in range(1, groups)]
    gate = jax.nn.sigmoid(
        jnp.einsum("cp,cd->pd", normed[:, :rows * cols], w_gate, preferred_element_type=jnp.float32)
    )
    half = groups // 2
    early, late = list(range(half, groups)) + [0], list(range(1, half))
    lines = make_lines([far_got[u] for u in early], rows, cols)
    parts = [list(range(1, half + 1)), [0] + list(range(half + 1, groups))]
    made = make_products(lines, near_got, [far_got[u] for u in late], parts, early, late, rows, cols)
    sums = {}
    for part, pieces in enumerate(parts):
        other = lax.ppermute(made[2 + part], "col", [(0, 1), (1, 0)])
        sums.update(zip(pieces, make_sums(made[part], other)))
    returned = [sums[0]] + [swap(sums[u], u) for u in range(1, groups)]
    update = make_update(returned, out_gain.reshape(hidden, 1), w_out.astype(jnp.float32), gate, rows, cols)
    return update.reshape(rows, cols, channels)


def solution(mesh):
    return jax.shard_map(
        shards,
        mesh=mesh,
        in_specs=(P(("grp", "row"), "col", None), P("grp"), P("grp"), P(), P(), P(), P(), P(), P()),
        out_specs=P(("grp", "row"), "col", None),
        check_vma=False,
    )
```

```python
import functools

import jax
import jax.numpy as jnp
from jax import lax
from jax.experimental import pallas as pl
from jax.experimental.pallas import tpu as pltpu
from jax.sharding import PartitionSpec as P

EPS = 1e-05
LANES = 128
VMEM_LIMIT = 32 * 1024 * 1024
STRIP = 16
VMEM_FIRST = 60 * 1024 * 1024


def ceil_to(n, m):
    return -(-n // m) * m


def line_step(ch):
    return (ceil_to(ch, 8) // 8 | 1) * 8


def place_of(groups, rows, cols):
    row, col = lax.axis_index("row"), lax.axis_index("col")
    return row * rows, col * cols, lax.rem(row, groups), row // groups, col


def sigmoid(x):
    return 0.5 + 0.5 * jnp.tanh(0.5 * x)


def mask_of(cols, first_row, first_col, lens_ref, res_ref, at, block):
    position = at + lax.broadcasted_iota(jnp.int32, (8, block), 1)
    i_here = jnp.floor((position.astype(jnp.float32) + 0.5) * (1.0 / cols)).astype(jnp.int32)
    i_at = first_row + i_here
    k_at = first_col + position - i_here * cols
    i_ok = jnp.zeros((8, block), jnp.float32)
    k_ok = jnp.zeros((8, block), jnp.float32)
    start = 0
    for q in range(lens_ref.shape[0]):
        length = lens_ref[q]
        stop = start + jnp.minimum(length, res_ref[q])
        i_ok = jnp.where((i_at >= start) & (i_at < stop), 1.0, i_ok)
        k_ok = jnp.where((k_at >= start) & (k_at < stop), 1.0, k_ok)
        start = start + length
    return i_ok * k_ok


def edge_of(weights, normed, mask, groups):
    hidden = weights.shape[0] // 2
    block = normed.shape[1]
    projected = jnp.dot(weights, normed, preferred_element_type=jnp.float32)
    edge = sigmoid(projected[:hidden]) * projected[hidden:]
    edge = edge.reshape(hidden // 8, 8, block) * mask[None]
    return edge.reshape(groups, hidden // groups, block)


def edges_kernel(groups, rows, cols, chunks, pair_ref, gain_ref, wl_ref, wr_ref, lens_ref, res_ref, normed_ref, *refs):
    both_refs, right_refs = refs[:groups], refs[groups:2 * groups]
    x_s, gain_s, wl_s, wr_s, lens_s, res_s, normed_s, both_s, right_s, in_sems, out_sems = refs[2 * groups:]
    count = rows * cols
    first_row, first_col, mine, _, _ = place_of(groups, rows, cols)
    own = wl_ref.shape[1] // 2 // groups
    loads = [
        pltpu.make_async_copy(src, dst, in_sems.at[n])
        for n, (src, dst) in enumerate(
            [(gain_ref, gain_s), (lens_ref, lens_s), (res_ref, res_s), (wr_ref, wr_s), (wl_ref, wl_s)]
        )
    ]
    pieces = [
        pltpu.make_async_copy(pair_ref.at[pl.ds(at, size)], x_s.at[pl.ds(at, size)], in_sems.at[len(loads) + n])
        for n, (at, size) in enumerate(chunks)
    ]
    for copy in pieces[:1] + loads + pieces[1:]:
        copy.start()
    block = chunks[0][1]
    whole, over = tiles_of(rows, cols)
    channels = x_s.shape[1]
    spare = x_s.shape[0] - count
    if spare:
        x_s[pl.ds(count, spare)] = jnp.zeros((spare, x_s.shape[1]), x_s.dtype)
    stores = []
    for n, (at, size) in enumerate(chunks):
        pieces[n].wait()
        x = x_s[pl.ds(at, block)].T.astype(jnp.float32)
        centred = x - jnp.mean(x, axis=0, keepdims=True)
        variance = jnp.mean(centred * centred, axis=0, keepdims=True)
        if n == 0:
            for copy in loads:
                copy.wait()
            gain = jnp.broadcast_to(gain_s[...], (LANES, channels)).T
            gain = jnp.concatenate([gain] * (block // LANES), axis=1)
            right_w, left_w = wr_s[...].T, wl_s[...].T
        normed = (centred * lax.rsqrt(variance + EPS) * gain).astype(jnp.bfloat16)
        mask = mask_of(cols, first_row, first_col, lens_s, res_s, at, block)
        lanes = pl.ds(at, block)
        normed_s[:, lanes] = normed
        right = edge_of(right_w, normed, mask, groups)
        left = edge_of(left_w, normed, mask, groups)
        begin, end = at // LANES, min((at + block) // LANES, whole)
        for t in range(begin, end):
            here = slice(t * LANES - at, (t + 1) * LANES - at)
            both_s[:, 2 * own * t:2 * own * t + own] = left[:, :, here].astype(jnp.bfloat16)
            both_s[:, 2 * own * t + own:2 * own * (t + 1)] = right[:, :, here].astype(jnp.bfloat16)
            right_s[:, own * t:own * (t + 1)] = right[:, :, here].astype(jnp.bfloat16)
        strip = STRIP if end == whole else 0
        if strip and over:
            here = slice(whole * LANES - at, (whole + 1) * LANES - at)
            for g in range(groups):
                pair = jnp.concatenate([left[g, :, here], right[g, :, here]], axis=0)
                both_s[g, 2 * own * whole:2 * own * whole + 8] = strip_of(pair, over).astype(jnp.bfloat16)
                right_s[g, own * whole:own * whole + 8] = strip_of(right[g, :, here], over).astype(jnp.bfloat16)
        both_rows = pl.ds(2 * own * begin, 2 * own * (end - begin) + strip)
        right_rows = pl.ds(own * begin, own * (end - begin) + strip)
        sent = []
        for u in range(groups):
            group = jnp.bitwise_xor(mine, u)
            sent.append((right_s.at[group, right_rows], right_refs[u].at[right_rows]))
            sent.append((both_s.at[group, both_rows], both_refs[u].at[both_rows]))
        sent.append((normed_s.at[:, lanes], normed_ref.at[:, lanes]))
        for m, (src, dst) in enumerate(sent):
            stores.append(pltpu.make_async_copy(src, dst, out_sems.at[n, m]))
            stores[-1].start()
    for copy in stores:
        copy.wait()


def make_edges(pair, lens, resolved, gain, w_left, w_right, groups, rows, cols):
    count, channels = pair.shape
    own = w_left.shape[1] // 2 // groups
    block = 1024
    flat = ceil_to(count, block)
    chunks = [(at, min(block, count - at)) for at in range(0, count, block)]
    here = pl.BlockSpec(memory_space=pltpu.HBM)
    return pl.pallas_call(
        functools.partial(edges_kernel, groups, rows, cols, chunks),
        in_specs=[here] * 6,
        out_specs=[here] * (1 + 2 * groups),
        out_shape=[jax.ShapeDtypeStruct((channels, flat), jnp.bfloat16)]
        + [jax.ShapeDtypeStruct((travel_rows(2 * own, rows, cols), LANES), jnp.bfloat16)] * groups
        + [jax.ShapeDtypeStruct((travel_rows(own, rows, cols), LANES), jnp.bfloat16)] * groups,
        scratch_shapes=[
            pltpu.VMEM((flat, channels), pair.dtype),
            pltpu.VMEM(gain.shape, gain.dtype),
            pltpu.VMEM(w_left.shape, w_left.dtype),
            pltpu.VMEM(w_right.shape, w_right.dtype),
            pltpu.SMEM(lens.shape, lens.dtype),
            pltpu.SMEM(resolved.shape, resolved.dtype),
            pltpu.VMEM((channels, flat), jnp.bfloat16),
            pltpu.VMEM((groups, travel_rows(2 * own, rows, cols), LANES), jnp.bfloat16),
            pltpu.VMEM((groups, travel_rows(own, rows, cols), LANES), jnp.bfloat16),
            pltpu.SemaphoreType.DMA((5 + len(chunks),)),
            pltpu.SemaphoreType.DMA((len(chunks), 1 + 2 * groups)),
        ],
        compiler_params=pltpu.CompilerParams(vmem_limit_bytes=VMEM_FIRST),
    )(pair, gain, w_left, w_right, lens, resolved)


def tiles_of(rows, cols):
    return divmod(rows * cols, LANES)


def travel_rows(ch, rows, cols):
    return tiles_of(rows, cols)[0] * ch + STRIP


def strip_of(tile, left):
    lane = lax.broadcasted_iota(jnp.int32, (8, LANES), 1)
    strip = jnp.zeros((8, LANES), jnp.float32)
    for g in range(tile.shape[0] // 8):
        piece = tile[8 * g:8 * g + 8]
        if g:
            piece = pltpu.roll(piece, g * left, 1)
        strip = jnp.where((lane >= g * left) & (lane < (g + 1) * left), piece, strip)
    return strip


def tile_at(ref, t, total, first, ch, rows, cols):
    whole, left = tiles_of(rows, cols)
    if t < whole:
        return ref[t * total + first:t * total + first + ch].astype(jnp.float32)
    strip = ref[whole * total:whole * total + 8].astype(jnp.float32)
    pieces = []
    for g in range(first // 8, (first + ch) // 8):
        pieces.append(pltpu.roll(strip, LANES - g * left, 1) if g else strip)
    return jnp.concatenate(pieces, axis=0)


def unpack(got_ref, held_refs, block, rows, cols, step):
    tiles = pl.cdiv(cols, LANES)
    total = (got_ref.shape[0] - STRIP) // tiles_of(rows, cols)[0]
    ch = total // len(held_refs)
    lane = lax.broadcasted_iota(jnp.int32, (ch, LANES), 1)
    for n, held in enumerate(held_refs):
        seen = {}

        def tile_of(t):
            if t not in seen:
                seen[t] = tile_at(got_ref, t, total, n * ch, ch, rows, cols)
            return seen[t]

        if tiles_of(rows, cols)[1]:
            tile_of(tiles_of(rows, cols)[0])
        for i in range(rows):
            for tt in range(tiles):
                length = min(LANES, cols - LANES * tt)
                t0, off = divmod(cols * i + LANES * tt, LANES)
                piece = tile_of(t0)
                if off:
                    piece = pltpu.roll(piece, LANES - off, 1)
                if off + length > LANES:
                    piece = jnp.where(lane < LANES - off, piece, pltpu.roll(tile_of(t0 + 1), LANES - off, 1))
                if length < LANES and n == 0:
                    piece = jnp.where(lane < length, piece, 0.0)
                base = pl.multiple_of((block * rows + i) * step, 8)
                held[tt, pl.ds(base, ch), :] = piece


def packed_tile(held, first, t, block, rows, cols, step, ch):
    tiles = pl.cdiv(cols, LANES)
    lane = lax.broadcasted_iota(jnp.int32, (ch, LANES), 1)
    tile = None
    for i in range(rows):
        for tt in range(tiles):
            shift = cols * i + LANES * tt - LANES * t
            length = min(LANES, cols - LANES * tt)
            if shift >= LANES or shift + length <= 0:
                continue
            base = pl.multiple_of((block * rows + i) * step, 8)
            piece = held[first + tt, pl.ds(base, ch), :]
            if shift % LANES:
                piece = pltpu.roll(piece, shift % LANES, 1)
            tile = piece if tile is None else jnp.where(lane < shift, tile, piece)
    return jnp.zeros((ch, LANES), jnp.float32) if tile is None else tile


def channel_of(held, d, count, step):
    return jnp.concatenate([held[t, pl.ds(d, count, stride=step), :] for t in range(held.shape[0])], axis=1)


def lines_kernel(rows, cols, *refs):
    count = len(refs) // 2
    for got_ref, lines_ref in zip(refs[:count], refs[count:]):
        unpack(got_ref, (lines_ref,), 0, rows, cols, lines_ref.shape[1] // rows)


def products_kernel(groups, rows, cols, parts, early, late, *refs):
    lines_refs, near_refs, far_refs = refs[:len(early)], refs[len(early):][:groups], refs[len(early) + groups:][:len(late)]
    keep_refs, send_refs = refs[2 * groups:2 * groups + 2], refs[2 * groups + 2:2 * groups + 4]
    left_s, right_s, far_s, prod_s = refs[2 * groups + 4:]
    _, _, mine, own_half, col = place_of(groups, rows, cols)
    full, over = tiles_of(rows, cols)
    ch = (keep_refs[0].shape[1] - STRIP) // full
    step = left_s.shape[1] // (groups * rows)
    count = groups * rows
    tiles = left_s.shape[0]
    for u, lines_ref in zip(early, lines_refs):
        far_s[:, pl.ds(pl.multiple_of(jnp.bitwise_xor(mine, u) * rows * step, 8), rows * step), :] = lines_ref[...]
    for u in range(groups):
        unpack(near_refs[u], (left_s, right_s), jnp.bitwise_xor(mine, u), rows, cols, step)
    for u, far_ref in zip(late, far_refs):
        unpack(far_ref, (far_s,), jnp.bitwise_xor(mine, u), rows, cols, step)
    pad = [jnp.zeros((tiles * LANES - count, tiles * LANES), jnp.float32)] if count % LANES else []
    for d in range(ch):
        left = channel_of(left_s, d, count, step)
        right = jnp.concatenate(
            [channel_of(right_s, d, count, step)] + pad + [channel_of(far_s, d, count, step)] + pad, axis=0
        )
        prod = lax.dot_general(
            left.astype(jnp.bfloat16), right.astype(jnp.bfloat16), (((1,), (1,)), ((), ())),
            preferred_element_type=jnp.float32,
        )
        for t in range(2 * tiles):
            prod_s[t, pl.ds(d, count, stride=step), :] = prod[:, t * LANES:(t + 1) * LANES]
    near_kept = col == own_half
    for part, pieces in enumerate(parts):
        for n, u in enumerate(pieces):
            block = jnp.bitwise_xor(mine, u)
            for t in ([full] if over else []) + list(range(full)):
                near = packed_tile(prod_s, 0, t, block, rows, cols, step, ch)
                far = packed_tile(prod_s, tiles, t, block, rows, cols, step, ch)
                if t == full:
                    near, far = strip_of(near, over), strip_of(far, over)
                there = pl.ds(t * ch, near.shape[0])
                keep_refs[part][n, there] = jnp.where(near_kept, near, far).astype(jnp.bfloat16)
                send_refs[part][n, there] = jnp.where(near_kept, far, near).astype(jnp.bfloat16)


def lines_of(blocks, ch, cols):
    return (pl.cdiv(cols, LANES), blocks * line_step(ch), LANES)


def make_lines(got, rows, cols):
    ch = (got[0].shape[0] - STRIP) // tiles_of(rows, cols)[0]
    whole = pl.BlockSpec(memory_space=pltpu.VMEM)
    return pl.pallas_call(
        functools.partial(lines_kernel, rows, cols),
        in_specs=[whole] * len(got),
        out_specs=[whole] * len(got),
        out_shape=[jax.ShapeDtypeStruct(lines_of(rows, ch, cols), jnp.float32)] * len(got),
        compiler_params=pltpu.CompilerParams(vmem_limit_bytes=VMEM_LIMIT),
        cost_estimate=pl.CostEstimate(flops=10 ** 5, bytes_accessed=10 ** 8, transcendentals=0),
    )(*got)


def make_products(lines, near, far, parts, early, late, rows, cols):
    groups = len(near)
    ch = (near[0].shape[0] - STRIP) // tiles_of(rows, cols)[0] // 2
    whole = pl.BlockSpec(memory_space=pltpu.VMEM)
    tiles, held, _ = lines_of(groups * rows, ch, cols)
    one = pltpu.VMEM((tiles, held, LANES), jnp.float32)
    sizes = [len(pieces) for pieces in parts] * 2
    return pl.pallas_call(
        functools.partial(products_kernel, groups, rows, cols, parts, early, late),
        in_specs=[whole] * (2 * groups),
        out_specs=[whole] * 4,
        out_shape=[jax.ShapeDtypeStruct((n, travel_rows(ch, rows, cols), LANES), jnp.bfloat16) for n in sizes],
        scratch_shapes=[one, one, one, pltpu.VMEM((2 * tiles, held, LANES), jnp.float32)],
        compiler_params=pltpu.CompilerParams(vmem_limit_bytes=VMEM_LIMIT),
        cost_estimate=pl.CostEstimate(flops=10 ** 5, bytes_accessed=10 ** 7, transcendentals=0),
    )(*lines, *near, *far)


def add_kernel(a_ref, b_ref, *out_refs):
    for u, out_ref in enumerate(out_refs):
        out_ref[...] = (a_ref[u].astype(jnp.float32) + b_ref[u].astype(jnp.float32)).astype(out_ref.dtype)


def make_sums(a, b):
    groups, ch, flat = a.shape
    whole = pl.BlockSpec(memory_space=pltpu.VMEM)
    return pl.pallas_call(
        add_kernel,
        in_specs=[whole] * 2,
        out_specs=[whole] * groups,
        out_shape=[jax.ShapeDtypeStruct((ch, flat), a.dtype)] * groups,
        compiler_params=pltpu.CompilerParams(vmem_limit_bytes=VMEM_LIMIT),
        cost_estimate=pl.CostEstimate(flops=10 ** 5, bytes_accessed=10 ** 5, transcendentals=0),
    )(a, b)


def update_kernel(groups, rows, cols, chunks, gain_ref, w_ref, gate_ref, *refs):
    prod_refs = refs[:groups]
    out_ref, gain_s, w_s, out_s, sems = refs[groups:]
    mine = place_of(groups, rows, cols)[2]
    ch = w_ref.shape[0] // groups
    block = chunks[0][1]
    for u in range(groups):
        there = pl.ds(pl.multiple_of(jnp.bitwise_xor(mine, u) * ch, 8), ch)
        gain_s[u * ch:(u + 1) * ch] = gain_ref[there]
        w_s[u * ch:(u + 1) * ch] = w_ref[there]
    gain, weights = gain_s[...], w_s[...].astype(jnp.bfloat16)
    stores = []
    for n, (at, size) in enumerate(chunks):
        prod = jnp.concatenate(
            [
                jnp.concatenate([tile_at(ref, t, ch, 0, ch, rows, cols) for ref in prod_refs], axis=0)
                for t in range(at // LANES, pl.cdiv(at + size, LANES))
            ],
            axis=1,
        )
        mean = jnp.mean(prod, axis=0, keepdims=True)
        centred = prod - mean
        variance = jnp.mean(centred * centred, axis=0, keepdims=True)
        normed = (centred * lax.rsqrt(variance + EPS) * gain).astype(jnp.bfloat16)
        projected = lax.dot_general(normed, weights, (((0,), (0,)), ((), ())), preferred_element_type=jnp.float32)
        out_s[pl.ds(at, size)] = (gate_ref[pl.ds(at, size)] * projected[:size]).astype(out_s.dtype)
        stores.append(pltpu.make_async_copy(out_s.at[pl.ds(at, size)], out_ref.at[pl.ds(at, size)], sems.at[n]))
        stores[-1].start()
    for copy in stores:
        copy.wait()


def make_update(prods, gain, w_out, gate, rows, cols):
    groups = len(prods)
    count, channels = gate.shape
    block = 512
    chunks = [(at, min(block, count - at)) for at in range(0, count, block)]
    whole = pl.BlockSpec(memory_space=pltpu.VMEM)
    return pl.pallas_call(
        functools.partial(update_kernel, groups, rows, cols, chunks),
        in_specs=[whole] * (3 + groups),
        out_specs=pl.BlockSpec(memory_space=pltpu.HBM),
        out_shape=jax.ShapeDtypeStruct((count, channels), jnp.bfloat16),
        scratch_shapes=[
            pltpu.VMEM(gain.shape, jnp.float32),
            pltpu.VMEM(w_out.shape, jnp.float32),
            pltpu.VMEM((count, channels), jnp.bfloat16),
            pltpu.SemaphoreType.DMA((len(chunks),)),
        ],
        compiler_params=pltpu.CompilerParams(vmem_limit_bytes=VMEM_LIMIT),
    )(gain, w_out, gate, *prods)


def swap(value, shift):
    return lax.ppermute(value, "row", [(r, r ^ shift) for r in range(lax.axis_size("row"))])


def shards(pair_act, chain_lengths, resolved, in_gain, out_gain, w_left, w_right, w_gate, w_out):
    rows, cols, channels = pair_act.shape
    hidden = w_out.shape[0]
    groups = lax.axis_size("row") // 2
    normed, *edges = make_edges(
        pair_act.reshape(rows * cols, channels), chain_lengths, resolved,
        in_gain.reshape(1, channels), w_left, w_right, groups, rows, cols,
    )
    both, right = edges[:groups], edges[groups:]
    far_got = [swap(right[u], groups + u) for u in range(groups)]
    near_got = [both[0]] + [swap(both[u], u) for u in range(1, groups)]
    gate = jax.nn.sigmoid(
        jnp.einsum("cp,cd->pd", normed[:, :rows * cols], w_gate, preferred_element_type=jnp.float32)
    )
    half = groups // 2
    early, late = list(range(half, groups)) + [0], list(range(1, half))
    lines = make_lines([far_got[u] for u in early], rows, cols)
    parts = [list(range(1, half + 1)), [0] + list(range(half + 1, groups))]
    made = make_products(lines, near_got, [far_got[u] for u in late], parts, early, late, rows, cols)
    sums = {}
    for part, pieces in enumerate(parts):
        other = lax.ppermute(made[2 + part], "col", [(0, 1), (1, 0)])
        sums.update(zip(pieces, make_sums(made[part], other)))
    returned = [sums[0]] + [swap(sums[u], u) for u in range(1, groups)]
    update = make_update(returned, out_gain.reshape(hidden, 1), w_out.astype(jnp.float32), gate, rows, cols)
    return update.reshape(rows, cols, channels)


def solution(mesh):
    return jax.shard_map(
        shards,
        mesh=mesh,
        in_specs=(P(("grp", "row"), "col", None), P("grp"), P("grp"), P(), P(), P(), P(), P(), P()),
        out_specs=P(("grp", "row"), "col", None),
        check_vma=False,
    )
```

```python
import functools

import jax
import jax.numpy as jnp
from jax import lax
from jax.experimental import pallas as pl
from jax.experimental.pallas import tpu as pltpu
from jax.sharding import PartitionSpec as P

EPS = 1e-05
LANES = 128
VMEM_LIMIT = 32 * 1024 * 1024
STRIP = 16
VMEM_FIRST = 60 * 1024 * 1024


def ceil_to(n, m):
    return -(-n // m) * m


def line_step(ch):
    return (ceil_to(ch, 8) // 8 | 1) * 8


def place_of(groups, rows, cols):
    row, col = lax.axis_index("row"), lax.axis_index("col")
    return row * rows, col * cols, lax.rem(row, groups), row // groups, col


def sigmoid(x):
    return 0.5 + 0.5 * jnp.tanh(0.5 * x)


def mask_of(cols, first_row, first_col, lens_ref, res_ref, at, block):
    position = at + lax.broadcasted_iota(jnp.int32, (8, block), 1)
    i_here = jnp.floor((position.astype(jnp.float32) + 0.5) * (1.0 / cols)).astype(jnp.int32)
    i_at = first_row + i_here
    k_at = first_col + position - i_here * cols
    i_ok = jnp.zeros((8, block), jnp.float32)
    k_ok = jnp.zeros((8, block), jnp.float32)
    start = 0
    for q in range(lens_ref.shape[0]):
        length = lens_ref[q]
        stop = start + jnp.minimum(length, res_ref[q])
        i_ok = jnp.where((i_at >= start) & (i_at < stop), 1.0, i_ok)
        k_ok = jnp.where((k_at >= start) & (k_at < stop), 1.0, k_ok)
        start = start + length
    return i_ok * k_ok


def edge_of(weights, normed, mask, groups):
    hidden = weights.shape[0] // 2
    block = normed.shape[1]
    projected = jnp.dot(weights, normed, preferred_element_type=jnp.float32)
    edge = sigmoid(projected[:hidden]) * projected[hidden:]
    edge = edge.reshape(hidden // 8, 8, block) * mask[None]
    return edge.reshape(groups, hidden // groups, block)


def edges_kernel(groups, rows, cols, chunks, pair_ref, gain_ref, wl_ref, wr_ref, lens_ref, res_ref, normed_ref, *refs):
    both_refs, right_refs = refs[:groups], refs[groups:2 * groups]
    x_s, gain_s, wl_s, wr_s, lens_s, res_s, normed_s, both_s, right_s, in_sems, out_sems = refs[2 * groups:]
    count = rows * cols
    first_row, first_col, mine, _, _ = place_of(groups, rows, cols)
    own = wl_ref.shape[1] // 2 // groups
    loads = [
        pltpu.make_async_copy(src, dst, in_sems.at[n])
        for n, (src, dst) in enumerate(
            [(gain_ref, gain_s), (lens_ref, lens_s), (res_ref, res_s), (wr_ref, wr_s), (wl_ref, wl_s)]
        )
    ]
    pieces = [
        pltpu.make_async_copy(pair_ref.at[pl.ds(at, size)], x_s.at[pl.ds(at, size)], in_sems.at[len(loads) + n])
        for n, (at, size) in enumerate(chunks)
    ]
    for copy in pieces[:1] + loads + pieces[1:]:
        copy.start()
    block = chunks[0][1]
    whole, over = tiles_of(rows, cols)
    channels = x_s.shape[1]
    spare = x_s.shape[0] - count
    if spare:
        x_s[pl.ds(count, spare)] = jnp.zeros((spare, x_s.shape[1]), x_s.dtype)
    stores = []
    for n, (at, size) in enumerate(chunks):
        pieces[n].wait()
        x = x_s[pl.ds(at, block)].T.astype(jnp.float32)
        centred = x - jnp.mean(x, axis=0, keepdims=True)
        variance = jnp.mean(centred * centred, axis=0, keepdims=True)
        if n == 0:
            for copy in loads:
                copy.wait()
            gain = jnp.broadcast_to(gain_s[...], (LANES, channels)).T
            gain = jnp.concatenate([gain] * (block // LANES), axis=1)
            right_w, left_w = wr_s[...].T, wl_s[...].T
        normed = (centred * lax.rsqrt(variance + EPS) * gain).astype(jnp.bfloat16)
        mask = mask_of(cols, first_row, first_col, lens_s, res_s, at, block)
        lanes = pl.ds(at, block)
        normed_s[:, lanes] = normed
        right = edge_of(right_w, normed, mask, groups)
        left = edge_of(left_w, normed, mask, groups)
        begin, end = at // LANES, min((at + block) // LANES, whole)
        for t in range(begin, end):
            here = slice(t * LANES - at, (t + 1) * LANES - at)
            both_s[:, 2 * own * t:2 * own * t + own] = left[:, :, here].astype(jnp.bfloat16)
            both_s[:, 2 * own * t + own:2 * own * (t + 1)] = right[:, :, here].astype(jnp.bfloat16)
            right_s[:, own * t:own * (t + 1)] = right[:, :, here].astype(jnp.bfloat16)
        strip = STRIP if end == whole else 0
        if strip and over:
            here = slice(whole * LANES - at, (whole + 1) * LANES - at)
            for g in range(groups):
                pair = jnp.concatenate([left[g, :, here], right[g, :, here]], axis=0)
                both_s[g, 2 * own * whole:2 * own * whole + 8] = strip_of(pair, over).astype(jnp.bfloat16)
                right_s[g, own * whole:own * whole + 8] = strip_of(right[g, :, here], over).astype(jnp.bfloat16)
        both_rows = pl.ds(2 * own * begin, 2 * own * (end - begin) + strip)
        right_rows = pl.ds(own * begin, own * (end - begin) + strip)
        sent = []
        for u in range(groups):
            group = jnp.bitwise_xor(mine, u)
            sent.append((right_s.at[group, right_rows], right_refs[u].at[right_rows]))
            sent.append((both_s.at[group, both_rows], both_refs[u].at[both_rows]))
        sent.append((normed_s.at[:, lanes], normed_ref.at[:, lanes]))
        for m, (src, dst) in enumerate(sent):
            stores.append(pltpu.make_async_copy(src, dst, out_sems.at[n, m]))
            stores[-1].start()
    for copy in stores:
        copy.wait()


def make_edges(pair, lens, resolved, gain, w_left, w_right, groups, rows, cols):
    count, channels = pair.shape
    own = w_left.shape[1] // 2 // groups
    block = 1024
    flat = ceil_to(count, block)
    chunks = [(at, min(block, count - at)) for at in range(0, count, block)]
    here = pl.BlockSpec(memory_space=pltpu.HBM)
    return pl.pallas_call(
        functools.partial(edges_kernel, groups, rows, cols, chunks),
        in_specs=[here] * 6,
        out_specs=[here] * (1 + 2 * groups),
        out_shape=[jax.ShapeDtypeStruct((channels, flat), jnp.bfloat16)]
        + [jax.ShapeDtypeStruct((travel_rows(2 * own, rows, cols), LANES), jnp.bfloat16)] * groups
        + [jax.ShapeDtypeStruct((travel_rows(own, rows, cols), LANES), jnp.bfloat16)] * groups,
        scratch_shapes=[
            pltpu.VMEM((flat, channels), pair.dtype),
            pltpu.VMEM(gain.shape, gain.dtype),
            pltpu.VMEM(w_left.shape, w_left.dtype),
            pltpu.VMEM(w_right.shape, w_right.dtype),
            pltpu.SMEM(lens.shape, lens.dtype),
            pltpu.SMEM(resolved.shape, resolved.dtype),
            pltpu.VMEM((channels, flat), jnp.bfloat16),
            pltpu.VMEM((groups, travel_rows(2 * own, rows, cols), LANES), jnp.bfloat16),
            pltpu.VMEM((groups, travel_rows(own, rows, cols), LANES), jnp.bfloat16),
            pltpu.SemaphoreType.DMA((5 + len(chunks),)),
            pltpu.SemaphoreType.DMA((len(chunks), 1 + 2 * groups)),
        ],
        compiler_params=pltpu.CompilerParams(vmem_limit_bytes=VMEM_FIRST),
    )(pair, gain, w_left, w_right, lens, resolved)


def tiles_of(rows, cols):
    return divmod(rows * cols, LANES)


def travel_rows(ch, rows, cols):
    return tiles_of(rows, cols)[0] * ch + STRIP


def strip_of(tile, left):
    lane = lax.broadcasted_iota(jnp.int32, (8, LANES), 1)
    strip = jnp.zeros((8, LANES), jnp.float32)
    for g in range(tile.shape[0] // 8):
        piece = tile[8 * g:8 * g + 8]
        if g:
            piece = pltpu.roll(piece, g * left, 1)
        strip = jnp.where((lane >= g * left) & (lane < (g + 1) * left), piece, strip)
    return strip


def tile_at(ref, t, total, first, ch, rows, cols):
    whole, left = tiles_of(rows, cols)
    if t < whole:
        return ref[t * total + first:t * total + first + ch].astype(jnp.float32)
    strip = ref[whole * total:whole * total + 8].astype(jnp.float32)
    pieces = []
    for g in range(first // 8, (first + ch) // 8):
        pieces.append(pltpu.roll(strip, LANES - g * left, 1) if g else strip)
    return jnp.concatenate(pieces, axis=0)


def unpack(got_ref, held_refs, block, rows, cols, step):
    tiles = pl.cdiv(cols, LANES)
    total = (got_ref.shape[0] - STRIP) // tiles_of(rows, cols)[0]
    ch = total // len(held_refs)
    lane = lax.broadcasted_iota(jnp.int32, (ch, LANES), 1)
    for n, held in enumerate(held_refs):
        seen = {}

        def tile_of(t):
            if t not in seen:
                seen[t] = tile_at(got_ref, t, total, n * ch, ch, rows, cols)
            return seen[t]

        if tiles_of(rows, cols)[1]:
            tile_of(tiles_of(rows, cols)[0])
        for i in range(rows):
            for tt in range(tiles):
                length = min(LANES, cols - LANES * tt)
                t0, off = divmod(cols * i + LANES * tt, LANES)
                piece = tile_of(t0)
                if off:
                    piece = pltpu.roll(piece, LANES - off, 1)
                if off + length > LANES:
                    piece = jnp.where(lane < LANES - off, piece, pltpu.roll(tile_of(t0 + 1), LANES - off, 1))
                if length < LANES and n == 0:
                    piece = jnp.where(lane < length, piece, 0.0)
                base = pl.multiple_of((block * rows + i) * step, 8)
                held[tt, pl.ds(base, ch), :] = piece


def packed_tile(held, first, t, block, rows, cols, step, ch):
    tiles = pl.cdiv(cols, LANES)
    lane = lax.broadcasted_iota(jnp.int32, (ch, LANES), 1)
    tile = None
    for i in range(rows):
        for tt in range(tiles):
            shift = cols * i + LANES * tt - LANES * t
            length = min(LANES, cols - LANES * tt)
            if shift >= LANES or shift + length <= 0:
                continue
            base = pl.multiple_of((block * rows + i) * step, 8)
            piece = held[first + tt, pl.ds(base, ch), :]
            if shift % LANES:
                piece = pltpu.roll(piece, shift % LANES, 1)
            tile = piece if tile is None else jnp.where(lane < shift, tile, piece)
    return jnp.zeros((ch, LANES), jnp.float32) if tile is None else tile


def channel_of(held, d, count, step):
    return jnp.concatenate([held[t, pl.ds(d, count, stride=step), :] for t in range(held.shape[0])], axis=1)


def lines_kernel(rows, cols, *refs):
    count = len(refs) // 2
    for got_ref, lines_ref in zip(refs[:count], refs[count:]):
        unpack(got_ref, (lines_ref,), 0, rows, cols, lines_ref.shape[1] // rows)


def products_kernel(groups, rows, cols, parts, early, late, *refs):
    lines_refs, near_refs, far_refs = refs[:len(early)], refs[len(early):][:groups], refs[len(early) + groups:][:len(late)]
    keep_refs, send_refs = refs[2 * groups:2 * groups + 2], refs[2 * groups + 2:2 * groups + 4]
    left_s, right_s, far_s, prod_s = refs[2 * groups + 4:]
    _, _, mine, own_half, col = place_of(groups, rows, cols)
    full, over = tiles_of(rows, cols)
    ch = (keep_refs[0].shape[1] - STRIP) // full
    step = left_s.shape[1] // (groups * rows)
    count = groups * rows
    tiles = left_s.shape[0]
    for u, lines_ref in zip(early, lines_refs):
        far_s[:, pl.ds(pl.multiple_of(jnp.bitwise_xor(mine, u) * rows * step, 8), rows * step), :] = lines_ref[...]
    for u in range(groups):
        unpack(near_refs[(groups - u) % groups], (left_s, right_s), jnp.bitwise_xor(mine, u), rows, cols, step)
    for u, far_ref in zip(late, far_refs):
        unpack(far_ref, (far_s,), jnp.bitwise_xor(mine, u), rows, cols, step)
    pad = [jnp.zeros((tiles * LANES - count, tiles * LANES), jnp.float32)] if count % LANES else []
    for d in range(ch):
        left = channel_of(left_s, d, count, step)
        right = jnp.concatenate(
            [channel_of(right_s, d, count, step)] + pad + [channel_of(far_s, d, count, step)] + pad, axis=0
        )
        prod = lax.dot_general(
            left.astype(jnp.bfloat16), right.astype(jnp.bfloat16), (((1,), (1,)), ((), ())),
            preferred_element_type=jnp.float32,
        )
        for t in range(2 * tiles):
            prod_s[t, pl.ds(d, count, stride=step), :] = prod[:, t * LANES:(t + 1) * LANES]
    near_kept = col == own_half
    for part, pieces in enumerate(parts):
        for n, u in enumerate(pieces):
            block = jnp.bitwise_xor(mine, u)
            for t in ([full] if over else []) + list(range(full)):
                near = packed_tile(prod_s, 0, t, block, rows, cols, step, ch)
                far = packed_tile(prod_s, tiles, t, block, rows, cols, step, ch)
                if t == full:
                    near, far = strip_of(near, over), strip_of(far, over)
                there = pl.ds(t * ch, near.shape[0])
                keep_refs[part][n, there] = jnp.where(near_kept, near, far).astype(jnp.bfloat16)
                send_refs[part][n, there] = jnp.where(near_kept, far, near).astype(jnp.bfloat16)


def lines_of(blocks, ch, cols):
    return (pl.cdiv(cols, LANES), blocks * line_step(ch), LANES)


def make_lines(got, rows, cols):
    ch = (got[0].shape[0] - STRIP) // tiles_of(rows, cols)[0]
    whole = pl.BlockSpec(memory_space=pltpu.VMEM)
    return pl.pallas_call(
        functools.partial(lines_kernel, rows, cols),
        in_specs=[whole] * len(got),
        out_specs=[whole] * len(got),
        out_shape=[jax.ShapeDtypeStruct(lines_of(rows, ch, cols), jnp.float32)] * len(got),
        compiler_params=pltpu.CompilerParams(vmem_limit_bytes=VMEM_LIMIT),
        cost_estimate=pl.CostEstimate(flops=10 ** 5, bytes_accessed=10 ** 8, transcendentals=0),
    )(*got)


def make_products(lines, near, far, parts, early, late, rows, cols):
    groups = len(near)
    ch = (near[0].shape[0] - STRIP) // tiles_of(rows, cols)[0] // 2
    whole = pl.BlockSpec(memory_space=pltpu.VMEM)
    tiles, held, _ = lines_of(groups * rows, ch, cols)
    one = pltpu.VMEM((tiles, held, LANES), jnp.float32)
    sizes = [len(pieces) for pieces in parts] * 2
    return pl.pallas_call(
        functools.partial(products_kernel, groups, rows, cols, parts, early, late),
        in_specs=[whole] * (2 * groups),
        out_specs=[whole] * 4,
        out_shape=[jax.ShapeDtypeStruct((n, travel_rows(ch, rows, cols), LANES), jnp.bfloat16) for n in sizes],
        scratch_shapes=[one, one, one, pltpu.VMEM((2 * tiles, held, LANES), jnp.float32)],
        compiler_params=pltpu.CompilerParams(vmem_limit_bytes=VMEM_LIMIT),
        cost_estimate=pl.CostEstimate(flops=10 ** 5, bytes_accessed=10 ** 7, transcendentals=0),
    )(*lines, *near[:1], *near[:0:-1], *far)


def add_kernel(a_ref, b_ref, *out_refs):
    for u, out_ref in enumerate(out_refs):
        out_ref[...] = (a_ref[u].astype(jnp.float32) + b_ref[u].astype(jnp.float32)).astype(out_ref.dtype)


def make_sums(a, b):
    groups, ch, flat = a.shape
    whole = pl.BlockSpec(memory_space=pltpu.VMEM)
    return pl.pallas_call(
        add_kernel,
        in_specs=[whole] * 2,
        out_specs=[whole] * groups,
        out_shape=[jax.ShapeDtypeStruct((ch, flat), a.dtype)] * groups,
        compiler_params=pltpu.CompilerParams(vmem_limit_bytes=VMEM_LIMIT),
        cost_estimate=pl.CostEstimate(flops=10 ** 5, bytes_accessed=10 ** 5, transcendentals=0),
    )(a, b)


def update_kernel(groups, rows, cols, chunks, gain_ref, w_ref, gate_ref, *refs):
    prod_refs = refs[:groups]
    out_ref, gain_s, w_s, out_s, sems = refs[groups:]
    mine = place_of(groups, rows, cols)[2]
    ch = w_ref.shape[0] // groups
    block = chunks[0][1]
    for u in range(groups):
        there = pl.ds(pl.multiple_of(jnp.bitwise_xor(mine, u) * ch, 8), ch)
        gain_s[u * ch:(u + 1) * ch] = gain_ref[there]
        w_s[u * ch:(u + 1) * ch] = w_ref[there]
    gain, weights = gain_s[...], w_s[...].astype(jnp.bfloat16)
    stores = []
    for n, (at, size) in enumerate(chunks):
        prod = jnp.concatenate(
            [
                jnp.concatenate([tile_at(ref, t, ch, 0, ch, rows, cols) for ref in prod_refs], axis=0)
                for t in range(at // LANES, pl.cdiv(at + size, LANES))
            ],
            axis=1,
        )
        mean = jnp.mean(prod, axis=0, keepdims=True)
        centred = prod - mean
        variance = jnp.mean(centred * centred, axis=0, keepdims=True)
        normed = (centred * lax.rsqrt(variance + EPS) * gain).astype(jnp.bfloat16)
        projected = lax.dot_general(normed, weights, (((0,), (0,)), ((), ())), preferred_element_type=jnp.float32)
        out_s[pl.ds(at, size)] = (gate_ref[pl.ds(at, size)] * projected[:size]).astype(out_s.dtype)
        stores.append(pltpu.make_async_copy(out_s.at[pl.ds(at, size)], out_ref.at[pl.ds(at, size)], sems.at[n]))
        stores[-1].start()
    for copy in stores:
        copy.wait()


def make_update(prods, gain, w_out, gate, rows, cols):
    groups = len(prods)
    count, channels = gate.shape
    block = 1024
    chunks = [(at, min(block, count - at)) for at in range(0, count, block)]
    whole = pl.BlockSpec(memory_space=pltpu.VMEM)
    return pl.pallas_call(
        functools.partial(update_kernel, groups, rows, cols, chunks),
        in_specs=[whole] * (3 + groups),
        out_specs=pl.BlockSpec(memory_space=pltpu.HBM),
        out_shape=jax.ShapeDtypeStruct((count, channels), jnp.bfloat16),
        scratch_shapes=[
            pltpu.VMEM(gain.shape, jnp.float32),
            pltpu.VMEM(w_out.shape, jnp.float32),
            pltpu.VMEM((count, channels), jnp.bfloat16),
            pltpu.SemaphoreType.DMA((len(chunks),)),
        ],
        compiler_params=pltpu.CompilerParams(vmem_limit_bytes=VMEM_LIMIT),
    )(gain, w_out, gate, *prods)


def swap(value, shift):
    return lax.ppermute(value, "row", [(r, r ^ shift) for r in range(lax.axis_size("row"))])


def shards(pair_act, chain_lengths, resolved, in_gain, out_gain, w_left, w_right, w_gate, w_out):
    rows, cols, channels = pair_act.shape
    hidden = w_out.shape[0]
    groups = lax.axis_size("row") // 2
    normed, *edges = make_edges(
        pair_act.reshape(rows * cols, channels), chain_lengths, resolved,
        in_gain.reshape(1, channels), w_left, w_right, groups, rows, cols,
    )
    both, right = edges[:groups], edges[groups:]
    far_got = [swap(right[u], groups + u) for u in range(groups)]
    near_got = [both[0]] + [swap(both[u], u) for u in range(1, groups)]
    gate = jax.nn.sigmoid(
        jnp.einsum("cp,cd->pd", normed[:, :rows * cols], w_gate, preferred_element_type=jnp.float32)
    )
    half = groups // 2
    early, late = list(range(half, groups)) + [0], list(range(1, half))
    lines = make_lines([far_got[u] for u in early], rows, cols)
    parts = [list(range(1, half + 1)), [0] + list(range(half + 1, groups))]
    made = make_products(lines, near_got, [far_got[u] for u in late], parts, early, late, rows, cols)
    sums = {}
    for part, pieces in enumerate(parts):
        other = lax.ppermute(made[2 + part], "col", [(0, 1), (1, 0)])
        sums.update(zip(pieces, make_sums(made[part], other)))
    returned = [sums[0]] + [swap(sums[u], u) for u in range(1, groups)]
    update = make_update(returned, out_gain.reshape(hidden, 1), w_out.astype(jnp.float32), gate, rows, cols)
    return update.reshape(rows, cols, channels)


def solution(mesh):
    return jax.shard_map(
        shards,
        mesh=mesh,
        in_specs=(P(("grp", "row"), "col", None), P("grp"), P("grp"), P(), P(), P(), P(), P(), P()),
        out_specs=P(("grp", "row"), "col", None),
        check_vma=False,
    )
```

```python
import functools

import jax
import jax.numpy as jnp
from jax import lax
from jax.experimental import pallas as pl
from jax.experimental.pallas import tpu as pltpu
from jax.sharding import PartitionSpec as P

EPS = 1e-05
LANES = 128
VMEM_LIMIT = 32 * 1024 * 1024
STRIP = 16
VMEM_FIRST = 60 * 1024 * 1024


def ceil_to(n, m):
    return -(-n // m) * m


def line_step(ch):
    return (ceil_to(ch, 8) // 8 | 1) * 8


def place_of(groups, rows, cols):
    row, col = lax.axis_index("row"), lax.axis_index("col")
    return row * rows, col * cols, lax.rem(row, groups), row // groups, col


def sigmoid(x):
    return 0.5 + 0.5 * jnp.tanh(0.5 * x)


def mask_of(cols, first_row, first_col, lens_ref, res_ref, at, block):
    position = at + lax.broadcasted_iota(jnp.int32, (8, block), 1)
    i_here = jnp.floor((position.astype(jnp.float32) + 0.5) * (1.0 / cols)).astype(jnp.int32)
    i_at = first_row + i_here
    k_at = first_col + position - i_here * cols
    i_ok = jnp.zeros((8, block), jnp.float32)
    k_ok = jnp.zeros((8, block), jnp.float32)
    start = 0
    for q in range(lens_ref.shape[0]):
        length = lens_ref[q]
        stop = start + jnp.minimum(length, res_ref[q])
        i_ok = jnp.where((i_at >= start) & (i_at < stop), 1.0, i_ok)
        k_ok = jnp.where((k_at >= start) & (k_at < stop), 1.0, k_ok)
        start = start + length
    return i_ok * k_ok


def edge_of(weights, normed, mask, groups):
    hidden = weights.shape[0] // 2
    block = normed.shape[1]
    projected = jnp.dot(weights, normed, preferred_element_type=jnp.float32)
    edge = sigmoid(projected[:hidden]) * projected[hidden:]
    edge = edge.reshape(hidden // 8, 8, block) * mask[None]
    return edge.reshape(groups, hidden // groups, block)


def edges_kernel(groups, rows, cols, chunks, pair_ref, gain_ref, wl_ref, wr_ref, lens_ref, res_ref, normed_ref, *refs):
    both_refs, right_refs = refs[:groups], refs[groups:2 * groups]
    x_s, gain_s, wl_s, wr_s, lens_s, res_s, normed_s, both_s, right_s, in_sems, out_sems = refs[2 * groups:]
    count = rows * cols
    first_row, first_col, mine, _, _ = place_of(groups, rows, cols)
    own = wl_ref.shape[1] // 2 // groups
    loads = [
        pltpu.make_async_copy(src, dst, in_sems.at[n])
        for n, (src, dst) in enumerate(
            [(gain_ref, gain_s), (lens_ref, lens_s), (res_ref, res_s), (wr_ref, wr_s), (wl_ref, wl_s)]
        )
    ]
    pieces = [
        pltpu.make_async_copy(pair_ref.at[pl.ds(at, size)], x_s.at[pl.ds(at, size)], in_sems.at[len(loads) + n])
        for n, (at, size) in enumerate(chunks)
    ]
    for copy in pieces[:1] + loads + pieces[1:]:
        copy.start()
    block = chunks[0][1]
    whole, over = tiles_of(rows, cols)
    channels = x_s.shape[1]
    spare = x_s.shape[0] - count
    if spare:
        x_s[pl.ds(count, spare)] = jnp.zeros((spare, x_s.shape[1]), x_s.dtype)
    stores = []
    for n, (at, size) in enumerate(chunks):
        pieces[n].wait()
        x = x_s[pl.ds(at, block)].T.astype(jnp.float32)
        centred = x - jnp.mean(x, axis=0, keepdims=True)
        variance = jnp.mean(centred * centred, axis=0, keepdims=True)
        if n == 0:
            for copy in loads:
                copy.wait()
            gain = jnp.broadcast_to(gain_s[...], (LANES, channels)).T
            gain = jnp.concatenate([gain] * (block // LANES), axis=1)
            right_w, left_w = wr_s[...].T, wl_s[...].T
        normed = (centred * lax.rsqrt(variance + EPS) * gain).astype(jnp.bfloat16)
        mask = mask_of(cols, first_row, first_col, lens_s, res_s, at, block)
        lanes = pl.ds(at, block)
        normed_s[:, lanes] = normed
        right = edge_of(right_w, normed, mask, groups)
        left = edge_of(left_w, normed, mask, groups)
        begin, end = at // LANES, min((at + block) // LANES, whole)
        for t in range(begin, end):
            here = slice(t * LANES - at, (t + 1) * LANES - at)
            both_s[:, 2 * own * t:2 * own * t + own] = left[:, :, here].astype(jnp.bfloat16)
            both_s[:, 2 * own * t + own:2 * own * (t + 1)] = right[:, :, here].astype(jnp.bfloat16)
            right_s[:, own * t:own * (t + 1)] = right[:, :, here].astype(jnp.bfloat16)
        strip = STRIP if end == whole else 0
        if strip and over:
            here = slice(whole * LANES - at, (whole + 1) * LANES - at)
            for g in range(groups):
                pair = jnp.concatenate([left[g, :, here], right[g, :, here]], axis=0)
                both_s[g, 2 * own * whole:2 * own * whole + 8] = strip_of(pair, over).astype(jnp.bfloat16)
                right_s[g, own * whole:own * whole + 8] = strip_of(right[g, :, here], over).astype(jnp.bfloat16)
        both_rows = pl.ds(2 * own * begin, 2 * own * (end - begin) + strip)
        right_rows = pl.ds(own * begin, own * (end - begin) + strip)
        sent = []
        for u in range(groups):
            group = jnp.bitwise_xor(mine, u)
            sent.append((right_s.at[group, right_rows], right_refs[u].at[right_rows]))
            sent.append((both_s.at[group, both_rows], both_refs[u].at[both_rows]))
        sent.append((normed_s.at[:, lanes], normed_ref.at[:, lanes]))
        for m, (src, dst) in enumerate(sent):
            stores.append(pltpu.make_async_copy(src, dst, out_sems.at[n, m]))
            stores[-1].start()
    for copy in stores:
        copy.wait()


def make_edges(pair, lens, resolved, gain, w_left, w_right, groups, rows, cols):
    count, channels = pair.shape
    own = w_left.shape[1] // 2 // groups
    block = 1024
    flat = ceil_to(count, block)
    chunks = [(at, min(block, count - at)) for at in range(0, count, block)]
    here = pl.BlockSpec(memory_space=pltpu.HBM)
    return pl.pallas_call(
        functools.partial(edges_kernel, groups, rows, cols, chunks),
        in_specs=[here] * 6,
        out_specs=[here] * (1 + 2 * groups),
        out_shape=[jax.ShapeDtypeStruct((channels, flat), jnp.bfloat16)]
        + [jax.ShapeDtypeStruct((travel_rows(2 * own, rows, cols), LANES), jnp.bfloat16)] * groups
        + [jax.ShapeDtypeStruct((travel_rows(own, rows, cols), LANES), jnp.bfloat16)] * groups,
        scratch_shapes=[
            pltpu.VMEM((flat, channels), pair.dtype),
            pltpu.VMEM(gain.shape, gain.dtype),
            pltpu.VMEM(w_left.shape, w_left.dtype),
            pltpu.VMEM(w_right.shape, w_right.dtype),
            pltpu.SMEM(lens.shape, lens.dtype),
            pltpu.SMEM(resolved.shape, resolved.dtype),
            pltpu.VMEM((channels, flat), jnp.bfloat16),
            pltpu.VMEM((groups, travel_rows(2 * own, rows, cols), LANES), jnp.bfloat16),
            pltpu.VMEM((groups, travel_rows(own, rows, cols), LANES), jnp.bfloat16),
            pltpu.SemaphoreType.DMA((5 + len(chunks),)),
            pltpu.SemaphoreType.DMA((len(chunks), 1 + 2 * groups)),
        ],
        compiler_params=pltpu.CompilerParams(vmem_limit_bytes=VMEM_FIRST),
    )(pair, gain, w_left, w_right, lens, resolved)


def tiles_of(rows, cols):
    return divmod(rows * cols, LANES)


def travel_rows(ch, rows, cols):
    return tiles_of(rows, cols)[0] * ch + STRIP


def strip_of(tile, left):
    lane = lax.broadcasted_iota(jnp.int32, (8, LANES), 1)
    strip = jnp.zeros((8, LANES), jnp.float32)
    for g in range(tile.shape[0] // 8):
        piece = tile[8 * g:8 * g + 8]
        if g:
            piece = pltpu.roll(piece, g * left, 1)
        strip = jnp.where((lane >= g * left) & (lane < (g + 1) * left), piece, strip)
    return strip


def tile_at(ref, t, total, first, ch, rows, cols):
    whole, left = tiles_of(rows, cols)
    if t < whole:
        return ref[t * total + first:t * total + first + ch].astype(jnp.float32)
    strip = ref[whole * total:whole * total + 8].astype(jnp.float32)
    pieces = []
    for g in range(first // 8, (first + ch) // 8):
        pieces.append(pltpu.roll(strip, LANES - g * left, 1) if g else strip)
    return jnp.concatenate(pieces, axis=0)


def unpack(got_ref, held_refs, block, rows, cols, step):
    tiles = pl.cdiv(cols, LANES)
    total = (got_ref.shape[0] - STRIP) // tiles_of(rows, cols)[0]
    ch = total // len(held_refs)
    lane = lax.broadcasted_iota(jnp.int32, (ch, LANES), 1)
    for n, held in enumerate(held_refs):
        seen = {}

        def tile_of(t):
            if t not in seen:
                seen[t] = tile_at(got_ref, t, total, n * ch, ch, rows, cols)
            return seen[t]

        if tiles_of(rows, cols)[1]:
            tile_of(tiles_of(rows, cols)[0])
        for i in range(rows):
            for tt in range(tiles):
                length = min(LANES, cols - LANES * tt)
                t0, off = divmod(cols * i + LANES * tt, LANES)
                piece = tile_of(t0)
                if off:
                    piece = pltpu.roll(piece, LANES - off, 1)
                if off + length > LANES:
                    piece = jnp.where(lane < LANES - off, piece, pltpu.roll(tile_of(t0 + 1), LANES - off, 1))
                if length < LANES and n == 0:
                    piece = jnp.where(lane < length, piece, 0.0)
                base = pl.multiple_of((block * rows + i) * step, 8)
                held[tt, pl.ds(base, ch), :] = piece


def packed_tile(held, first, t, block, rows, cols, step, ch):
    tiles = pl.cdiv(cols, LANES)
    lane = lax.broadcasted_iota(jnp.int32, (ch, LANES), 1)
    tile = None
    for i in range(rows):
        for tt in range(tiles):
            shift = cols * i + LANES * tt - LANES * t
            length = min(LANES, cols - LANES * tt)
            if shift >= LANES or shift + length <= 0:
                continue
            base = pl.multiple_of((block * rows + i) * step, 8)
            piece = held[first + tt, pl.ds(base, ch), :]
            if shift % LANES:
                piece = pltpu.roll(piece, shift % LANES, 1)
            tile = piece if tile is None else jnp.where(lane < shift, tile, piece)
    return jnp.zeros((ch, LANES), jnp.float32) if tile is None else tile


def channel_of(held, d, count, step):
    return jnp.concatenate([held[t, pl.ds(d, count, stride=step), :] for t in range(held.shape[0])], axis=1)


def lines_kernel(rows, cols, *refs):
    count = len(refs) // 2
    for got_ref, lines_ref in zip(refs[:count], refs[count:]):
        unpack(got_ref, (lines_ref,), 0, rows, cols, lines_ref.shape[1] // rows)


def products_kernel(groups, rows, cols, parts, early, late, *refs):
    lines_refs, near_refs, far_refs = refs[:len(early)], refs[len(early):][:groups], refs[len(early) + groups:][:len(late)]
    keep_refs, send_refs = refs[2 * groups:2 * groups + 2], refs[2 * groups + 2:2 * groups + 4]
    left_s, right_s, far_s, prod_s = refs[2 * groups + 4:]
    _, _, mine, own_half, col = place_of(groups, rows, cols)
    full, over = tiles_of(rows, cols)
    ch = (keep_refs[0].shape[1] - STRIP) // full
    step = left_s.shape[1] // (groups * rows)
    count = groups * rows
    tiles = left_s.shape[0]
    for u, lines_ref in zip(early, lines_refs):
        far_s[:, pl.ds(pl.multiple_of(jnp.bitwise_xor(mine, u) * rows * step, 8), rows * step), :] = lines_ref[...]
    for u in range(groups):
        unpack(near_refs[u], (left_s, right_s), jnp.bitwise_xor(mine, u), rows, cols, step)
    for u, far_ref in zip(late, far_refs):
        unpack(far_ref, (far_s,), jnp.bitwise_xor(mine, u), rows, cols, step)
    pad = [jnp.zeros((tiles * LANES - count, tiles * LANES), jnp.float32)] if count % LANES else []
    for d in range(ch):
        left = channel_of(left_s, d, count, step)
        right = jnp.concatenate(
            [channel_of(right_s, d, count, step)] + pad + [channel_of(far_s, d, count, step)] + pad, axis=0
        )
        prod = lax.dot_general(
            left.astype(jnp.bfloat16), right.astype(jnp.bfloat16), (((1,), (1,)), ((), ())),
            preferred_element_type=jnp.float32,
        )
        for t in range(2 * tiles):
            prod_s[t, pl.ds(d, count, stride=step), :] = prod[:, t * LANES:(t + 1) * LANES]
    near_kept = col == own_half
    for part, pieces in enumerate(parts):
        for n, u in enumerate(pieces):
            block = jnp.bitwise_xor(mine, u)
            for t in ([full] if over else []) + list(range(full)):
                near = packed_tile(prod_s, 0, t, block, rows, cols, step, ch)
                far = packed_tile(prod_s, tiles, t, block, rows, cols, step, ch)
                if t == full:
                    near, far = strip_of(near, over), strip_of(far, over)
                there = pl.ds(t * ch, near.shape[0])
                keep_refs[part][n, there] = jnp.where(near_kept, near, far).astype(jnp.bfloat16)
                send_refs[part][n, there] = jnp.where(near_kept, far, near).astype(jnp.bfloat16)


def lines_of(blocks, ch, cols):
    return (pl.cdiv(cols, LANES), blocks * line_step(ch), LANES)


def make_lines(got, rows, cols):
    ch = (got[0].shape[0] - STRIP) // tiles_of(rows, cols)[0]
    whole = pl.BlockSpec(memory_space=pltpu.VMEM)
    return pl.pallas_call(
        functools.partial(lines_kernel, rows, cols),
        in_specs=[whole] * len(got),
        out_specs=[whole] * len(got),
        out_shape=[jax.ShapeDtypeStruct(lines_of(rows, ch, cols), jnp.float32)] * len(got),
        compiler_params=pltpu.CompilerParams(vmem_limit_bytes=VMEM_LIMIT),
        cost_estimate=pl.CostEstimate(flops=10 ** 5, bytes_accessed=10 ** 8, transcendentals=0),
    )(*got)


def make_products(lines, near, far, parts, early, late, rows, cols):
    groups = len(near)
    ch = (near[0].shape[0] - STRIP) // tiles_of(rows, cols)[0] // 2
    whole = pl.BlockSpec(memory_space=pltpu.VMEM)
    tiles, held, _ = lines_of(groups * rows, ch, cols)
    one = pltpu.VMEM((tiles, held, LANES), jnp.float32)
    sizes = [len(pieces) for pieces in parts] * 2
    return pl.pallas_call(
        functools.partial(products_kernel, groups, rows, cols, parts, early, late),
        in_specs=[whole] * (2 * groups),
        out_specs=[whole] * 4,
        out_shape=[jax.ShapeDtypeStruct((n, travel_rows(ch, rows, cols), LANES), jnp.bfloat16) for n in sizes],
        scratch_shapes=[one, one, one, pltpu.VMEM((2 * tiles, held, LANES), jnp.float32)],
        compiler_params=pltpu.CompilerParams(vmem_limit_bytes=VMEM_LIMIT),
        cost_estimate=pl.CostEstimate(flops=10 ** 5, bytes_accessed=10 ** 7, transcendentals=0),
    )(*lines, *near, *far)


def add_kernel(a_ref, b_ref, *out_refs):
    for u, out_ref in enumerate(out_refs):
        out_ref[...] = (a_ref[u].astype(jnp.float32) + b_ref[u].astype(jnp.float32)).astype(out_ref.dtype)


def make_sums(a, b):
    groups, ch, flat = a.shape
    whole = pl.BlockSpec(memory_space=pltpu.VMEM)
    return pl.pallas_call(
        add_kernel,
        in_specs=[whole] * 2,
        out_specs=[whole] * groups,
        out_shape=[jax.ShapeDtypeStruct((ch, flat), a.dtype)] * groups,
        compiler_params=pltpu.CompilerParams(vmem_limit_bytes=VMEM_LIMIT),
        cost_estimate=pl.CostEstimate(flops=10 ** 5, bytes_accessed=10 ** 5, transcendentals=0),
    )(a, b)


def update_kernel(groups, rows, cols, chunks, gain_ref, w_ref, gate_ref, *refs):
    prod_refs = refs[:groups]
    out_ref, gain_s, w_s, out_s, sems = refs[groups:]
    mine = place_of(groups, rows, cols)[2]
    ch = w_ref.shape[0] // groups
    block = chunks[0][1]
    for u in range(groups):
        there = pl.ds(pl.multiple_of(jnp.bitwise_xor(mine, u) * ch, 8), ch)
        gain_s[u * ch:(u + 1) * ch] = gain_ref[there]
        w_s[u * ch:(u + 1) * ch] = w_ref[there]
    gain, weights = gain_s[...], w_s[...].astype(jnp.bfloat16)
    stores = []
    for n, (at, size) in enumerate(chunks):
        prod = jnp.concatenate(
            [
                jnp.concatenate([tile_at(ref, t, ch, 0, ch, rows, cols) for ref in prod_refs], axis=0)
                for t in range(at // LANES, pl.cdiv(at + size, LANES))
            ],
            axis=1,
        )
        mean = jnp.mean(prod, axis=0, keepdims=True)
        centred = prod - mean
        variance = jnp.mean(centred * centred, axis=0, keepdims=True)
        normed = (centred * lax.rsqrt(variance + EPS) * gain).astype(jnp.bfloat16)
        projected = lax.dot_general(normed, weights, (((0,), (0,)), ((), ())), preferred_element_type=jnp.float32)
        out_s[pl.ds(at, size)] = (gate_ref[pl.ds(at, size)] * projected[:size]).astype(out_s.dtype)
        stores.append(pltpu.make_async_copy(out_s.at[pl.ds(at, size)], out_ref.at[pl.ds(at, size)], sems.at[n]))
        stores[-1].start()
    for copy in stores:
        copy.wait()


def make_update(prods, gain, w_out, gate, rows, cols):
    groups = len(prods)
    count, channels = gate.shape
    block = 512
    chunks = [(at, min(block, count - at)) for at in range(0, count, block)]
    whole = pl.BlockSpec(memory_space=pltpu.VMEM)
    return pl.pallas_call(
        functools.partial(update_kernel, groups, rows, cols, chunks),
        in_specs=[whole] * (3 + groups),
        out_specs=pl.BlockSpec(memory_space=pltpu.HBM),
        out_shape=jax.ShapeDtypeStruct((count, channels), jnp.bfloat16),
        scratch_shapes=[
            pltpu.VMEM(gain.shape, jnp.float32),
            pltpu.VMEM(w_out.shape, jnp.float32),
            pltpu.VMEM((count, channels), jnp.bfloat16),
            pltpu.SemaphoreType.DMA((len(chunks),)),
        ],
        compiler_params=pltpu.CompilerParams(vmem_limit_bytes=VMEM_LIMIT),
    )(gain, w_out, gate, *prods)


def swap(value, shift):
    return lax.ppermute(value, "row", [(r, r ^ shift) for r in range(lax.axis_size("row"))])


def shards(pair_act, chain_lengths, resolved, in_gain, out_gain, w_left, w_right, w_gate, w_out):
    rows, cols, channels = pair_act.shape
    hidden = w_out.shape[0]
    groups = lax.axis_size("row") // 2
    normed, *edges = make_edges(
        pair_act.reshape(rows * cols, channels), chain_lengths, resolved,
        in_gain.reshape(1, channels), w_left, w_right, groups, rows, cols,
    )
    both, right = edges[:groups], edges[groups:]
    far_got = [swap(right[u], groups + u) for u in range(groups)]
    near_got = [both[0]] + [swap(both[u], u) for u in range(1, groups)]
    gate = jax.nn.sigmoid(
        jnp.einsum("cp,cd->pd", normed[:, :rows * cols], w_gate, preferred_element_type=jnp.float32)
    )
    half = groups // 2
    early, late = list(range(half, groups)) + [0], list(range(1, half))
    lines = make_lines([far_got[u] for u in early], rows, cols)
    parts = [list(range(half)), list(range(half, groups))]
    made = make_products(lines, near_got, [far_got[u] for u in late], parts, early, late, rows, cols)
    sums = {}
    for part, pieces in enumerate(parts):
        other = lax.ppermute(made[2 + part], "col", [(0, 1), (1, 0)])
        sums.update(zip(pieces, make_sums(made[part], other)))
    returned = [sums[0]] + [swap(sums[u], u) for u in range(1, groups)]
    update = make_update(returned, out_gain.reshape(hidden, 1), w_out.astype(jnp.float32), gate, rows, cols)
    return update.reshape(rows, cols, channels)


def solution(mesh):
    return jax.shard_map(
        shards,
        mesh=mesh,
        in_specs=(P(("grp", "row"), "col", None), P("grp"), P("grp"), P(), P(), P(), P(), P(), P()),
        out_specs=P(("grp", "row"), "col", None),
        check_vma=False,
    )
```
